256 devices in a mesh: alt: 64 (over y, z, core), raan: 4 (over x).
Axes of the slice: x: 4, y: 4, z: 8, core: 2. Of those that a mesh axis runs over, the one named last changes fastest.
Arguments:
- source: float32 [256, 64, 1024], P('alt', None, 'raan'), may hold values from -6 to 6
- k_alt: float32 [256, 64, 1024], P('alt', None, 'raan'), may hold values from 20 to 400
- k_inc: float32 [256, 64, 1024], P('alt', None, 'raan'), may hold values from 20 to 400
- k_raan: float32 [256, 64, 1024], P('alt', None, 'raan'), may hold values from 20 to 400
Outputs:
- density: float32 [256, 64, 1024], P('alt', None, 'raan')
- scaled_residual: float32 [256, 64, 1024], P('alt', None, 'raan')
The draws below stay inside these ranges and needn't reach their ends.
All inputs are finite; a program needn't handle non-finite values.
Results may differ from the reference program's by a relative error of at most 0.00018.
Values sent between devices are 32-bit elements; how exact they have to be, the bound alone decides.
A program may use at most 128 MiB of HBM per device.

```python
import math
import jax
import jax.numpy as jnp

INC = 64
RAAN = 1024
SWEEPS = 2
COARSE_SWEEPS = 4
NA = 256


def draw_source(key, part):
    base = jax.random.normal(key, (NA, INC, RAAN), jnp.float32)
    return jnp.clip(base, -6.0, 6.0)


def shard_levels(key, dims, split, smallest, top_value):
    gain, own = 1.0, jax.random.fold_in(key, 6)
    for dim, parts in split:
        draws = jnp.exp(jax.random.uniform(jax.random.fold_in(own, dim), (parts,), jnp.float32, smallest / len(split), top_value / len(split)))
        gain = gain * jnp.repeat(draws, dims[dim] // parts).reshape([-1 if axis == dim else 1 for axis in range(len(dims))])
    return gain


def setup_inputs(seed: int = 0) -> dict:
    arg_keys = jax.random.split(jax.random.key(seed), 5)
    source = draw_source(jax.random.fold_in(arg_keys[4], 71), 0)
    k_alt = jnp.clip(jnp.exp(math.log(400.0) - 2.9957323 * jax.random.uniform(arg_keys[1], (NA, INC, RAAN), jnp.float32) ** shard_levels(arg_keys[1], (NA, INC, RAAN), ((0, 64), (2, 4)), -0.2, 0.2)), 20.0, 400.0)
    k_inc = jnp.clip(jnp.exp(math.log(400.0) - 2.9957323 * jax.random.uniform(arg_keys[2], (NA, INC, RAAN), jnp.float32) ** shard_levels(arg_keys[2], (NA, INC, RAAN), ((0, 64), (2, 4)), -0.2, 0.2)), 20.0, 400.0)
    k_raan = jnp.clip(jnp.exp(math.log(400.0) - 2.9957323 * jax.random.uniform(arg_keys[3], (NA, INC, RAAN), jnp.float32) ** shard_levels(arg_keys[3], (NA, INC, RAAN), ((0, 64), (2, 4)), -0.2, 0.2)), 20.0, 400.0)
    return dict(source=source, k_alt=k_alt, k_inc=k_inc, k_raan=k_raan)


OMEGA = 0.75


def coarsen(values):
    depth, width, length = values.shape
    return values.reshape(depth // 2, 2, width // 2, 2, length // 2, 2).mean(axis=(1, 3, 5))


def refine(values):
    return jnp.repeat(jnp.repeat(jnp.repeat(values, 2, 0), 2, 1), 2, 2)


def make_weights(coef_alt, coef_inc, coef_raan, factor):
    zero_alt = jnp.zeros_like(coef_alt[:1])
    alt_down = jnp.concatenate([zero_alt, coef_alt[:-1]], 0)
    alt_up = jnp.concatenate([coef_alt[1:], zero_alt], 0)
    w_alt_lo = factor * 0.5 * (coef_alt + alt_down)
    w_alt_hi = factor * 0.5 * (coef_alt + alt_up)
    inner_faces = factor * 0.5 * (coef_inc[:, :-1] + coef_inc[:, 1:])
    zero_inc = jnp.zeros_like(coef_inc[:, :1])
    w_inc_lo = jnp.concatenate([zero_inc, inner_faces], 1)
    w_inc_hi = jnp.concatenate([inner_faces, zero_inc], 1)
    w_raan_lo = factor * 0.5 * (coef_raan + jnp.roll(coef_raan, 1, 2))
    w_raan_hi = factor * 0.5 * (coef_raan + jnp.roll(coef_raan, -1, 2))
    diagonal = 1.0 + (w_alt_lo + w_alt_hi + w_inc_lo + w_inc_hi + w_raan_lo + w_raan_hi)
    return (w_alt_lo, w_alt_hi, w_inc_lo, w_inc_hi, w_raan_lo, w_raan_hi, diagonal)


def apply_op(weights, field):
    w_alt_lo, w_alt_hi, w_inc_lo, w_inc_hi, w_raan_lo, w_raan_hi, diagonal = weights
    zero_alt = jnp.zeros_like(field[:1])
    v_down = jnp.concatenate([zero_alt, field[:-1]], 0)
    v_up = jnp.concatenate([field[1:], zero_alt], 0)
    zero_inc = jnp.zeros_like(field[:, :1])
    v_prev = jnp.concatenate([zero_inc, field[:, :-1]], 1)
    v_next = jnp.concatenate([field[:, 1:], zero_inc], 1)
    v_left = jnp.roll(field, 1, 2)
    v_right = jnp.roll(field, -1, 2)
    beside = (w_alt_lo * v_down + w_alt_hi * v_up + w_inc_lo * v_prev + w_inc_hi * v_next
              + w_raan_lo * v_left + w_raan_hi * v_right)
    return diagonal * field - beside


def smooth(field, target, weights, repeats):
    for _ in range(repeats):
        field = field + OMEGA * (target - apply_op(weights, field)) / weights[6]
    return field


def reference(source, k_alt, k_inc, k_raan):
    weights_one = make_weights(k_alt, k_inc, k_raan, 1.0)
    coef_two = (coarsen(k_alt), coarsen(k_inc), coarsen(k_raan))
    weights_two = make_weights(coef_two[0], coef_two[1], coef_two[2], 0.25)
    coef_three = (coarsen(coef_two[0]), coarsen(coef_two[1]), coarsen(coef_two[2]))
    weights_three = make_weights(coef_three[0], coef_three[1], coef_three[2], 0.0625)
    density = smooth(source, source, weights_one, SWEEPS)
    rhs_two = coarsen(source - apply_op(weights_one, density))
    correction = OMEGA * rhs_two / weights_two[6]
    correction = smooth(correction, rhs_two, weights_two, SWEEPS - 1)
    rhs_three = coarsen(rhs_two - apply_op(weights_two, correction))
    coarse_part = OMEGA * rhs_three / weights_three[6]
    coarse_part = smooth(coarse_part, rhs_three, weights_three, COARSE_SWEEPS - 1)
    correction = correction + refine(coarse_part)
    correction = smooth(correction, rhs_two, weights_two, SWEEPS)
    density = density + refine(correction)
    density = smooth(density, source, weights_one, SWEEPS)
    scaled_residual = (source - apply_op(weights_one, density)) / weights_one[6]
    return density, scaled_residual
```

```python
import functools

import jax
import jax.numpy as jnp
from jax import lax
from jax.experimental import pallas as pl
from jax.experimental.pallas import tpu as pltpu
from jax.sharding import PartitionSpec as P

OMEGA = 0.75
MESH = pl.DeviceIdType.MESH

INC = 64
COLS = 256
WIDE = 384
HALO = 3
OWN = 4
TILES = WIDE // 128
LAYERS = OWN + 2 * HALO
FAR = 4


def lane_roll(x, shift):
    return pltpu.roll(x, shift % x.shape[-1], axis=x.ndim - 1)


def row_roll(x, shift):
    return pltpu.roll(x, shift % x.shape[-2], axis=x.ndim - 2)


def iota(shape, dim):
    return lax.broadcasted_iota(jnp.int32, shape, dim)


def beside_fine(v, down, up, w_down, w_up, w_inc, w_raan):
    total = w_down * down + w_up * up
    total = total + w_inc * row_roll(v, 1) + row_roll(w_inc * v, -1)
    return total + w_raan * lane_roll(v, 1) + lane_roll(w_raan * v, -1)


def prev_row(v):
    turned = row_roll(v, 1)
    return jnp.where(iota(v.shape, 0) == 0, lane_roll(turned, 1), turned)


def next_row(v):
    turned = row_roll(v, -1)
    return jnp.where(iota(v.shape, 0) == v.shape[0] - 1, lane_roll(turned, -1), turned)


def coarse_weights(k_alt, k_down, k_up, m_down, m_up, k_inc, k_raan, factor, step):
    half = 0.5 * factor
    lo = half * (k_alt + m_down * k_down)
    hi = half * (k_alt + m_up * k_up)
    outer = (iota(k_inc.shape, 0) == 0) & (iota(k_inc.shape, 1) % 2 == 0)
    w_inc = jnp.where(outer, 0.0, half * (k_inc + prev_row(k_inc)))
    w_raan = half * (k_raan + lane_roll(k_raan, step))
    diagonal = 1.0 + (lo + hi + w_inc + next_row(w_inc) + w_raan + lane_roll(w_raan, -step))
    return m_down * lo, m_up * hi, w_inc, w_raan, diagonal


def beside_coarse(v, down, up, w_down, w_up, w_inc, w_raan, step):
    total = w_down * down + w_up * up
    total = total + w_inc * prev_row(v) + next_row(w_inc * v)
    return total + w_raan * lane_roll(v, step) + lane_roll(w_raan * v, -step)


def kernel(n_alt, n_raan, f_hbm, ka_hbm, ki_hbm, kr_hbm, dens_hbm, sres_hbm,
           ef, eka, eki, ekr, v1, v2, p0, wa, wi, wr, invd, diag, sres,
           pack, rb, xb, tmp, tmp2,
           k2a, k2b, w2, sb4, rb4, rhs2, c2a, c2b, q0, q1, q2, rf,
           k3, w3, r3, c3,
           load_sem, out_sem, send_sem, recv_sem):
    a = lax.axis_index("alt")
    r = lax.axis_index("raan")
    m_lo = jnp.where(a == 0, 0.0, 1.0).astype(jnp.float32)
    m_hi = jnp.where(a == n_alt - 1, 0.0, 1.0).astype(jnp.float32)

    def alt_dev(d):
        return (lax.rem(a + d + n_alt, n_alt), r)

    def raan_dev(d):
        return (a, lax.rem(r + d + n_raan, n_raan))

    count = [0]
    sends = []

    def remote(src, dst, device):
        k = count[0]
        count[0] += 1
        copy = pltpu.make_async_remote_copy(
            src_ref=src, dst_ref=dst, send_sem=send_sem.at[k], recv_sem=recv_sem.at[k],
            device_id=device, device_id_type=MESH)
        copy.start()
        sends.append(copy)
        return copy

    def settle():
        while sends:
            sends.pop().wait_send()

    hbm = (f_hbm, ka_hbm, ki_hbm, kr_hbm)
    ext = (ef, eka, eki, ekr)
    loads = []
    for i in range(4):
        loads.append(pltpu.make_async_copy(
            hbm[i], ext[i].at[HALO:HALO + OWN, :, 0:COLS], load_sem.at[i]))
        loads[i].start()

    barrier = pltpu.get_barrier_semaphore()
    for d in range(1, FAR + 1):
        for side in (d, -d):
            pl.semaphore_signal(barrier, inc=1, device_id=alt_dev(side), device_id_type=MESH)
    for side in (1, -1):
        pl.semaphore_signal(barrier, inc=1, device_id=raan_dev(side), device_id_type=MESH)
    pl.semaphore_wait(barrier, 2 * FAR + 2)

    cols = slice(0, COLS)
    bulk = []
    for i, (up_src, up_dst, down_src, down_dst) in enumerate((
            (slice(2, 4), slice(1, 3), slice(0, 2), slice(7, 9)),
            (slice(2, 4), slice(1, 3), slice(0, 2), slice(7, 9)),
            (slice(3, 4), slice(2, 3), slice(0, 1), slice(7, 8)),
            (slice(3, 4), slice(2, 3), slice(0, 1), slice(7, 8)))):
        bulk.append(remote(hbm[i].at[up_src], ext[i].at[up_dst, :, cols], alt_dev(1)))
        bulk.append(remote(hbm[i].at[down_src], ext[i].at[down_dst, :, cols], alt_dev(-1)))

    quarter = iota((16, 128), 1) // 32
    ring = []
    for i in range(4):
        loads[i].wait()
        for l in range(OWN):
            low = ext[i][HALO + l, :, 0:128]
            high = ext[i][HALO + l, :, 128:256]
            first = low[0:16]
            last = high[0:16]
            for g in range(1, 4):
                first = jnp.where(quarter == g, lane_roll(low[16 * g:16 * g + 16], 32 * g), first)
                last = jnp.where(quarter == (3 + g) % 4, lane_roll(high[16 * g:16 * g + 16], 32 * g), last)
            pack[i, l, 0] = first
            pack[i, l, 1] = last
        ring.append(remote(pack.at[i, :, 0], rb.at[i, :, 0], raan_dev(-1)))
        ring.append(remote(pack.at[i, :, 1], rb.at[i, :, 1], raan_dev(1)))

    def unpack(first, last, dst, layer):
        for g in range(4):
            both = jnp.where(quarter == g, first, last)
            dst[layer, 16 * g:16 * g + 16, COLS:WIDE] = lane_roll(both, -32 * g) if g else both

    for copy in ring:
        copy.wait_recv()
    relay = []
    for i, x_slot, up_src, down_src in (
            (0, slice(0, 2), slice(2, 4), slice(0, 2)),
            (1, slice(2, 4), slice(2, 4), slice(0, 2)),
            (2, slice(4, 5), slice(3, 4), slice(0, 1)),
            (3, slice(5, 6), slice(3, 4), slice(0, 1))):
        relay.append(remote(rb.at[i, up_src], xb.at[0, x_slot], alt_dev(1)))
        relay.append(remote(rb.at[i, down_src], xb.at[1, x_slot], alt_dev(-1)))
    for i in range(4):
        for l in range(OWN):
            unpack(rb[i, l, 0], rb[i, l, 1], ext[i], HALO + l)

    row0 = iota((INC, WIDE), 0) == 0

    def fine_weights(l):
        m_down = jnp.where(l == HALO, m_lo, jnp.where(l == HALO + OWN, m_hi, 1.0))
        m_up = jnp.where(l == HALO - 1, m_lo, jnp.where(l == HALO + OWN - 1, m_hi, 1.0))
        k_alt = eka[l]
        lo = 0.5 * (k_alt + m_down * eka[l - 1])
        hi = 0.5 * (k_alt + m_up * eka[l + 1])
        k_inc = eki[l]
        w_inc = jnp.where(row0, 0.0, 0.5 * (k_inc + row_roll(k_inc, 1)))
        k_raan = ekr[l]
        w_raan = 0.5 * (k_raan + lane_roll(k_raan, 1))
        dg = 1.0 + (lo + hi + w_inc + row_roll(w_inc, -1) + w_raan + lane_roll(w_raan, -1))
        wa[l - 1] = m_down * lo
        wa[l] = m_up * hi
        wi[l] = w_inc
        wr[l] = w_raan
        diag[l] = dg
        invd[l] = OMEGA / dg

    def target_fine(src, l):
        return ef[l] + beside_fine(src[l], src[l - 1], src[l + 1], wa[l - 1], wa[l], wi[l], wr[l])

    def sweep_fine(src, dst, l):
        dst[l] = 0.25 * src[l] + invd[l] * target_fine(src, l)

    def layers(lo, hi, *bodies):
        def body(l, carry):
            for one in bodies:
                one(l)
            return carry
        lax.fori_loop(lo, hi, body, 0)

    first_sweep = functools.partial(sweep_fine, ef, v1)
    layers(4, 6, fine_weights, first_sweep)
    swept = [remote(v1.at[5], v1.at[1], alt_dev(1)), remote(v1.at[4], v1.at[8], alt_dev(-1))]

    even2 = iota((16, WIDE), 1) % 2 == 0

    def row_pairs(scratch, x):
        n = x.shape[0] // 2
        for t in range(TILES):
            scratch[t] = x[:, 128 * t:128 * t + 128]
        return jnp.concatenate(
            [scratch[t, pl.ds(0, n, stride=2)] + scratch[t, pl.ds(1, n, stride=2)] for t in range(TILES)], axis=1)

    def twice(scratch, x):
        n = x.shape[0]
        for t in range(TILES):
            part = x[:, 128 * t:128 * t + 128]
            scratch[t, pl.ds(0, n, stride=2)] = part
            scratch[t, pl.ds(1, n, stride=2)] = part
        return jnp.concatenate([scratch[t] for t in range(TILES)], axis=1)

    def coarsen_fine(total):
        pairs = row_pairs(tmp, total)
        t_a, t_b = pairs[0:16], pairs[16:32]
        return 0.125 * (jnp.where(even2, t_a, t_b) + jnp.where(even2, lane_roll(t_a, -1), lane_roll(t_b, 1)))

    low3 = iota((8, WIDE), 1) % 4 < 2

    def coarsen_mid(total):
        t = row_pairs(tmp2, total)
        return 0.125 * (t + jnp.where(low3, lane_roll(t, -2), lane_roll(t, 2)))

    for j in range(2):
        k2a[2 + j] = coarsen_fine(eka[3 + 2 * j] + eka[4 + 2 * j])
        k2b[2 + j, 0] = coarsen_fine(eki[3 + 2 * j] + eki[4 + 2 * j])
        k2b[2 + j, 1] = coarsen_fine(ekr[3 + 2 * j] + ekr[4 + 2 * j])
    k3[FAR, 0] = coarsen_mid(k2a[2] + k2a[3])
    k3[FAR, 1] = coarsen_mid(k2b[2, 0] + k2b[3, 0])
    k3[FAR, 2] = coarsen_mid(k2b[2, 1] + k2b[3, 1])
    coarse = [
        remote(k2a.at[2:4], k2a.at[0:2], alt_dev(1)), remote(k2a.at[2:4], k2a.at[4:6], alt_dev(-1)),
        remote(k2b.at[3], k2b.at[1], alt_dev(1)), remote(k2b.at[2], k2b.at[4], alt_dev(-1))]

    for copy in bulk + relay:
        copy.wait_recv()
    for side, at in ((0, (1, 2, 2)), (1, (7, 8, 7))):
        for i, slot, layer in ((0, 0, at[0]), (0, 1, at[1]), (1, 2, at[0]), (1, 3, at[1]), (2, 4, at[2]), (3, 5, at[2])):
            unpack(xb[side, slot, 0], xb[side, slot, 1], ext[i], layer)
    layers(2, 4, fine_weights, first_sweep)
    layers(6, 8, fine_weights, first_sweep)
    for copy in swept:
        copy.wait_recv()

    later = []
    for i, x_slot, up_src, up_dst, down_src, down_dst in (
            (1, 6, 1, 0, 2, 9), (2, 7, 2, 1, 1, 8), (3, 8, 2, 1, 1, 8)):
        later.append(remote(hbm[i].at[up_src], ext[i].at[up_dst, :, cols], alt_dev(1)))
        later.append(remote(hbm[i].at[down_src], ext[i].at[down_dst, :, cols], alt_dev(-1)))
        later.append(remote(rb.at[i, up_src], xb.at[0, x_slot], alt_dev(1)))
        later.append(remote(rb.at[i, down_src], xb.at[1, x_slot], alt_dev(-1)))

    layers(2, 8, functools.partial(sweep_fine, v1, v2))

    def residual_fine(l):
        return target_fine(v2, l) - diag[l] * v2[l]

    for copy in coarse:
        copy.wait_recv()
    for x in range(1, 5):
        m_down = {2: m_lo, 4: m_hi}.get(x, 1.0)
        m_up = {1: m_lo, 3: m_hi}.get(x, 1.0)
        w_down, w_up, w_inc, w_raan, dg = coarse_weights(
            k2a[x], k2a[x - 1], k2a[x + 1], m_down, m_up, k2b[x, 0], k2b[x, 1], 0.25, 2)
        for n, value in enumerate((w_down, w_up, w_inc, w_raan, dg, OMEGA / dg)):
            w2[x, n] = value

    for j in range(2):
        rhs2[2 + j] = coarsen_fine(residual_fine(3 + 2 * j) + residual_fine(4 + 2 * j))
        c2a[2 + j] = rhs2[2 + j] * w2[2 + j, 5]
    sb4[0, 0] = rhs2[3]
    sb4[0, 1] = c2a[2]
    sb4[1, 0] = rhs2[2]
    sb4[1, 1] = c2a[3]
    mid = [remote(sb4.at[0], rb4.at[0], alt_dev(1)), remote(sb4.at[1], rb4.at[1], alt_dev(-1))]
    far_k = []
    for d in range(1, FAR + 1):
        for side in (d, -d):
            far_k.append(remote(k3.at[FAR], k3.at[FAR - side], alt_dev(side)))
    dens2 = [remote(v2.at[4:6], v2.at[0:2], alt_dev(1)), remote(v2.at[4:6], v2.at[8:10], alt_dev(-1))]

    for copy in mid:
        copy.wait_recv()
    rhs2[1] = rb4[0, 0]
    c2a[0] = rb4[0, 1]
    rhs2[4] = rb4[1, 0]
    c2a[5] = rb4[1, 1]
    c2a[1] = rhs2[1] * w2[1, 5]
    c2a[4] = rhs2[4] * w2[4, 5]

    def target_mid(src, x):
        return rhs2[x] + beside_coarse(src[x], src[x - 1], src[x + 1], w2[x, 0], w2[x, 1], w2[x, 2], w2[x, 3], 2)

    def sweep_mid(src, dst, x):
        dst[x] = 0.25 * src[x] + w2[x, 5] * target_mid(src, x)

    for x in range(1, 5):
        sweep_mid(c2a, c2b, x)
    residual = [target_mid(c2b, x) - w2[x, 4] * c2b[x] for x in (2, 3)]
    r3[FAR] = coarsen_mid(residual[0] + residual[1])

    for copy in far_k:
        copy.wait_recv()
    for x in range(1, 2 * FAR):
        m_down = jnp.where(lax.rem(a + x - FAR + n_alt, n_alt) == 0, 0.0, 1.0).astype(jnp.float32)
        m_up = jnp.where(lax.rem(a + x - FAR + 1 + n_alt, n_alt) == 0, 0.0, 1.0).astype(jnp.float32)
        w_down, w_up, w_inc, w_raan, dg = coarse_weights(
            k3[x, 0], k3[x - 1, 0], k3[x + 1, 0], m_down, m_up, k3[x, 1], k3[x, 2], 0.0625, 4)
        for n, value in enumerate((w_down, w_up, w_inc, w_raan, OMEGA / dg)):
            w3[x, n] = value
    c3[0, FAR] = r3[FAR] * w3[FAR, 4]
    far = []
    for d in range(1, FAR):
        for side in (d, -d):
            far.append(remote(r3.at[FAR], r3.at[FAR - side], alt_dev(side)))
    for side in (FAR, -FAR):
        far.append(remote(c3.at[0, FAR], c3.at[0, FAR - side], alt_dev(side)))
    ends = [remote(c2b.at[2], c2b.at[0], alt_dev(1)), remote(c2b.at[3], c2b.at[5], alt_dev(-1))]

    for copy in later:
        copy.wait_recv()
    for side, at in ((0, (0, 1)), (1, (9, 8))):
        for i, slot, layer in ((1, 6, at[0]), (2, 7, at[1]), (3, 8, at[1])):
            unpack(xb[side, slot, 0], xb[side, slot, 1], ext[i], layer)
    fine_weights(1)
    fine_weights(8)

    for copy in far:
        copy.wait_recv()
    for x in range(1, 2 * FAR):
        if x != FAR:
            c3[0, x] = r3[x] * w3[x, 4]
    for n in range(3):
        for x in range(1 + n, 2 * FAR - n):
            v = c3[n, x]
            total = r3[x] + beside_coarse(v, c3[n, x - 1], c3[n, x + 1], w3[x, 0], w3[x, 1], w3[x, 2], w3[x, 3], 4)
            c3[n + 1, x] = 0.25 * v + w3[x, 4] * total

    for copy in ends:
        copy.wait_recv()
    for j in range(3):
        part = twice(tmp2, c3[3, FAR - 1 + j])
        for x in (2 * j, 2 * j + 1):
            q0[x] = c2b[x] + part
    for x in range(1, 5):
        sweep_mid(q0, q1, x)
    for x in (2, 3):
        sweep_mid(q1, q2, x)
    up2 = [remote(q2.at[2:4], q2.at[0:2], alt_dev(1)), remote(q2.at[2:4], q2.at[4:6], alt_dev(-1))]

    def refine_mid(x):
        c = q2[x]
        part_a = jnp.where(even2, c, lane_roll(c, 1))
        part_b = jnp.where(even2, lane_roll(c, -1), c)
        rf[x] = twice(tmp, jnp.concatenate([part_a, part_b], axis=0))

    def correct(l):
        p0[l] = v2[l] + rf[(l - 1) // 2 + 1 if l else 0]

    for x in (2, 3):
        refine_mid(x)
    for l in range(HALO, HALO + OWN):
        correct(l)
    for copy in dens2:
        copy.wait_recv()
    settle_now = list(sends)
    sends.clear()
    for copy in settle_now:
        copy.wait_send()
    last_sweep = functools.partial(sweep_fine, p0, v1)
    layers(4, 6, last_sweep)
    for copy in up2:
        copy.wait_recv()
    for x in (0, 1, 4, 5):
        refine_mid(x)
    for l in (0, 1, 2, 7, 8, 9):
        correct(l)
    layers(1, 4, last_sweep)
    layers(6, 9, last_sweep)
    layers(2, 8, functools.partial(sweep_fine, v1, v2))
    outs = [pltpu.make_async_copy(v2.at[HALO:HALO + OWN, :, cols], dens_hbm, out_sem.at[0])]
    outs[0].start()

    def last_residual(l):
        value = (1.0 / OMEGA) * (invd[l] * target_fine(v2, l)) - v2[l]
        sres[l - HALO] = value[:, 0:COLS]

    layers(HALO, HALO + OWN, last_residual)
    outs.append(pltpu.make_async_copy(sres, sres_hbm, out_sem.at[1]))
    outs[1].start()
    settle()
    for copy in outs:
        copy.wait()


def solution(mesh):
    n_alt, n_raan = mesh.shape["alt"], mesh.shape["raan"]
    spec = P("alt", None, "raan")
    anywhere = pl.BlockSpec(memory_space=pl.ANY)

    def vmem(*shape):
        return pltpu.VMEM(shape, jnp.float32)

    def shards(source, k_alt, k_inc, k_raan):
        big = [vmem(LAYERS, INC, WIDE)] * 12
        scratch = big + [vmem(OWN, INC, COLS)]
        scratch += [vmem(4, OWN, 2, 16, 128), vmem(4, OWN, 2, 16, 128), vmem(2, 9, 2, 16, 128),
                    vmem(TILES, INC, 128), vmem(TILES, 16, 128)]
        scratch += [vmem(6, 16, WIDE), vmem(6, 2, 16, WIDE), vmem(6, 6, 16, WIDE), vmem(2, 2, 16, WIDE),
                    vmem(2, 2, 16, WIDE)] + [vmem(6, 16, WIDE)] * 6 + [vmem(6, INC, WIDE)]
        scratch += [vmem(2 * FAR + 1, 3, 8, WIDE), vmem(2 * FAR + 1, 5, 8, WIDE), vmem(2 * FAR + 1, 8, WIDE),
                    vmem(4, 2 * FAR + 1, 8, WIDE)]
        scratch += [pltpu.SemaphoreType.DMA((4,)), pltpu.SemaphoreType.DMA((2,)),
                    pltpu.SemaphoreType.DMA((72,)), pltpu.SemaphoreType.DMA((72,))]
        shape = jax.ShapeDtypeStruct(source.shape, source.dtype)
        return pl.pallas_call(
            functools.partial(kernel, n_alt, n_raan),
            out_shape=(shape, shape),
            in_specs=[anywhere] * 4,
            out_specs=(anywhere, anywhere),
            scratch_shapes=scratch,
            compiler_params=pltpu.CompilerParams(
                collective_id=0, has_side_effects=True, vmem_limit_bytes=48 * 1024 * 1024),
            name="vcycle",
        )(source, k_alt, k_inc, k_raan)

    return jax.shard_map(shards, mesh=mesh, in_specs=(spec,) * 4, out_specs=(spec, spec), check_vma=False)
```

```python
import functools

import jax
import jax.numpy as jnp
from jax import lax
from jax.experimental import pallas as pl
from jax.experimental.pallas import tpu as pltpu
from jax.sharding import PartitionSpec as P

OMEGA = 0.75
MESH = pl.DeviceIdType.MESH

INC = 64
COLS = 256
WIDE = 384
HALO = 2
OWN = 4
TILES = WIDE // 128
LAYERS = OWN + 2 * HALO
FAR = 4


def lane_roll(x, shift):
    return pltpu.roll(x, shift % x.shape[-1], axis=x.ndim - 1)


def row_roll(x, shift):
    return pltpu.roll(x, shift % x.shape[-2], axis=x.ndim - 2)


def iota(shape, dim):
    return lax.broadcasted_iota(jnp.int32, shape, dim)


def beside_fine(v, down, up, w_down, w_up, w_inc, w_raan):
    total = w_down * down + w_up * up
    total = total + w_inc * row_roll(v, 1) + row_roll(w_inc * v, -1)
    return total + w_raan * lane_roll(v, 1) + lane_roll(w_raan * v, -1)


def prev_row(v):
    turned = row_roll(v, 1)
    return jnp.where(iota(v.shape, 0) == 0, lane_roll(turned, 1), turned)


def next_row(v):
    turned = row_roll(v, -1)
    return jnp.where(iota(v.shape, 0) == v.shape[0] - 1, lane_roll(turned, -1), turned)


def coarse_weights(k_alt, k_down, k_up, m_down, m_up, k_inc, k_raan, factor, step):
    half = 0.5 * factor
    lo = half * (k_alt + m_down * k_down)
    hi = half * (k_alt + m_up * k_up)
    outer = (iota(k_inc.shape, 0) == 0) & (iota(k_inc.shape, 1) % 2 == 0)
    w_inc = jnp.where(outer, 0.0, half * (k_inc + prev_row(k_inc)))
    w_raan = half * (k_raan + lane_roll(k_raan, step))
    diagonal = 1.0 + (lo + hi + w_inc + next_row(w_inc) + w_raan + lane_roll(w_raan, -step))
    return m_down * lo, m_up * hi, w_inc, w_raan, diagonal


def beside_coarse(v, down, up, w_down, w_up, w_inc, w_raan, step):
    total = w_down * down + w_up * up
    total = total + w_inc * prev_row(v) + next_row(w_inc * v)
    return total + w_raan * lane_roll(v, step) + lane_roll(w_raan * v, -step)


class Exchange:
    def __init__(self, ups, downs, distance, has_up, has_down):
        self.ups, self.downs = ups, downs
        self.has_up, self.has_down = has_up(distance), has_down(distance)

    def start(self):
        @pl.when(self.has_up)
        def _():
            for copy in self.ups:
                copy.start()

        @pl.when(self.has_down)
        def _():
            for copy in self.downs:
                copy.start()

    def wait_recv(self):
        @pl.when(self.has_down)
        def _():
            for copy in self.ups:
                copy.wait_recv()

        @pl.when(self.has_up)
        def _():
            for copy in self.downs:
                copy.wait_recv()

    def wait_send(self):
        @pl.when(self.has_up)
        def _():
            for copy in self.ups:
                copy.wait_send()

        @pl.when(self.has_down)
        def _():
            for copy in self.downs:
                copy.wait_send()


def kernel(n_alt, n_raan, f_hbm, ka_hbm, ki_hbm, kr_hbm, dens_hbm, sres_hbm,
           ef, eka, eki, ekr, v1, v2, p0, p1, p2, wa, wi, wr, invd, diag, sres,
           pack, rb, xb, tmp, tmp2,
           k2a, k2b, w2, sb4, rb4, rhs2, c2a, c2b, q0, q1, q2, rf,
           k3, w3, r3, c3, s3, l3,
           load_sem, out_sem, send_sem, recv_sem, near):
    a = lax.axis_index("alt")
    r = lax.axis_index("raan")
    m_lo = jnp.where(a == 0, 0.0, 1.0).astype(jnp.float32)
    m_hi = jnp.where(a == n_alt - 1, 0.0, 1.0).astype(jnp.float32)

    def has_up(d):
        return a < n_alt - d

    def has_down(d):
        return a >= d

    def alt_dev(d):
        return (lax.rem(a + d + n_alt, n_alt), r)

    def raan_dev(d):
        return (a, lax.rem(r + d + n_raan, n_raan))

    count = [0]
    sends = []

    def describe(src, dst, device):
        k = count[0]
        count[0] += 1
        return pltpu.make_async_remote_copy(
            src_ref=src, dst_ref=dst, send_sem=send_sem.at[k], recv_sem=recv_sem.at[k],
            device_id=device, device_id_type=MESH)

    def remote(src, dst, device):
        copy = describe(src, dst, device)
        copy.start()
        sends.append(copy)
        return copy

    def exchange(ups, downs, distance=1):
        copy = Exchange([describe(s, d, alt_dev(distance)) for s, d in ups],
                        [describe(s, d, alt_dev(-distance)) for s, d in downs], distance, has_up, has_down)
        copy.start()
        sends.append(copy)
        return copy

    hbm = (f_hbm, ka_hbm, ki_hbm, kr_hbm)
    ext = (ef, eka, eki, ekr)
    cols = slice(0, COLS)
    own = slice(HALO, HALO + OWN)
    loads = []
    for i in range(4):
        loads.append(pltpu.make_async_copy(hbm[i], ext[i].at[own, :, cols], load_sem.at[i]))

    barrier = pltpu.get_barrier_semaphore()

    def greet(sem_up, sem_down):
        @pl.when(has_up(1))
        def _():
            pl.semaphore_signal(sem_up, inc=1, device_id=alt_dev(1), device_id_type=MESH)

        @pl.when(has_down(1))
        def _():
            pl.semaphore_signal(sem_down, inc=1, device_id=alt_dev(-1), device_id_type=MESH)

    greet(barrier, barrier)
    for side in (1, -1):
        pl.semaphore_signal(barrier, inc=1, device_id=raan_dev(side), device_id_type=MESH)
    for i in range(4):
        loads[i].start()

    @pl.when(a == 0)
    def _():
        for ref in (ef, eka, eki, ekr, v1, v2, p1):
            ref[0:HALO] = jnp.zeros((HALO, INC, WIDE), jnp.float32)
        xb[0] = jnp.zeros(xb.shape[1:], jnp.float32)
        rb4[0] = jnp.zeros(rb4.shape[1:], jnp.float32)
        for ref in (k2a, k2b, c2b, q2):
            ref[0:2] = jnp.zeros((2,) + ref.shape[1:], jnp.float32)

    @pl.when(a == n_alt - 1)
    def _():
        for ref in (ef, eka, eki, ekr, v1, v2, p1):
            ref[HALO + OWN:LAYERS] = jnp.zeros((HALO, INC, WIDE), jnp.float32)
        xb[1] = jnp.zeros(xb.shape[1:], jnp.float32)
        rb4[1] = jnp.zeros(rb4.shape[1:], jnp.float32)
        for ref in (k2a, k2b, c2b, q2):
            ref[4:6] = jnp.zeros((2,) + ref.shape[1:], jnp.float32)

    for d in range(1, FAR + 1):
        for side, here in ((d, has_up(d)), (-d, has_down(d))):
            @pl.when(jnp.logical_not(here))
            def _():
                l3[:, FAR + side] = jnp.zeros((2, 8, WIDE), jnp.float32)

    pl.semaphore_wait(barrier, 2 + has_up(1).astype(jnp.int32) + has_down(1).astype(jnp.int32))

    low2, high2, low1, high1 = slice(0, 2), slice(2, 4), slice(0, 1), slice(3, 4)
    below2, above2, below1, above1 = slice(0, 2), slice(6, 8), slice(1, 2), slice(6, 7)
    bulk = exchange(
        [(hbm[i].at[high2 if i < 2 else high1], ext[i].at[below2 if i < 2 else below1, :, cols]) for i in range(4)],
        [(hbm[i].at[low2 if i < 2 else low1], ext[i].at[above2 if i < 2 else above1, :, cols]) for i in range(4)])

    quarter = iota((16, 128), 1) // 32
    ring = []
    for i in range(4):
        loads[i].wait()
        for l in range(OWN):
            low = ext[i][HALO + l, :, 0:128]
            high = ext[i][HALO + l, :, 128:256]
            first = low[0:16]
            last = high[0:16]
            for g in range(1, 4):
                first = jnp.where(quarter == g, lane_roll(low[16 * g:16 * g + 16], 32 * g), first)
                last = jnp.where(quarter == (3 + g) % 4, lane_roll(high[16 * g:16 * g + 16], 32 * g), last)
            pack[i, l, 0] = first
            pack[i, l, 1] = last
        ring.append((remote(pack.at[i, :, 0], rb.at[i, :, 0], raan_dev(-1)),
                     remote(pack.at[i, :, 1], rb.at[i, :, 1], raan_dev(1))))

    greet(near.at[0, 0], near.at[0, 1])

    def unpack(first, last, dst, layer):
        for g in range(4):
            both = jnp.where(quarter == g, first, last)
            dst[layer, 16 * g:16 * g + 16, COLS:WIDE] = lane_roll(both, -32 * g) if g else both

    relay = []
    x_slot = (slice(0, 2), slice(2, 4), slice(4, 5), slice(5, 6))
    for i in range(4):
        for copy in ring[i]:
            copy.wait_recv()
        relay.append(exchange([(rb.at[i, high2 if i < 2 else high1], xb.at[0, x_slot[i]])],
                              [(rb.at[i, low2 if i < 2 else low1], xb.at[1, x_slot[i]])]))
        for l in range(OWN):
            unpack(rb[i, l, 0], rb[i, l, 1], ext[i], HALO + l)

    row0 = iota((INC, WIDE), 0) == 0

    def fine_weights(l):
        m_down = jnp.where(l == HALO, m_lo, jnp.where(l == HALO + OWN, m_hi, 1.0))
        m_up = jnp.where(l == HALO - 1, m_lo, jnp.where(l == HALO + OWN - 1, m_hi, 1.0))
        k_alt = eka[l]
        lo = 0.5 * (k_alt + m_down * eka[l - 1])
        hi = 0.5 * (k_alt + m_up * eka[l + 1])
        k_inc = eki[l]
        w_inc = jnp.where(row0, 0.0, 0.5 * (k_inc + row_roll(k_inc, 1)))
        k_raan = ekr[l]
        w_raan = 0.5 * (k_raan + lane_roll(k_raan, 1))
        dg = 1.0 + (lo + hi + w_inc + row_roll(w_inc, -1) + w_raan + lane_roll(w_raan, -1))
        wa[l - 1] = m_down * lo
        wa[l] = m_up * hi
        wi[l] = w_inc
        wr[l] = w_raan
        diag[l] = dg
        invd[l] = OMEGA / dg

    def target_fine(src, l):
        return ef[l] + beside_fine(src[l], src[l - 1], src[l + 1], wa[l - 1], wa[l], wi[l], wr[l])

    def sweep_fine(src, dst, l):
        dst[l] = 0.25 * src[l] + invd[l] * target_fine(src, l)

    def layers(lo, hi, *bodies):
        def body(l, carry):
            for one in bodies:
                one(l)
            return carry
        lax.fori_loop(lo, hi, body, 0)

    first_sweep = functools.partial(sweep_fine, ef, v1)
    layers(3, 5, fine_weights, first_sweep)
    swept = exchange([(v1.at[4], v1.at[0])], [(v1.at[3], v1.at[7])])

    even2 = iota((16, WIDE), 1) % 2 == 0

    def row_pairs(scratch, x):
        n = x.shape[0] // 2
        for t in range(TILES):
            scratch[t] = x[:, 128 * t:128 * t + 128]
        return jnp.concatenate(
            [scratch[t, pl.ds(0, n, stride=2)] + scratch[t, pl.ds(1, n, stride=2)] for t in range(TILES)], axis=1)

    def twice(scratch, x):
        n = x.shape[0]
        for t in range(TILES):
            part = x[:, 128 * t:128 * t + 128]
            scratch[t, pl.ds(0, n, stride=2)] = part
            scratch[t, pl.ds(1, n, stride=2)] = part
        return jnp.concatenate([scratch[t] for t in range(TILES)], axis=1)

    def coarsen_fine(total):
        pairs = row_pairs(tmp, total)
        t_a, t_b = pairs[0:16], pairs[16:32]
        return 0.125 * (jnp.where(even2, t_a, t_b) + jnp.where(even2, lane_roll(t_a, -1), lane_roll(t_b, 1)))

    low3 = iota((8, WIDE), 1) % 4 < 2

    def coarsen_mid(total):
        t = row_pairs(tmp2, total)
        return 0.125 * (t + jnp.where(low3, lane_roll(t, -2), lane_roll(t, 2)))

    def first_of(pair):
        return jnp.where(low3, pair, lane_roll(pair, 2))

    def second_of(pair):
        return jnp.where(low3, lane_roll(pair, -2), pair)

    for j in range(2):
        k2a[2 + j] = coarsen_fine(eka[2 + 2 * j] + eka[3 + 2 * j])
        k2b[2 + j, 0] = coarsen_fine(eki[2 + 2 * j] + eki[3 + 2 * j])
        k2b[2 + j, 1] = coarsen_fine(ekr[2 + 2 * j] + ekr[3 + 2 * j])
    k3[FAR, 0] = coarsen_mid(k2a[2] + k2a[3])
    k3[FAR, 1] = coarsen_mid(k2b[2, 0] + k2b[3, 0])
    k3[FAR, 2] = coarsen_mid(k2b[2, 1] + k2b[3, 1])
    coarse = exchange([(k2a.at[2:4], k2a.at[0:2]), (k2b.at[3], k2b.at[1])],
                      [(k2a.at[2:4], k2a.at[4:6]), (k2b.at[2], k2b.at[4])])

    def hear(step):
        @pl.when(has_down(1))
        def _():
            pl.semaphore_wait(near.at[step, 0], 1)

        @pl.when(has_up(1))
        def _():
            pl.semaphore_wait(near.at[step, 1], 1)

    for step in range(2):
        hear(step)
        greet(near.at[step + 1, 0], near.at[step + 1, 1])

    bulk.wait_recv()
    for copy in relay:
        copy.wait_recv()
    for side, two, one in ((0, (0, 1), 1), (1, (6, 7), 6)):
        for i, slot, layer in ((0, 0, two[0]), (0, 1, two[1]), (1, 2, two[0]), (1, 3, two[1]), (2, 4, one), (3, 5, one)):
            unpack(xb[side, slot, 0], xb[side, slot, 1], ext[i], layer)
    layers(1, 3, fine_weights, first_sweep)
    layers(5, 7, fine_weights, first_sweep)

    hear(2)
    s3[0] = jnp.where(low3, k3[FAR, 0], k3[FAR, 1])
    far_k = []
    for d in range(1, FAR + 1):
        far_k.append(exchange([(s3.at[0], l3.at[0, FAR - d])], [(s3.at[0], l3.at[0, FAR + d])], d))

    coarse.wait_recv()
    for x in range(1, 5):
        m_down = {2: m_lo, 4: m_hi}.get(x, 1.0)
        m_up = {1: m_lo, 3: m_hi}.get(x, 1.0)
        w_down, w_up, w_inc, w_raan, dg = coarse_weights(
            k2a[x], k2a[x - 1], k2a[x + 1], m_down, m_up, k2b[x, 0], k2b[x, 1], 0.25, 2)
        for n, value in enumerate((w_down, w_up, w_inc, w_raan, dg, OMEGA / dg)):
            w2[x, n] = value

    swept.wait_recv()
    layers(1, 7, functools.partial(sweep_fine, v1, v2))

    def residual_fine(l):
        return target_fine(v2, l) - diag[l] * v2[l]

    for j in range(2):
        rhs2[2 + j] = coarsen_fine(residual_fine(2 + 2 * j) + residual_fine(3 + 2 * j))
        c2a[2 + j] = rhs2[2 + j] * w2[2 + j, 5]
    sb4[0, 0] = rhs2[3]
    sb4[0, 1] = c2a[2]
    sb4[1, 0] = rhs2[2]
    sb4[1, 1] = c2a[3]
    mid = exchange([(sb4.at[0], rb4.at[0])], [(sb4.at[1], rb4.at[1])])
    dens2 = exchange([(v2.at[4], v2.at[0])], [(v2.at[3], v2.at[7])])

    for copy in far_k:
        copy.wait_recv()
    for x in range(2 * FAR + 1):
        if x != FAR:
            k3[x, 0] = first_of(l3[0, x])
            k3[x, 1] = second_of(l3[0, x])

    def weights_far(x):
        at = a + x - FAR
        m_down = jnp.where(at == 0, 0.0, 1.0).astype(jnp.float32)
        m_up = jnp.where(at == n_alt - 1, 0.0, 1.0).astype(jnp.float32)
        w_down, w_up, w_inc, w_raan, dg = coarse_weights(
            k3[x, 0], k3[x - 1, 0], k3[x + 1, 0], m_down, m_up, k3[x, 1], k3[x, 2], 0.0625, 4)
        for n, value in enumerate((w_down, w_up, w_inc, w_raan, OMEGA / dg)):
            w3[x, n] = value

    weights_far(FAR)

    mid.wait_recv()
    rhs2[1] = rb4[0, 0]
    c2a[0] = rb4[0, 1]
    rhs2[4] = rb4[1, 0]
    c2a[5] = rb4[1, 1]
    c2a[1] = rhs2[1] * w2[1, 5]
    c2a[4] = rhs2[4] * w2[4, 5]

    def target_mid(src, x):
        return rhs2[x] + beside_coarse(src[x], src[x - 1], src[x + 1], w2[x, 0], w2[x, 1], w2[x, 2], w2[x, 3], 2)

    def sweep_mid(src, dst, x):
        dst[x] = 0.25 * src[x] + w2[x, 5] * target_mid(src, x)

    for x in range(1, 5):
        sweep_mid(c2a, c2b, x)
    residual = [target_mid(c2b, x) - w2[x, 4] * c2b[x] for x in (2, 3)]
    r3[FAR] = coarsen_mid(residual[0] + residual[1])
    c3[0, FAR] = r3[FAR] * w3[FAR, 4]
    s3[1] = jnp.where(low3, r3[FAR], k3[FAR, 2])
    s3[2] = c3[0, FAR]
    far = []
    for d in range(FAR, 0, -1):
        part = s3.at[1 if d < FAR else 2]
        far.append(exchange([(part, l3.at[1, FAR - d])], [(part, l3.at[1, FAR + d])], d))
    ends = exchange([(c2b.at[2], c2b.at[0])], [(c2b.at[3], c2b.at[5])])

    for copy in far:
        copy.wait_recv()
    for x in range(1, 2 * FAR):
        if x != FAR:
            r3[x] = first_of(l3[1, x])
            k3[x, 2] = second_of(l3[1, x])
            weights_far(x)
            c3[0, x] = r3[x] * w3[x, 4]
    for x in (0, 2 * FAR):
        c3[0, x] = l3[1, x]
    for n in range(3):
        for x in range(1 + n, 2 * FAR - n):
            v = c3[n, x]
            total = r3[x] + beside_coarse(v, c3[n, x - 1], c3[n, x + 1], w3[x, 0], w3[x, 1], w3[x, 2], w3[x, 3], 4)
            c3[n + 1, x] = 0.25 * v + w3[x, 4] * total

    ends.wait_recv()
    for j in range(3):
        part = twice(tmp2, c3[3, FAR - 1 + j])
        for x in (2 * j, 2 * j + 1):
            q0[x] = c2b[x] + part
    for x in range(1, 5):
        sweep_mid(q0, q1, x)
    for x in (2, 3):
        sweep_mid(q1, q2, x)
    up2 = exchange([(q2.at[3], q2.at[1])], [(q2.at[2], q2.at[4])])

    def refine_mid(x):
        c = q2[x]
        part_a = jnp.where(even2, c, lane_roll(c, 1))
        part_b = jnp.where(even2, lane_roll(c, -1), c)
        rf[x] = twice(tmp, jnp.concatenate([part_a, part_b], axis=0))

    def correct(x):
        refine_mid(x)
        for l in (2 * x - 2, 2 * x - 1):
            p0[l] = v2[l] + rf[x]

    correct(2)
    correct(3)
    last_sweep = functools.partial(sweep_fine, p0, p1)
    layers(3, 5, last_sweep)
    inner = exchange([(p1.at[4], p1.at[0])], [(p1.at[3], p1.at[7])])
    dens2.wait_recv()
    up2.wait_recv()
    correct(1)
    correct(4)
    layers(1, 3, last_sweep)
    layers(5, 7, last_sweep)
    layers(2, 6, functools.partial(sweep_fine, p1, p2))
    outs = [pltpu.make_async_copy(p2.at[own, :, cols], dens_hbm, out_sem.at[0])]
    outs[0].start()

    def last_residual(l):
        value = (1.0 / OMEGA) * (invd[l] * target_fine(p2, l)) - p2[l]
        sres[l - HALO] = value[:, 0:COLS]

    layers(3, 5, last_residual)
    inner.wait_recv()
    sweep_fine(p1, p2, 1)
    sweep_fine(p1, p2, 6)
    last_residual(2)
    last_residual(5)
    outs.append(pltpu.make_async_copy(sres, sres_hbm, out_sem.at[1]))
    outs[1].start()
    for copy in sends:
        copy.wait_send()
    for copy in outs:
        copy.wait()


def solution(mesh):
    n_alt, n_raan = mesh.shape["alt"], mesh.shape["raan"]
    spec = P("alt", None, "raan")
    anywhere = pl.BlockSpec(memory_space=pl.ANY)

    def vmem(*shape):
        return pltpu.VMEM(shape, jnp.float32)

    def shards(source, k_alt, k_inc, k_raan):
        scratch = [vmem(LAYERS, INC, WIDE)] * 14 + [vmem(OWN, INC, COLS)]
        scratch += [vmem(4, OWN, 2, 16, 128), vmem(4, OWN, 2, 16, 128), vmem(2, 6, 2, 16, 128),
                    vmem(TILES, INC, 128), vmem(TILES, 16, 128)]
        scratch += [vmem(6, 16, WIDE), vmem(6, 2, 16, WIDE), vmem(6, 6, 16, WIDE), vmem(2, 2, 16, WIDE),
                    vmem(2, 2, 16, WIDE)] + [vmem(6, 16, WIDE)] * 6 + [vmem(6, INC, WIDE)]
        scratch += [vmem(2 * FAR + 1, 3, 8, WIDE), vmem(2 * FAR + 1, 5, 8, WIDE), vmem(2 * FAR + 1, 8, WIDE),
                    vmem(4, 2 * FAR + 1, 8, WIDE), vmem(3, 8, WIDE), vmem(2, 2 * FAR + 1, 8, WIDE)]
        scratch += [pltpu.SemaphoreType.DMA((4,)), pltpu.SemaphoreType.DMA((2,)),
                    pltpu.SemaphoreType.DMA((64,)), pltpu.SemaphoreType.DMA((64,)),
                    pltpu.SemaphoreType.REGULAR((3, 2))]
        shape = jax.ShapeDtypeStruct(source.shape, source.dtype)
        return pl.pallas_call(
            functools.partial(kernel, n_alt, n_raan),
            out_shape=(shape, shape),
            in_specs=[pl.BlockSpec(memory_space=pltpu.HBM)] * 4,
            out_specs=(anywhere, anywhere),
            scratch_shapes=scratch,
            compiler_params=pltpu.CompilerParams(
                collective_id=0, has_side_effects=True, vmem_limit_bytes=64 * 1024 * 1024 - 512 * 1024),
            name="vcycle",
        )(source, k_alt, k_inc, k_raan)

    return jax.shard_map(shards, mesh=mesh, in_specs=(spec,) * 4, out_specs=(spec, spec), check_vma=False)
```

```python
import functools

import jax
import jax.numpy as jnp
from jax import lax
from jax.experimental import pallas as pl
from jax.experimental.pallas import tpu as pltpu
from jax.sharding import PartitionSpec as P

OMEGA = 0.75
MESH = pl.DeviceIdType.MESH

INC = 64
COLS = 256
WIDE = 384
HALO = 2
OWN = 4
TILES = WIDE // 128
LAYERS = OWN + 2 * HALO
FAR = 4


def lane_roll(x, shift):
    return pltpu.roll(x, shift % x.shape[-1], axis=x.ndim - 1)


def row_roll(x, shift):
    return pltpu.roll(x, shift % x.shape[-2], axis=x.ndim - 2)


def iota(shape, dim):
    return lax.broadcasted_iota(jnp.int32, shape, dim)


def beside_fine(v, down, up, w_down, w_up, w_inc, w_raan):
    total = w_down * down + w_up * up
    total = total + w_inc * row_roll(v, 1) + row_roll(w_inc * v, -1)
    return total + w_raan * lane_roll(v, 1) + lane_roll(w_raan * v, -1)


def prev_row(v):
    turned = row_roll(v, 1)
    return jnp.where(iota(v.shape, 0) == 0, lane_roll(turned, 1), turned)


def next_row(v):
    turned = row_roll(v, -1)
    return jnp.where(iota(v.shape, 0) == v.shape[0] - 1, lane_roll(turned, -1), turned)


def coarse_weights(k_alt, k_down, k_up, m_down, m_up, k_inc, k_raan, factor, step):
    half = 0.5 * factor
    lo = half * (k_alt + m_down * k_down)
    hi = half * (k_alt + m_up * k_up)
    outer = (iota(k_inc.shape, 0) == 0) & (iota(k_inc.shape, 1) % 2 == 0)
    w_inc = jnp.where(outer, 0.0, half * (k_inc + prev_row(k_inc)))
    w_raan = half * (k_raan + lane_roll(k_raan, step))
    diagonal = 1.0 + (lo + hi + w_inc + next_row(w_inc) + w_raan + lane_roll(w_raan, -step))
    return m_down * lo, m_up * hi, w_inc, w_raan, diagonal


def beside_coarse(v, down, up, w_down, w_up, w_inc, w_raan, step):
    total = w_down * down + w_up * up
    total = total + w_inc * prev_row(v) + next_row(w_inc * v)
    return total + w_raan * lane_roll(v, step) + lane_roll(w_raan * v, -step)


class Exchange:
    def __init__(self, ups, downs, distance, has_up, has_down):
        self.ups, self.downs = ups, downs
        self.has_up, self.has_down = has_up(distance), has_down(distance)

    def start(self):
        @pl.when(self.has_up)
        def _():
            for copy in self.ups:
                copy.start()

        @pl.when(self.has_down)
        def _():
            for copy in self.downs:
                copy.start()

    def wait_recv(self):
        @pl.when(self.has_down)
        def _():
            for copy in self.ups:
                copy.wait_recv()

        @pl.when(self.has_up)
        def _():
            for copy in self.downs:
                copy.wait_recv()

    def wait_send(self):
        @pl.when(self.has_up)
        def _():
            for copy in self.ups:
                copy.wait_send()

        @pl.when(self.has_down)
        def _():
            for copy in self.downs:
                copy.wait_send()


def kernel(n_alt, n_raan, f_hbm, ka_hbm, ki_hbm, kr_hbm, dens, sres,
           ef, eka, eki, ekr, v1, v2, p0, p1, p2, wa, wi, wr, invd, diag,
           pack, rb, xb, tmp, tmp2,
           k2a, k2b, w2, sb4, rb4, rhs2, c2a, c2b, q0, q1, q2, rf,
           k3, w3, r3, c3, sk, lk,
           load_sem, send_sem, recv_sem, near):
    a = lax.axis_index("alt")
    r = lax.axis_index("raan")
    m_lo = jnp.where(a == 0, 0.0, 1.0).astype(jnp.float32)
    m_hi = jnp.where(a == n_alt - 1, 0.0, 1.0).astype(jnp.float32)

    def has_up(d):
        return a < n_alt - d

    def has_down(d):
        return a >= d

    def alt_dev(d):
        return (lax.rem(a + d + n_alt, n_alt), r)

    def raan_dev(d):
        return (a, lax.rem(r + d + n_raan, n_raan))

    count = [0]
    sends = []

    def describe(src, dst, device):
        k = count[0]
        count[0] += 1
        return pltpu.make_async_remote_copy(
            src_ref=src, dst_ref=dst, send_sem=send_sem.at[k], recv_sem=recv_sem.at[k],
            device_id=device, device_id_type=MESH)

    def remote(src, dst, device):
        copy = describe(src, dst, device)
        copy.start()
        sends.append(copy)
        return copy

    def exchange(ups, downs, distance=1):
        copy = Exchange([describe(s, d, alt_dev(distance)) for s, d in ups],
                        [describe(s, d, alt_dev(-distance)) for s, d in downs], distance, has_up, has_down)
        copy.start()
        sends.append(copy)
        return copy

    hbm = (f_hbm, ka_hbm, ki_hbm, kr_hbm)
    ext = (ef, eka, eki, ekr)
    cols = slice(0, COLS)
    own = slice(HALO, HALO + OWN)
    loads = []
    for i in range(4):
        loads.append(pltpu.make_async_copy(hbm[i], ext[i].at[own, :, cols], load_sem.at[i]))

    barrier = pltpu.get_barrier_semaphore()

    def greet(sem_up, sem_down):
        @pl.when(has_up(1))
        def _():
            pl.semaphore_signal(sem_up, inc=1, device_id=alt_dev(1), device_id_type=MESH)

        @pl.when(has_down(1))
        def _():
            pl.semaphore_signal(sem_down, inc=1, device_id=alt_dev(-1), device_id_type=MESH)

    greet(barrier, barrier)
    for side in (1, -1):
        pl.semaphore_signal(barrier, inc=1, device_id=raan_dev(side), device_id_type=MESH)
    for i in range(4):
        loads[i].start()

    @pl.when(a == 0)
    def _():
        for ref in (ef, eka, eki, ekr, v1, v2, p1):
            ref[0:HALO] = jnp.zeros((HALO, INC, WIDE), jnp.float32)
        xb[0] = jnp.zeros(xb.shape[1:], jnp.float32)
        rb4[0] = jnp.zeros(rb4.shape[1:], jnp.float32)
        for ref in (k2a, k2b, c2b, q2):
            ref[0:2] = jnp.zeros((2,) + ref.shape[1:], jnp.float32)

    @pl.when(a == n_alt - 1)
    def _():
        for ref in (ef, eka, eki, ekr, v1, v2, p1):
            ref[HALO + OWN:LAYERS] = jnp.zeros((HALO, INC, WIDE), jnp.float32)
        xb[1] = jnp.zeros(xb.shape[1:], jnp.float32)
        rb4[1] = jnp.zeros(rb4.shape[1:], jnp.float32)
        for ref in (k2a, k2b, c2b, q2):
            ref[4:6] = jnp.zeros((2,) + ref.shape[1:], jnp.float32)

    for d in range(1, FAR + 1):
        for side, here in ((d, has_up(d)), (-d, has_down(d))):
            @pl.when(jnp.logical_not(here))
            def _():
                lk[FAR + side] = jnp.zeros((2, 8, WIDE), jnp.float32)
                r3[FAR + side] = jnp.zeros((8, WIDE), jnp.float32)
                c3[0, FAR + side] = jnp.zeros((8, WIDE), jnp.float32)

    pl.semaphore_wait(barrier, 2 + has_up(1).astype(jnp.int32) + has_down(1).astype(jnp.int32))

    def hear(step):
        @pl.when(has_down(1))
        def _():
            pl.semaphore_wait(near.at[step, 0], 1)

        @pl.when(has_up(1))
        def _():
            pl.semaphore_wait(near.at[step, 1], 1)

    greet(near.at[0, 0], near.at[0, 1])

    low2, high2, low1, high1 = slice(0, 2), slice(2, 4), slice(0, 1), slice(3, 4)
    below2, above2, below1, above1 = slice(0, 2), slice(6, 8), slice(1, 2), slice(6, 7)
    bulk = exchange(
        [(hbm[i].at[high2 if i < 2 else high1], ext[i].at[below2 if i < 2 else below1, :, cols]) for i in range(4)],
        [(hbm[i].at[low2 if i < 2 else low1], ext[i].at[above2 if i < 2 else above1, :, cols]) for i in range(4)])

    quarter = iota((16, 128), 1) // 32
    ring = []
    for i in range(4):
        loads[i].wait()
        for l in range(OWN):
            low = ext[i][HALO + l, :, 0:128]
            high = ext[i][HALO + l, :, 128:256]
            first = low[0:16]
            last = high[0:16]
            for g in range(1, 4):
                first = jnp.where(quarter == g, lane_roll(low[16 * g:16 * g + 16], 32 * g), first)
                last = jnp.where(quarter == (3 + g) % 4, lane_roll(high[16 * g:16 * g + 16], 32 * g), last)
            pack[i, l, 0] = first
            pack[i, l, 1] = last
        ring.append((remote(pack.at[i, :, 0], rb.at[i, :, 0], raan_dev(-1)),
                     remote(pack.at[i, :, 1], rb.at[i, :, 1], raan_dev(1))))

    def unpack(first, last, dst, layer):
        for g in range(4):
            both = jnp.where(quarter == g, first, last)
            dst[layer, 16 * g:16 * g + 16, COLS:WIDE] = lane_roll(both, -32 * g) if g else both

    relay = []
    x_slot = (slice(0, 2), slice(2, 4), slice(4, 5), slice(5, 6))
    for i in range(4):
        for copy in ring[i]:
            copy.wait_recv()
        relay.append(exchange([(rb.at[i, high2 if i < 2 else high1], xb.at[0, x_slot[i]])],
                              [(rb.at[i, low2 if i < 2 else low1], xb.at[1, x_slot[i]])]))
        if i == 1:
            hear(0)
            greet(near.at[1, 0], near.at[1, 1])
        for l in range(OWN):
            unpack(rb[i, l, 0], rb[i, l, 1], ext[i], HALO + l)

    row0 = iota((INC, WIDE), 0) == 0

    def fine_weights(l):
        m_down = jnp.where(l == HALO, m_lo, jnp.where(l == HALO + OWN, m_hi, 1.0))
        m_up = jnp.where(l == HALO - 1, m_lo, jnp.where(l == HALO + OWN - 1, m_hi, 1.0))
        k_alt = eka[l]
        lo = 0.5 * (k_alt + m_down * eka[l - 1])
        hi = 0.5 * (k_alt + m_up * eka[l + 1])
        k_inc = eki[l]
        w_inc = jnp.where(row0, 0.0, 0.5 * (k_inc + row_roll(k_inc, 1)))
        k_raan = ekr[l]
        w_raan = 0.5 * (k_raan + lane_roll(k_raan, 1))
        dg = 1.0 + (lo + hi + w_inc + row_roll(w_inc, -1) + w_raan + lane_roll(w_raan, -1))
        wa[l - 1] = m_down * lo
        wa[l] = m_up * hi
        wi[l] = w_inc
        wr[l] = w_raan
        diag[l] = dg
        invd[l] = OMEGA / dg

    def target_fine(src, l):
        return ef[l] + beside_fine(src[l], src[l - 1], src[l + 1], wa[l - 1], wa[l], wi[l], wr[l])

    def sweep_fine(src, dst, l):
        dst[l] = 0.25 * src[l] + invd[l] * target_fine(src, l)

    def layers(lo, hi, *bodies):
        def body(l, carry):
            for one in bodies:
                one(l)
            return carry
        lax.fori_loop(lo, hi, body, 0)

    first_sweep = functools.partial(sweep_fine, ef, v1)
    layers(3, 5, fine_weights, first_sweep)
    swept = exchange([(v1.at[4], v1.at[0])], [(v1.at[3], v1.at[7])])

    even2 = iota((16, WIDE), 1) % 2 == 0

    def row_pairs(scratch, x):
        n = x.shape[0] // 2
        for t in range(TILES):
            scratch[t] = x[:, 128 * t:128 * t + 128]
        return jnp.concatenate(
            [scratch[t, pl.ds(0, n, stride=2)] + scratch[t, pl.ds(1, n, stride=2)] for t in range(TILES)], axis=1)

    def twice(scratch, x):
        n = x.shape[0]
        for t in range(TILES):
            part = x[:, 128 * t:128 * t + 128]
            scratch[t, pl.ds(0, n, stride=2)] = part
            scratch[t, pl.ds(1, n, stride=2)] = part
        return jnp.concatenate([scratch[t] for t in range(TILES)], axis=1)

    def coarsen_fine(total):
        pairs = row_pairs(tmp, total)
        t_a, t_b = pairs[0:16], pairs[16:32]
        return 0.125 * (jnp.where(even2, t_a, t_b) + jnp.where(even2, lane_roll(t_a, -1), lane_roll(t_b, 1)))

    low3 = iota((8, WIDE), 1) % 4 < 2

    def coarsen_mid(total):
        t = row_pairs(tmp2, total)
        return 0.125 * (t + jnp.where(low3, lane_roll(t, -2), lane_roll(t, 2)))

    def first_of(pair):
        return jnp.where(low3, pair, lane_roll(pair, 2))

    def second_of(pair):
        return jnp.where(low3, lane_roll(pair, -2), pair)

    for j in range(2):
        k2a[2 + j] = coarsen_fine(eka[2 + 2 * j] + eka[3 + 2 * j])
        k2b[2 + j, 0] = coarsen_fine(eki[2 + 2 * j] + eki[3 + 2 * j])
        k2b[2 + j, 1] = coarsen_fine(ekr[2 + 2 * j] + ekr[3 + 2 * j])
    k3[FAR, 0] = coarsen_mid(k2a[2] + k2a[3])
    k3[FAR, 1] = coarsen_mid(k2b[2, 0] + k2b[3, 0])
    k3[FAR, 2] = coarsen_mid(k2b[2, 1] + k2b[3, 1])
    coarse_alt = exchange([(k2a.at[3], k2a.at[1])], [(k2a.at[2], k2a.at[4])])
    coarse = exchange([(k2a.at[2], k2a.at[0]), (k2b.at[3], k2b.at[1])],
                      [(k2a.at[3], k2a.at[5]), (k2b.at[2], k2b.at[4])])
    sk[0] = jnp.where(low3, k3[FAR, 0], k3[FAR, 1])
    sk[1] = k3[FAR, 2]
    far_k = []

    def send_far_k(d):
        part = slice(0, 2) if d < FAR else slice(0, 1)
        far_k.append(exchange([(sk.at[part], lk.at[FAR - d, part])], [(sk.at[part], lk.at[FAR + d, part])], d))

    send_far_k(1)
    send_far_k(2)
    hear(1)
    greet(near.at[2, 0], near.at[2, 1])
    send_far_k(3)

    bulk.wait_recv()
    for copy in relay:
        copy.wait_recv()
    for side, two, one in ((0, (0, 1), 1), (1, (6, 7), 6)):
        for i, slot, layer in ((0, 0, two[0]), (0, 1, two[1]), (1, 2, two[0]), (1, 3, two[1]), (2, 4, one), (3, 5, one)):
            unpack(xb[side, slot, 0], xb[side, slot, 1], ext[i], layer)
    layers(1, 3, fine_weights, first_sweep)
    layers(5, 7, fine_weights, first_sweep)

    def weights_mid(x):
        m_down = {2: m_lo, 4: m_hi}.get(x, 1.0)
        m_up = {1: m_lo, 3: m_hi}.get(x, 1.0)
        w_down, w_up, w_inc, w_raan, dg = coarse_weights(
            k2a[x], k2a[x - 1], k2a[x + 1], m_down, m_up, k2b[x, 0], k2b[x, 1], 0.25, 2)
        for n, value in enumerate((w_down, w_up, w_inc, w_raan, dg, OMEGA / dg)):
            w2[x, n] = value

    second_sweep = functools.partial(sweep_fine, v1, v2)
    layers(2, 6, second_sweep)

    def residual_fine(l):
        return target_fine(v2, l) - diag[l] * v2[l]

    for l in (3, 4):
        p2[l] = residual_fine(l)
    swept.wait_recv()
    second_sweep(1)
    second_sweep(6)
    coarse_alt.wait_recv()
    weights_mid(2)
    weights_mid(3)
    for j in range(2):
        rhs2[2 + j] = coarsen_fine(p2[3 + j] + residual_fine(2 + 3 * j))
        c2a[2 + j] = rhs2[2 + j] * w2[2 + j, 5]
    sb4[0, 0] = rhs2[3]
    sb4[0, 1] = c2a[2]
    sb4[1, 0] = rhs2[2]
    sb4[1, 1] = c2a[3]
    mid = exchange([(sb4.at[0], rb4.at[0])], [(sb4.at[1], rb4.at[1])])
    dens2 = exchange([(v2.at[4], v2.at[0])], [(v2.at[3], v2.at[7])])

    hear(2)
    send_far_k(4)
    coarse.wait_recv()
    weights_mid(1)
    weights_mid(4)

    def weights_far(x):
        at = a + x - FAR
        m_down = jnp.where(at == 0, 0.0, 1.0).astype(jnp.float32)
        m_up = jnp.where(at == n_alt - 1, 0.0, 1.0).astype(jnp.float32)
        w_down, w_up, w_inc, w_raan, dg = coarse_weights(
            k3[x, 0], k3[x - 1, 0], k3[x + 1, 0], m_down, m_up, k3[x, 1], k3[x, 2], 0.0625, 4)
        for n, value in enumerate((w_down, w_up, w_inc, w_raan, OMEGA / dg)):
            w3[x, n] = value

    def take_far(x):
        k3[x, 0] = first_of(lk[x, 0])
        if x not in (0, 2 * FAR):
            k3[x, 1] = second_of(lk[x, 0])
            k3[x, 2] = lk[x, 1]

    for copy in far_k[0:3]:
        copy.wait_recv()
    for x in range(1, 2 * FAR):
        if x != FAR:
            take_far(x)
    for x in range(2, 2 * FAR - 1):
        weights_far(x)

    mid.wait_recv()
    rhs2[1] = rb4[0, 0]
    c2a[0] = rb4[0, 1]
    rhs2[4] = rb4[1, 0]
    c2a[5] = rb4[1, 1]
    c2a[1] = rhs2[1] * w2[1, 5]
    c2a[4] = rhs2[4] * w2[4, 5]

    def target_mid(src, x):
        return rhs2[x] + beside_coarse(src[x], src[x - 1], src[x + 1], w2[x, 0], w2[x, 1], w2[x, 2], w2[x, 3], 2)

    def sweep_mid(src, dst, x):
        dst[x] = 0.25 * src[x] + w2[x, 5] * target_mid(src, x)

    for x in range(1, 5):
        sweep_mid(c2a, c2b, x)
    residual = [target_mid(c2b, x) - w2[x, 4] * c2b[x] for x in (2, 3)]
    r3[FAR] = coarsen_mid(residual[0] + residual[1])
    c3[0, FAR] = r3[FAR] * w3[FAR, 4]
    far = []
    for d in range(FAR, 0, -1):
        part = r3 if d < FAR else c3.at[0]
        far.append(exchange([(part.at[FAR], part.at[FAR - d])], [(part.at[FAR], part.at[FAR + d])], d))
    ends = exchange([(c2b.at[2], c2b.at[0])], [(c2b.at[3], c2b.at[5])])

    far_k[3].wait_recv()
    for x in (0, 2 * FAR):
        take_far(x)
    for x in (1, 2 * FAR - 1):
        weights_far(x)
    for copy in far:
        copy.wait_recv()
    for x in range(1, 2 * FAR):
        if x != FAR:
            c3[0, x] = r3[x] * w3[x, 4]
    for n in range(3):
        for x in range(1 + n, 2 * FAR - n):
            v = c3[n, x]
            total = r3[x] + beside_coarse(v, c3[n, x - 1], c3[n, x + 1], w3[x, 0], w3[x, 1], w3[x, 2], w3[x, 3], 4)
            c3[n + 1, x] = 0.25 * v + w3[x, 4] * total

    ends.wait_recv()
    for j in range(3):
        part = twice(tmp2, c3[3, FAR - 1 + j])
        for x in (2 * j, 2 * j + 1):
            q0[x] = c2b[x] + part
    for x in range(1, 5):
        sweep_mid(q0, q1, x)
    for x in (2, 3):
        sweep_mid(q1, q2, x)
    up2 = exchange([(q2.at[3], q2.at[1])], [(q2.at[2], q2.at[4])])

    def refine_mid(x):
        c = q2[x]
        part_a = jnp.where(even2, c, lane_roll(c, 1))
        part_b = jnp.where(even2, lane_roll(c, -1), c)
        rf[x] = twice(tmp, jnp.concatenate([part_a, part_b], axis=0))

    def correct(x):
        refine_mid(x)
        for l in (2 * x - 2, 2 * x - 1):
            p0[l] = v2[l] + rf[x]

    correct(2)
    correct(3)
    last_sweep = functools.partial(sweep_fine, p0, p1)
    layers(3, 5, last_sweep)
    inner = exchange([(p1.at[4, :, cols], p1.at[0, :, cols])], [(p1.at[3, :, cols], p1.at[7, :, cols])])
    dens2.wait_recv()
    up2.wait_recv()
    correct(1)
    correct(4)
    layers(1, 3, last_sweep)
    layers(5, 7, last_sweep)
    def final_sweep(l):
        sweep_fine(p1, p2, l)
        dens[l - HALO] = p2[l, :, cols]

    def last_residual(l):
        value = (1.0 / OMEGA) * (invd[l] * target_fine(p2, l)) - p2[l]
        sres[l - HALO] = value[:, 0:COLS]

    layers(2, 6, final_sweep)
    layers(3, 5, last_residual)
    inner.wait_recv()
    sweep_fine(p1, p2, 1)
    sweep_fine(p1, p2, 6)
    last_residual(2)
    last_residual(5)
    for copy in sends:
        copy.wait_send()


def solution(mesh):
    n_alt, n_raan = mesh.shape["alt"], mesh.shape["raan"]
    spec = P("alt", None, "raan")

    def vmem(*shape):
        return pltpu.VMEM(shape, jnp.float32)

    def shards(source, k_alt, k_inc, k_raan):
        scratch = [vmem(LAYERS, INC, WIDE)] * 14
        scratch += [vmem(4, OWN, 2, 16, 128), vmem(4, OWN, 2, 16, 128), vmem(2, 6, 2, 16, 128),
                    vmem(TILES, INC, 128), vmem(TILES, 16, 128)]
        scratch += [vmem(6, 16, WIDE), vmem(6, 2, 16, WIDE), vmem(6, 6, 16, WIDE), vmem(2, 2, 16, WIDE),
                    vmem(2, 2, 16, WIDE)] + [vmem(6, 16, WIDE)] * 6 + [vmem(6, INC, WIDE)]
        scratch += [vmem(2 * FAR + 1, 3, 8, WIDE), vmem(2 * FAR + 1, 5, 8, WIDE), vmem(2 * FAR + 1, 8, WIDE),
                    vmem(4, 2 * FAR + 1, 8, WIDE), vmem(2, 8, WIDE), vmem(2 * FAR + 1, 2, 8, WIDE)]
        scratch += [pltpu.SemaphoreType.DMA((4,)),
                    pltpu.SemaphoreType.DMA((64,)), pltpu.SemaphoreType.DMA((64,)),
                    pltpu.SemaphoreType.REGULAR((3, 2))]
        shape = pltpu.VMEM(source.shape, source.dtype)
        return pl.pallas_call(
            functools.partial(kernel, n_alt, n_raan),
            out_shape=(shape, shape),
            in_specs=[pl.BlockSpec(memory_space=pltpu.HBM)] * 4,
            out_specs=(pl.BlockSpec(memory_space=pltpu.VMEM),) * 2,
            scratch_shapes=scratch,
            compiler_params=pltpu.CompilerParams(
                collective_id=0, has_side_effects=True, vmem_limit_bytes=60 * 1024 * 1024),
            name="vcycle",
        )(source, k_alt, k_inc, k_raan)

    return jax.shard_map(shards, mesh=mesh, in_specs=(spec,) * 4, out_specs=(spec, spec), check_vma=False)
```

```python
import functools

import jax
import jax.numpy as jnp
from jax import lax
from jax.experimental import pallas as pl
from jax.experimental.pallas import tpu as pltpu
from jax.sharding import PartitionSpec as P

OMEGA = 0.75
MESH = pl.DeviceIdType.MESH

INC = 64
COLS = 256
WIDE = 384
HALO = 2
OWN = 4
TILES = WIDE // 128
LAYERS = OWN + 2 * HALO
FAR = 4


def lane_roll(x, shift):
    return pltpu.roll(x, shift % x.shape[-1], axis=x.ndim - 1)


def row_roll(x, shift):
    return pltpu.roll(x, shift % x.shape[-2], axis=x.ndim - 2)


def iota(shape, dim):
    return lax.broadcasted_iota(jnp.int32, shape, dim)


def beside_fine(v, down, up, w_down, w_up, w_inc, w_raan):
    total = w_down * down + w_up * up
    total = total + w_inc * row_roll(v, 1) + row_roll(w_inc * v, -1)
    return total + w_raan * lane_roll(v, 1) + lane_roll(w_raan * v, -1)


def prev_row(v):
    turned = row_roll(v, 1)
    top = turned[0:8]
    top = jnp.where(iota(top.shape, 0) == 0, lane_roll(top, 1), top)
    return top if v.shape[0] == 8 else jnp.concatenate([top, turned[8:]], axis=0)


def next_row(v):
    turned = row_roll(v, -1)
    end = turned[-8:]
    end = jnp.where(iota(end.shape, 0) == 7, lane_roll(end, -1), end)
    return end if v.shape[0] == 8 else jnp.concatenate([turned[:-8], end], axis=0)


def coarse_weights(k_alt, k_down, k_up, m_down, m_up, k_inc, k_raan, factor, step):
    half = 0.5 * factor
    lo = half * (k_alt + m_down * k_down)
    hi = half * (k_alt + m_up * k_up)
    outer = (iota(k_inc.shape, 0) == 0) & (iota(k_inc.shape, 1) % 2 == 0)
    w_inc = jnp.where(outer, 0.0, half * (k_inc + prev_row(k_inc)))
    w_raan = half * (k_raan + lane_roll(k_raan, step))
    diagonal = 1.0 + (lo + hi + w_inc + next_row(w_inc) + w_raan + lane_roll(w_raan, -step))
    return m_down * lo, m_up * hi, w_inc, w_raan, diagonal


def beside_coarse(v, down, up, w_down, w_up, w_inc, w_raan, step):
    total = w_down * down + w_up * up
    total = total + w_inc * prev_row(v) + next_row(w_inc * v)
    return total + w_raan * lane_roll(v, step) + lane_roll(w_raan * v, -step)


class Exchange:
    def __init__(self, ups, downs, distance, has_up, has_down):
        self.ups, self.downs = ups, downs
        self.has_up, self.has_down = has_up(distance), has_down(distance)

    def start(self):
        @pl.when(self.has_up)
        def _():
            for copy in self.ups:
                copy.start()

        @pl.when(self.has_down)
        def _():
            for copy in self.downs:
                copy.start()

    def wait_recv(self):
        @pl.when(self.has_down)
        def _():
            for copy in self.ups:
                copy.wait_recv()

        @pl.when(self.has_up)
        def _():
            for copy in self.downs:
                copy.wait_recv()

    def wait_send(self):
        @pl.when(self.has_up)
        def _():
            for copy in self.ups:
                copy.wait_send()

        @pl.when(self.has_down)
        def _():
            for copy in self.downs:
                copy.wait_send()


def kernel(n_alt, n_raan, f_hbm, ka_hbm, ki_hbm, kr_hbm, dens, sres,
           ef, eka, eki, ekr, v1, v2, p0, p1, p2, wa, wi, wr, invd, diag,
           pack, rb, xb, tmp, tmp2,
           k2a, k2b, w2, sb4, rb4, rhs2, c2a, c2b, q2, rf,
           k3, w3, r3, sk, lk, sr, lr,
           load_sem, send_sem, recv_sem, near):
    a = lax.axis_index("alt")
    r = lax.axis_index("raan")
    m_lo = jnp.where(a == 0, 0.0, 1.0).astype(jnp.float32)
    m_hi = jnp.where(a == n_alt - 1, 0.0, 1.0).astype(jnp.float32)

    def has_up(d):
        return a < n_alt - d

    def has_down(d):
        return a >= d

    def alt_dev(d):
        return (lax.rem(a + d + n_alt, n_alt), r)

    def raan_dev(d):
        return (a, lax.rem(r + d + n_raan, n_raan))

    count = [0]
    sends = []

    def describe(src, dst, device):
        k = count[0]
        count[0] += 1
        return pltpu.make_async_remote_copy(
            src_ref=src, dst_ref=dst, send_sem=send_sem.at[k], recv_sem=recv_sem.at[k],
            device_id=device, device_id_type=MESH)

    def remote(src, dst, device):
        copy = describe(src, dst, device)
        copy.start()
        sends.append(copy)
        return copy

    def exchange(ups, downs, distance=1):
        copy = Exchange([describe(s, d, alt_dev(distance)) for s, d in ups],
                        [describe(s, d, alt_dev(-distance)) for s, d in downs], distance, has_up, has_down)
        copy.start()
        sends.append(copy)
        return copy

    hbm = (f_hbm, ka_hbm, ki_hbm, kr_hbm)
    ext = (ef, eka, eki, ekr)
    cols = slice(0, COLS)
    own = slice(HALO, HALO + OWN)
    loads = []
    for i in range(4):
        loads.append(pltpu.make_async_copy(hbm[i], ext[i].at[own, :, cols], load_sem.at[i]))

    barrier = pltpu.get_barrier_semaphore()

    def greet(sem_up, sem_down):
        @pl.when(has_up(1))
        def _():
            pl.semaphore_signal(sem_up, inc=1, device_id=alt_dev(1), device_id_type=MESH)

        @pl.when(has_down(1))
        def _():
            pl.semaphore_signal(sem_down, inc=1, device_id=alt_dev(-1), device_id_type=MESH)

    greet(barrier, barrier)
    for side in (1, -1):
        pl.semaphore_signal(barrier, inc=1, device_id=raan_dev(side), device_id_type=MESH)
    for i in range(4):
        loads[i].start()

    @pl.when(a == 0)
    def _():
        for ref in (ef, eka, eki, ekr, v1, v2, p1):
            ref[0:HALO] = jnp.zeros((HALO, INC, WIDE), jnp.float32)
        xb[0] = jnp.zeros(xb.shape[1:], jnp.float32)
        rb4[0] = jnp.zeros(rb4.shape[1:], jnp.float32)
        for ref in (k2a, k2b, c2b, q2):
            ref[0:2] = jnp.zeros((2,) + ref.shape[1:], jnp.float32)

    @pl.when(a == n_alt - 1)
    def _():
        for ref in (ef, eka, eki, ekr, v1, v2, p1):
            ref[HALO + OWN:LAYERS] = jnp.zeros((HALO, INC, WIDE), jnp.float32)
        xb[1] = jnp.zeros(xb.shape[1:], jnp.float32)
        rb4[1] = jnp.zeros(rb4.shape[1:], jnp.float32)
        for ref in (k2a, k2b, c2b, q2):
            ref[4:6] = jnp.zeros((2,) + ref.shape[1:], jnp.float32)

    for d in range(1, FAR + 1):
        for side, here in ((d, has_up(d)), (-d, has_down(d))):
            @pl.when(jnp.logical_not(here))
            def _():
                lk[FAR + side] = jnp.zeros((3, 4, WIDE), jnp.float32)
                lr[FAR + side] = jnp.zeros((4, WIDE), jnp.float32)

    pl.semaphore_wait(barrier, 2 + has_up(1).astype(jnp.int32) + has_down(1).astype(jnp.int32))

    def hear(step):
        @pl.when(has_down(1))
        def _():
            pl.semaphore_wait(near.at[step, 0], 1)

        @pl.when(has_up(1))
        def _():
            pl.semaphore_wait(near.at[step, 1], 1)

    greet(near.at[0, 0], near.at[0, 1])

    low2, high2, low1, high1 = slice(0, 2), slice(2, 4), slice(0, 1), slice(3, 4)
    below2, above2, below1, above1 = slice(0, 2), slice(6, 8), slice(1, 2), slice(6, 7)
    bulk = exchange(
        [(hbm[i].at[high2 if i < 2 else high1], ext[i].at[below2 if i < 2 else below1, :, cols]) for i in range(4)],
        [(hbm[i].at[low2 if i < 2 else low1], ext[i].at[above2 if i < 2 else above1, :, cols]) for i in range(4)])

    quarter = iota((16, 128), 1) // 32
    ring = []
    for i in range(4):
        loads[i].wait()
        for l in range(OWN):
            low = ext[i][HALO + l, :, 0:128]
            high = ext[i][HALO + l, :, 128:256]
            first = low[0:16]
            last = high[0:16]
            for g in range(1, 4):
                first = jnp.where(quarter == g, lane_roll(low[16 * g:16 * g + 16], 32 * g), first)
                last = jnp.where(quarter == (3 + g) % 4, lane_roll(high[16 * g:16 * g + 16], 32 * g), last)
            pack[i, l, 0] = first
            pack[i, l, 1] = last
        ring.append((remote(pack.at[i, :, 0], rb.at[i, :, 0], raan_dev(-1)),
                     remote(pack.at[i, :, 1], rb.at[i, :, 1], raan_dev(1))))

    def unpack(first, last, dst, layer):
        for g in range(4):
            both = jnp.where(quarter == g, first, last)
            dst[layer, 16 * g:16 * g + 16, COLS:WIDE] = lane_roll(both, -32 * g) if g else both

    relay = []
    x_slot = (slice(0, 2), slice(2, 4), slice(4, 5), slice(5, 6))
    for i in range(4):
        for copy in ring[i]:
            copy.wait_recv()
        relay.append(exchange([(rb.at[i, high2 if i < 2 else high1], xb.at[0, x_slot[i]])],
                              [(rb.at[i, low2 if i < 2 else low1], xb.at[1, x_slot[i]])]))
        if i == 1:
            hear(0)
            greet(near.at[1, 0], near.at[1, 1])
        for l in range(OWN):
            unpack(rb[i, l, 0], rb[i, l, 1], ext[i], HALO + l)

    row0 = iota((INC, WIDE), 0) == 0

    def fine_weights(l):
        m_down = {HALO: m_lo, HALO + OWN: m_hi}.get(l, 1.0)
        m_up = {HALO - 1: m_lo, HALO + OWN - 1: m_hi}.get(l, 1.0)
        k_alt = eka[l]
        lo = 0.5 * (k_alt + m_down * eka[l - 1])
        hi = 0.5 * (k_alt + m_up * eka[l + 1])
        k_inc = eki[l]
        w_inc = jnp.where(row0, 0.0, 0.5 * (k_inc + row_roll(k_inc, 1)))
        k_raan = ekr[l]
        w_raan = 0.5 * (k_raan + lane_roll(k_raan, 1))
        dg = 1.0 + (lo + hi + w_inc + row_roll(w_inc, -1) + w_raan + lane_roll(w_raan, -1))
        wa[l - 1] = m_down * lo
        wa[l] = m_up * hi
        wi[l] = w_inc
        wr[l] = w_raan
        diag[l] = dg
        invd[l] = OMEGA / dg

    def target_fine(src, l):
        return ef[l] + beside_fine(src[l], src[l - 1], src[l + 1], wa[l - 1], wa[l], wi[l], wr[l])

    def sweep_fine(src, dst, l):
        dst[l] = 0.25 * src[l] + invd[l] * target_fine(src, l)

    def layers(lo, hi, *bodies):
        for l in range(lo, hi):
            for one in bodies:
                one(l)

    first_sweep = functools.partial(sweep_fine, ef, v1)
    layers(3, 5, fine_weights, first_sweep)
    swept = exchange([(v1.at[4], v1.at[0])], [(v1.at[3], v1.at[7])])

    def edge_before(l, inner):
        face = wa[min(l, inner)]
        k_inc = eki[l]
        w_inc = jnp.where(row0, 0.0, 0.5 * (k_inc + row_roll(k_inc, 1)))
        k_raan = ekr[l]
        w_raan = 0.5 * (k_raan + lane_roll(k_raan, 1))
        wi[l] = w_inc
        wr[l] = w_raan
        diag[l] = 1.0 + (face + w_inc + row_roll(w_inc, -1) + w_raan + lane_roll(w_raan, -1))
        v = ef[l]
        total = v + face * ef[inner] + w_inc * row_roll(v, 1) + row_roll(w_inc * v, -1)
        v1[l] = total + w_raan * lane_roll(v, 1) + lane_roll(w_raan * v, -1)

    def edge_after(l, outer, m):
        face = 0.5 * (eka[l] + m * eka[outer])
        dg = diag[l] + face
        inv = OMEGA / dg
        wa[min(l, outer)] = m * face
        diag[l] = dg
        invd[l] = inv
        v1[l] = 0.25 * ef[l] + inv * (v1[l] + (m * face) * ef[outer])

    edge_before(2, 3)
    edge_before(5, 4)

    even2 = iota((16, WIDE), 1) % 2 == 0

    slot_of = [0]

    def fresh(scratch):
        slot_of[0] += 1
        return scratch.at[slot_of[0] % scratch.shape[0]]

    def row_pairs(slots, x):
        scratch = fresh(slots)
        n = x.shape[0] // 2
        for t in range(TILES):
            scratch[t] = x[:, 128 * t:128 * t + 128]
        return jnp.concatenate(
            [scratch[t, pl.ds(0, n, stride=2)] + scratch[t, pl.ds(1, n, stride=2)] for t in range(TILES)], axis=1)

    def twice(slots, x):
        scratch = fresh(slots)
        n = x.shape[0]
        for t in range(TILES):
            part = x[:, 128 * t:128 * t + 128]
            scratch[t, pl.ds(0, n, stride=2)] = part
            scratch[t, pl.ds(1, n, stride=2)] = part
        return jnp.concatenate([scratch[t] for t in range(TILES)], axis=1)

    def coarsen_fine(total):
        pairs = row_pairs(tmp, total)
        t_a, t_b = pairs[0:16], pairs[16:32]
        return 0.125 * (jnp.where(even2, t_a, t_b) + jnp.where(even2, lane_roll(t_a, -1), lane_roll(t_b, 1)))

    low3 = iota((8, WIDE), 1) % 4 < 2

    def coarsen_mid(total):
        t = row_pairs(tmp2, total)
        return 0.125 * (t + jnp.where(low3, lane_roll(t, -2), lane_roll(t, 2)))

    def fold(x):
        return jnp.where(low3, x, row_roll(x, 4))[0:4]

    upper3 = iota((8, WIDE), 0) < 4

    def unfold(part):
        both = jnp.concatenate([part, part], axis=0)
        return jnp.where(upper3, jnp.where(low3, both, lane_roll(both, 2)), jnp.where(low3, lane_roll(both, -2), both))

    for j in range(2):
        k2a[2 + j] = coarsen_fine(eka[2 + 2 * j] + eka[3 + 2 * j])
        k2b[2 + j, 0] = coarsen_fine(eki[2 + 2 * j] + eki[3 + 2 * j])
        k2b[2 + j, 1] = coarsen_fine(ekr[2 + 2 * j] + ekr[3 + 2 * j])
    k3[FAR, 0] = coarsen_mid(k2a[2] + k2a[3])
    k3[FAR, 1] = coarsen_mid(k2b[2, 0] + k2b[3, 0])
    k3[FAR, 2] = coarsen_mid(k2b[2, 1] + k2b[3, 1])
    coarse_alt = exchange([(k2a.at[3], k2a.at[1])], [(k2a.at[2], k2a.at[4])])
    coarse = exchange([(k2a.at[2], k2a.at[0]), (k2b.at[3], k2b.at[1])],
                      [(k2a.at[3], k2a.at[5]), (k2b.at[2], k2b.at[4])])
    for n in range(3):
        sk[n] = fold(k3[FAR, n])
    far_k = []

    def send_far_k(d):
        part = slice(0, 3) if d < FAR else slice(0, 1)
        far_k.append(exchange([(sk.at[part], lk.at[FAR - d, part])], [(sk.at[part], lk.at[FAR + d, part])], d))

    send_far_k(1)
    hear(1)
    greet(near.at[2, 0], near.at[2, 1])

    bulk.wait_recv()
    for i, slots in ((0, (0, 1)), (1, (2, 3)), (2, (4,)), (3, (5,))):
        relay[i].wait_recv()
        for n, slot in enumerate(slots):
            unpack(xb[0, slot, 0], xb[0, slot, 1], ext[i], n if len(slots) == 2 else 1)
            unpack(xb[1, slot, 0], xb[1, slot, 1], ext[i], 6 + n)
        if i == 1:
            edge_after(2, 1, m_lo)
            edge_after(5, 6, m_hi)
    for l in (1, 6):
        fine_weights(l)
        first_sweep(l)

    def weights_mid(x):
        m_down = {2: m_lo, 4: m_hi}.get(x, 1.0)
        m_up = {1: m_lo, 3: m_hi}.get(x, 1.0)
        w_down, w_up, w_inc, w_raan, dg = coarse_weights(
            k2a[x], k2a[x - 1], k2a[x + 1], m_down, m_up, k2b[x, 0], k2b[x, 1], 0.25, 2)
        for n, value in enumerate((w_down, w_up, w_inc, w_raan, dg, OMEGA / dg)):
            w2[x, n] = value

    second_sweep = functools.partial(sweep_fine, v1, v2)
    layers(2, 6, second_sweep)

    def residual_fine(l):
        return target_fine(v2, l) - diag[l] * v2[l]

    for l in (3, 4):
        p2[l] = residual_fine(l)
    swept.wait_recv()
    second_sweep(1)
    second_sweep(6)
    coarse_alt.wait_recv()
    weights_mid(2)
    weights_mid(3)
    for j in range(2):
        rhs2[2 + j] = coarsen_fine(p2[3 + j] + residual_fine(2 + 3 * j))
        c2a[2 + j] = rhs2[2 + j] * w2[2 + j, 5]
    sb4[0, 0] = rhs2[3]
    sb4[0, 1] = c2a[2]
    sb4[1, 0] = rhs2[2]
    sb4[1, 1] = c2a[3]
    mid = exchange([(sb4.at[0], rb4.at[0])], [(sb4.at[1], rb4.at[1])])

    send_far_k(2)
    send_far_k(3)
    hear(2)
    send_far_k(4)
    coarse.wait_recv()
    weights_mid(1)
    weights_mid(4)

    def weights_far(x):
        at = a + x - FAR
        m_down = jnp.where(at == 0, 0.0, 1.0).astype(jnp.float32)
        m_up = jnp.where(at == n_alt - 1, 0.0, 1.0).astype(jnp.float32)
        w_down, w_up, w_inc, w_raan, dg = coarse_weights(
            k3[x, 0], k3[x - 1, 0], k3[x + 1, 0], m_down, m_up, k3[x, 1], k3[x, 2], 0.0625, 4)
        for n, value in enumerate((w_down, w_up, w_inc, w_raan, OMEGA / dg)):
            w3[x, n] = value

    def take_far(x):
        for n in range(1 if x in (0, 2 * FAR) else 3):
            k3[x, n] = unfold(lk[x, n])

    far_k[0].wait_recv()
    take_far(FAR - 1)
    take_far(FAR + 1)
    weights_far(FAR)

    mid.wait_recv()
    rhs2[1] = rb4[0, 0]
    rhs2[4] = rb4[1, 0]

    def target_mid(values, x):
        return rhs2[x] + beside_coarse(
            values[x], values[x - 1], values[x + 1], w2[x, 0], w2[x, 1], w2[x, 2], w2[x, 3], 2)

    def sweep_mid(values, x):
        return 0.25 * values[x] + w2[x, 5] * target_mid(values, x)

    before = [rb4[0, 1], rb4[0, 0] * w2[1, 5], c2a[2], c2a[3], rb4[1, 0] * w2[4, 5], rb4[1, 1]]
    before[1:5] = [sweep_mid(before, x) for x in range(1, 5)]
    residual = [target_mid(before, x) - w2[x, 4] * before[x] for x in (2, 3)]
    r3[FAR] = coarsen_mid(residual[0] + residual[1])
    sr[0] = fold(r3[FAR])
    first3 = r3[FAR] * w3[FAR, 4]
    sr[1] = fold(first3)
    far = []
    for d in range(FAR, 0, -1):
        part = sr.at[0 if d < FAR else 1]
        far.append(exchange([(part, lr.at[FAR - d])], [(part, lr.at[FAR + d])], d))
    for x in range(1, 5):
        c2b[x] = before[x]
    ends = exchange([(c2b.at[2], c2b.at[0])], [(c2b.at[3], c2b.at[5])])
    dens2 = exchange([(v2.at[4], v2.at[0])], [(v2.at[3], v2.at[7])])

    for copy in far_k[1:]:
        copy.wait_recv()
    for x in range(2 * FAR + 1):
        if abs(x - FAR) > 1:
            take_far(x)
    for x in range(1, 2 * FAR):
        if x != FAR:
            weights_far(x)
    for copy in far:
        copy.wait_recv()
    for x in range(2 * FAR + 1):
        if x != FAR:
            r3[x] = unfold(lr[x])
    v3 = [r3[x] if x in (0, 2 * FAR) else r3[x] * w3[x, 4] for x in range(2 * FAR + 1)]
    for n in range(3):
        old = list(v3)
        for x in range(1 + n, 2 * FAR - n):
            total = r3[x] + beside_coarse(old[x], old[x - 1], old[x + 1], w3[x, 0], w3[x, 1], w3[x, 2], w3[x, 3], 4)
            v3[x] = 0.25 * old[x] + w3[x, 4] * total

    ends.wait_recv()
    after = [None] * 6
    for j in range(3):
        part = twice(tmp2, v3[FAR - 1 + j])
        for x in (2 * j, 2 * j + 1):
            after[x] = c2b[x] + part
    after[1:5] = [sweep_mid(after, x) for x in range(1, 5)]
    for x in (2, 3):
        q2[x] = sweep_mid(after, x)
    up2 = exchange([(q2.at[3], q2.at[1])], [(q2.at[2], q2.at[4])])

    def refine_mid(x):
        c = q2[x]
        part_a = jnp.where(even2, c, lane_roll(c, 1))
        part_b = jnp.where(even2, lane_roll(c, -1), c)
        rf[x] = twice(tmp, jnp.concatenate([part_a, part_b], axis=0))

    def correct(x):
        refine_mid(x)
        for l in (2 * x - 2, 2 * x - 1):
            p0[l] = v2[l] + rf[x]

    correct(2)
    correct(3)
    last_sweep = functools.partial(sweep_fine, p0, p1)
    layers(3, 5, last_sweep)
    inner = exchange([(p1.at[4, :, cols], p1.at[0, :, cols])], [(p1.at[3, :, cols], p1.at[7, :, cols])])
    dens2.wait_recv()
    up2.wait_recv()
    correct(1)
    correct(4)
    layers(1, 3, last_sweep)
    layers(5, 7, last_sweep)
    def final_sweep(l):
        sweep_fine(p1, p2, l)
        dens[l - HALO] = p2[l, :, cols]

    def last_residual(l):
        value = (1.0 / OMEGA) * (invd[l] * target_fine(p2, l)) - p2[l]
        sres[l - HALO] = value[:, 0:COLS]

    layers(2, 6, final_sweep)
    layers(3, 5, last_residual)
    inner.wait_recv()
    sweep_fine(p1, p2, 1)
    sweep_fine(p1, p2, 6)
    last_residual(2)
    last_residual(5)
    for copy in sends:
        copy.wait_send()


def solution(mesh):
    n_alt, n_raan = mesh.shape["alt"], mesh.shape["raan"]
    spec = P("alt", None, "raan")

    def vmem(*shape):
        return pltpu.VMEM(shape, jnp.float32)

    def shards(source, k_alt, k_inc, k_raan):
        scratch = [vmem(LAYERS, INC, WIDE)] * 14
        scratch += [vmem(4, OWN, 2, 16, 128), vmem(4, OWN, 2, 16, 128), vmem(2, 6, 2, 16, 128),
                    vmem(4, TILES, INC, 128), vmem(4, TILES, 16, 128)]
        scratch += [vmem(6, 16, WIDE), vmem(6, 2, 16, WIDE), vmem(6, 6, 16, WIDE), vmem(2, 2, 16, WIDE),
                    vmem(2, 2, 16, WIDE)] + [vmem(6, 16, WIDE)] * 4 + [vmem(6, INC, WIDE)]
        scratch += [vmem(2 * FAR + 1, 3, 8, WIDE), vmem(2 * FAR + 1, 5, 8, WIDE), vmem(2 * FAR + 1, 8, WIDE),
                    vmem(3, 4, WIDE), vmem(2 * FAR + 1, 3, 4, WIDE),
                    vmem(2, 4, WIDE), vmem(2 * FAR + 1, 4, WIDE)]
        scratch += [pltpu.SemaphoreType.DMA((4,)),
                    pltpu.SemaphoreType.DMA((64,)), pltpu.SemaphoreType.DMA((64,)),
                    pltpu.SemaphoreType.REGULAR((3, 2))]
        shape = pltpu.VMEM(source.shape, source.dtype)
        return pl.pallas_call(
            functools.partial(kernel, n_alt, n_raan),
            out_shape=(shape, shape),
            in_specs=[pl.BlockSpec(memory_space=pltpu.HBM)] * 4,
            out_specs=(pl.BlockSpec(memory_space=pltpu.VMEM),) * 2,
            scratch_shapes=scratch,
            compiler_params=pltpu.CompilerParams(
                collective_id=0, has_side_effects=True, vmem_limit_bytes=60 * 1024 * 1024),
            name="vcycle",
        )(source, k_alt, k_inc, k_raan)

    return jax.shard_map(shards, mesh=mesh, in_specs=(spec,) * 4, out_specs=(spec, spec), check_vma=False)
```

```python
import functools

import jax
import jax.numpy as jnp
from jax import lax
from jax.experimental import pallas as pl
from jax.experimental.pallas import tpu as pltpu
from jax.sharding import PartitionSpec as P

OMEGA = 0.75
MESH = pl.DeviceIdType.MESH

INC = 64
COLS = 256
WIDE = 384
HALO = 2
OWN = 4
TILES = WIDE // 128
LAYERS = OWN + 2 * HALO
FAR = 4


def lane_roll(x, shift):
    return pltpu.roll(x, shift % x.shape[-1], axis=x.ndim - 1)


def row_roll(x, shift):
    return pltpu.roll(x, shift % x.shape[-2], axis=x.ndim - 2)


def iota(shape, dim):
    return lax.broadcasted_iota(jnp.int32, shape, dim)


def beside_fine(v, down, up, w_down, w_up, w_inc, w_raan):
    total = w_down * down + w_up * up
    total = total + w_inc * row_roll(v, 1) + row_roll(w_inc * v, -1)
    return total + w_raan * lane_roll(v, 1) + lane_roll(w_raan * v, -1)


def prev_row(v):
    turned = row_roll(v, 1)
    top = turned[0:8]
    top = jnp.where(iota(top.shape, 0) == 0, lane_roll(top, 1), top)
    return top if v.shape[0] == 8 else jnp.concatenate([top, turned[8:]], axis=0)


def next_row(v):
    turned = row_roll(v, -1)
    end = turned[-8:]
    end = jnp.where(iota(end.shape, 0) == 7, lane_roll(end, -1), end)
    return end if v.shape[0] == 8 else jnp.concatenate([turned[:-8], end], axis=0)


def coarse_weights(k_alt, k_down, k_up, m_down, m_up, k_inc, k_raan, factor, step):
    half = 0.5 * factor
    lo = half * (k_alt + m_down * k_down)
    hi = half * (k_alt + m_up * k_up)
    outer = (iota(k_inc.shape, 0) == 0) & (iota(k_inc.shape, 1) % 2 == 0)
    w_inc = jnp.where(outer, 0.0, half * (k_inc + prev_row(k_inc)))
    w_raan = half * (k_raan + lane_roll(k_raan, step))
    diagonal = 1.0 + (lo + hi + w_inc + next_row(w_inc) + w_raan + lane_roll(w_raan, -step))
    return m_down * lo, m_up * hi, w_inc, w_raan, diagonal


def beside_coarse(v, down, up, w_down, w_up, w_inc, w_raan, step):
    total = w_down * down + w_up * up
    total = total + w_inc * prev_row(v) + next_row(w_inc * v)
    return total + w_raan * lane_roll(v, step) + lane_roll(w_raan * v, -step)


class Exchange:
    def __init__(self, ups, downs, distance, has_up, has_down):
        self.ups, self.downs = ups, downs
        self.has_up, self.has_down = has_up(distance), has_down(distance)

    def start(self):
        @pl.when(self.has_up)
        def _():
            for copy in self.ups:
                copy.start()

        @pl.when(self.has_down)
        def _():
            for copy in self.downs:
                copy.start()

    def wait_recv(self):
        @pl.when(self.has_down)
        def _():
            for copy in self.ups:
                copy.wait_recv()

        @pl.when(self.has_up)
        def _():
            for copy in self.downs:
                copy.wait_recv()

    def wait_send(self):
        @pl.when(self.has_up)
        def _():
            for copy in self.ups:
                copy.wait_send()

        @pl.when(self.has_down)
        def _():
            for copy in self.downs:
                copy.wait_send()


def kernel(n_alt, n_raan, f_hbm, ka_hbm, ki_hbm, kr_hbm, result,
           ef, eka, eki, ekr, v1, v2, p0, p1, p2, wa, wi, wr, invd, diag,
           pack, rb, xb, tmp, tmp2,
           k2a, k2b, w2, sb4, rb4, rhs2, c2a, c2b, q2, rf,
           k3, w3, r3, sk, lk, sr, lr,
           load_sem, send_sem, recv_sem, near):
    a = lax.axis_index("alt")
    r = lax.axis_index("raan")
    m_lo = jnp.where(a == 0, 0.0, 1.0).astype(jnp.float32)
    m_hi = jnp.where(a == n_alt - 1, 0.0, 1.0).astype(jnp.float32)

    def has_up(d):
        return a < n_alt - d

    def has_down(d):
        return a >= d

    def alt_dev(d):
        return (lax.rem(a + d + n_alt, n_alt), r)

    def raan_dev(d):
        return (a, lax.rem(r + d + n_raan, n_raan))

    count = [0]
    sends = []

    def describe(src, dst, device):
        k = count[0]
        count[0] += 1
        return pltpu.make_async_remote_copy(
            src_ref=src, dst_ref=dst, send_sem=send_sem.at[k], recv_sem=recv_sem.at[k],
            device_id=device, device_id_type=MESH)

    def remote(src, dst, device):
        copy = describe(src, dst, device)
        copy.start()
        sends.append(copy)
        return copy

    def exchange(ups, downs, distance=1):
        copy = Exchange([describe(s, d, alt_dev(distance)) for s, d in ups],
                        [describe(s, d, alt_dev(-distance)) for s, d in downs], distance, has_up, has_down)
        copy.start()
        sends.append(copy)
        return copy

    hbm = (f_hbm, ka_hbm, ki_hbm, kr_hbm)
    ext = (ef, eka, eki, ekr)
    cols = slice(0, COLS)
    own = slice(HALO, HALO + OWN)
    loads = []
    for i in range(4):
        loads.append(pltpu.make_async_copy(hbm[i], ext[i].at[own, :, cols], load_sem.at[i]))

    barrier = pltpu.get_barrier_semaphore()

    def greet(sem_up, sem_down):
        @pl.when(has_up(1))
        def _():
            pl.semaphore_signal(sem_up, inc=1, device_id=alt_dev(1), device_id_type=MESH)

        @pl.when(has_down(1))
        def _():
            pl.semaphore_signal(sem_down, inc=1, device_id=alt_dev(-1), device_id_type=MESH)

    greet(barrier, barrier)
    for side in (1, -1):
        pl.semaphore_signal(barrier, inc=1, device_id=raan_dev(side), device_id_type=MESH)
    for i in range(4):
        loads[i].start()

    @pl.when(a == 0)
    def _():
        for ref in (ef, eka, eki, ekr, v1, v2, p1):
            ref[0:HALO] = jnp.zeros((HALO, INC, WIDE), jnp.float32)
        xb[0] = jnp.zeros(xb.shape[1:], jnp.float32)
        rb4[0] = jnp.zeros(rb4.shape[1:], jnp.float32)
        for ref in (k2a, k2b, c2b, q2):
            ref[0:2] = jnp.zeros((2,) + ref.shape[1:], jnp.float32)

    @pl.when(a == n_alt - 1)
    def _():
        for ref in (ef, eka, eki, ekr, v1, v2, p1):
            ref[HALO + OWN:LAYERS] = jnp.zeros((HALO, INC, WIDE), jnp.float32)
        xb[1] = jnp.zeros(xb.shape[1:], jnp.float32)
        rb4[1] = jnp.zeros(rb4.shape[1:], jnp.float32)
        for ref in (k2a, k2b, c2b, q2):
            ref[4:6] = jnp.zeros((2,) + ref.shape[1:], jnp.float32)

    for d in range(1, FAR + 1):
        for side, here in ((d, has_up(d)), (-d, has_down(d))):
            @pl.when(jnp.logical_not(here))
            def _():
                lk[FAR + side] = jnp.zeros((3, 4, WIDE), jnp.float32)
                lr[FAR + side] = jnp.zeros((4, WIDE), jnp.float32)

    quarter = iota((16, 128), 1) // 32
    for i in range(4):
        loads[i].wait()
        for l in range(OWN):
            low = ext[i][HALO + l, :, 0:128]
            high = ext[i][HALO + l, :, 128:256]
            first = low[0:16]
            last = high[0:16]
            for g in range(1, 4):
                first = jnp.where(quarter == g, lane_roll(low[16 * g:16 * g + 16], 32 * g), first)
                last = jnp.where(quarter == (3 + g) % 4, lane_roll(high[16 * g:16 * g + 16], 32 * g), last)
            pack[i, l, 0] = first
            pack[i, l, 1] = last

    pl.semaphore_wait(barrier, 2 + has_up(1).astype(jnp.int32) + has_down(1).astype(jnp.int32))

    def hear(step):
        @pl.when(has_down(1))
        def _():
            pl.semaphore_wait(near.at[step, 0], 1)

        @pl.when(has_up(1))
        def _():
            pl.semaphore_wait(near.at[step, 1], 1)

    greet(near.at[0, 0], near.at[0, 1])

    ring = []
    for i in range(4):
        ring.append((remote(pack.at[i, :, 0], rb.at[i, :, 0], raan_dev(-1)),
                     remote(pack.at[i, :, 1], rb.at[i, :, 1], raan_dev(1))))

    low2, high2, low1, high1 = slice(0, 2), slice(2, 4), slice(0, 1), slice(3, 4)
    below2, above2, below1, above1 = slice(0, 2), slice(6, 8), slice(1, 2), slice(6, 7)
    bulk = exchange(
        [(hbm[i].at[high2 if i < 2 else high1], ext[i].at[below2 if i < 2 else below1, :, cols]) for i in range(4)],
        [(hbm[i].at[low2 if i < 2 else low1], ext[i].at[above2 if i < 2 else above1, :, cols]) for i in range(4)])

    def unpack(first, last, dst, layer):
        for g in range(4):
            both = jnp.where(quarter == g, first, last)
            dst[layer, 16 * g:16 * g + 16, COLS:WIDE] = lane_roll(both, -32 * g) if g else both

    relay = []
    x_slot = (slice(0, 2), slice(2, 4), slice(4, 5), slice(5, 6))
    for i in range(4):
        for copy in ring[i]:
            copy.wait_recv()
        relay.append(exchange([(rb.at[i, high2 if i < 2 else high1], xb.at[0, x_slot[i]])],
                              [(rb.at[i, low2 if i < 2 else low1], xb.at[1, x_slot[i]])]))
        if i == 1:
            hear(0)
            greet(near.at[1, 0], near.at[1, 1])
        for l in range(OWN) if i < 2 else (1, 2):
            unpack(rb[i, l, 0], rb[i, l, 1], ext[i], HALO + l)

    row0 = iota((INC, WIDE), 0) == 0

    def fine_weights(l):
        m_down = {HALO: m_lo, HALO + OWN: m_hi}.get(l, 1.0)
        m_up = {HALO - 1: m_lo, HALO + OWN - 1: m_hi}.get(l, 1.0)
        k_alt = eka[l]
        lo = 0.5 * (k_alt + m_down * eka[l - 1])
        hi = 0.5 * (k_alt + m_up * eka[l + 1])
        k_inc = eki[l]
        w_inc = jnp.where(row0, 0.0, 0.5 * (k_inc + row_roll(k_inc, 1)))
        k_raan = ekr[l]
        w_raan = 0.5 * (k_raan + lane_roll(k_raan, 1))
        dg = 1.0 + (lo + hi + w_inc + row_roll(w_inc, -1) + w_raan + lane_roll(w_raan, -1))
        wa[l - 1] = m_down * lo
        wa[l] = m_up * hi
        wi[l] = w_inc
        wr[l] = w_raan
        diag[l] = dg
        invd[l] = OMEGA / dg

    def target_fine(src, l):
        return ef[l] + beside_fine(src[l], src[l - 1], src[l + 1], wa[l - 1], wa[l], wi[l], wr[l])

    def sweep_fine(src, dst, l):
        dst[l] = 0.25 * src[l] + invd[l] * target_fine(src, l)

    def layers(lo, hi, *bodies):
        for l in range(lo, hi):
            for one in bodies:
                one(l)

    first_sweep = functools.partial(sweep_fine, ef, v1)
    layers(3, 5, fine_weights, first_sweep)
    swept = exchange([(v1.at[4], v1.at[0])], [(v1.at[3], v1.at[7])])

    def edge_before(l, inner):
        face = wa[min(l, inner)]
        k_inc = eki[l]
        w_inc = jnp.where(row0, 0.0, 0.5 * (k_inc + row_roll(k_inc, 1)))
        k_raan = ekr[l]
        w_raan = 0.5 * (k_raan + lane_roll(k_raan, 1))
        wi[l] = w_inc
        wr[l] = w_raan
        diag[l] = 1.0 + (face + w_inc + row_roll(w_inc, -1) + w_raan + lane_roll(w_raan, -1))
        v = ef[l]
        total = v + face * ef[inner] + w_inc * row_roll(v, 1) + row_roll(w_inc * v, -1)
        v1[l] = total + w_raan * lane_roll(v, 1) + lane_roll(w_raan * v, -1)

    def edge_after(l, outer, m):
        face = 0.5 * (eka[l] + m * eka[outer])
        dg = diag[l] + face
        inv = OMEGA / dg
        wa[min(l, outer)] = m * face
        diag[l] = dg
        invd[l] = inv
        v1[l] = 0.25 * ef[l] + inv * (v1[l] + (m * face) * ef[outer])

    for i in (2, 3):
        for l in (0, 3):
            unpack(rb[i, l, 0], rb[i, l, 1], ext[i], HALO + l)
    edge_before(2, 3)
    edge_before(5, 4)

    even2 = iota((16, WIDE), 1) % 2 == 0

    slot_of = [0]

    def fresh(scratch):
        slot_of[0] += 1
        return scratch.at[slot_of[0] % scratch.shape[0]]

    def row_pairs(slots, x):
        scratch = fresh(slots)
        n = x.shape[0] // 2
        for t in range(TILES):
            scratch[t] = x[:, 128 * t:128 * t + 128]
        return jnp.concatenate(
            [scratch[t, pl.ds(0, n, stride=2)] + scratch[t, pl.ds(1, n, stride=2)] for t in range(TILES)], axis=1)

    def twice(slots, x):
        scratch = fresh(slots)
        n = x.shape[0]
        for t in range(TILES):
            part = x[:, 128 * t:128 * t + 128]
            scratch[t, pl.ds(0, n, stride=2)] = part
            scratch[t, pl.ds(1, n, stride=2)] = part
        return jnp.concatenate([scratch[t] for t in range(TILES)], axis=1)

    def coarsen_fine(total):
        pairs = row_pairs(tmp, total)
        t_a, t_b = pairs[0:16], pairs[16:32]
        return 0.125 * (jnp.where(even2, t_a, t_b) + jnp.where(even2, lane_roll(t_a, -1), lane_roll(t_b, 1)))

    low3 = iota((8, WIDE), 1) % 4 < 2

    def coarsen_mid(total):
        t = row_pairs(tmp2, total)
        return 0.125 * (t + jnp.where(low3, lane_roll(t, -2), lane_roll(t, 2)))

    def fold(x):
        return jnp.where(low3, x, row_roll(x, 4))[0:4]

    upper3 = iota((8, WIDE), 0) < 4

    def unfold(part):
        both = jnp.concatenate([part, part], axis=0)
        return jnp.where(upper3, jnp.where(low3, both, lane_roll(both, 2)), jnp.where(low3, lane_roll(both, -2), both))

    for j in range(2):
        k2a[2 + j] = coarsen_fine(eka[2 + 2 * j] + eka[3 + 2 * j])
        k2b[2 + j, 0] = coarsen_fine(eki[2 + 2 * j] + eki[3 + 2 * j])
        k2b[2 + j, 1] = coarsen_fine(ekr[2 + 2 * j] + ekr[3 + 2 * j])
    k3[FAR, 0] = coarsen_mid(k2a[2] + k2a[3])
    k3[FAR, 1] = coarsen_mid(k2b[2, 0] + k2b[3, 0])
    k3[FAR, 2] = coarsen_mid(k2b[2, 1] + k2b[3, 1])
    coarse_alt = exchange([(k2a.at[3], k2a.at[1])], [(k2a.at[2], k2a.at[4])])
    coarse = exchange([(k2a.at[2], k2a.at[0]), (k2b.at[3], k2b.at[1])],
                      [(k2a.at[3], k2a.at[5]), (k2b.at[2], k2b.at[4])])
    for n in range(3):
        sk[n] = fold(k3[FAR, n])
    far_k = []

    def send_far_k(d):
        part = slice(0, 3) if d < FAR else slice(0, 1)
        far_k.append(exchange([(sk.at[part], lk.at[FAR - d, part])], [(sk.at[part], lk.at[FAR + d, part])], d))

    send_far_k(1)
    hear(1)
    greet(near.at[2, 0], near.at[2, 1])

    bulk.wait_recv()
    for i, slots in ((0, (0, 1)), (1, (2, 3)), (2, (4,)), (3, (5,))):
        relay[i].wait_recv()
        for n, slot in enumerate(slots):
            unpack(xb[0, slot, 0], xb[0, slot, 1], ext[i], n if len(slots) == 2 else 1)
            unpack(xb[1, slot, 0], xb[1, slot, 1], ext[i], 6 + n)
        if i == 1:
            edge_after(2, 1, m_lo)
            edge_after(5, 6, m_hi)
    for l in (1, 6):
        fine_weights(l)
        first_sweep(l)

    def weights_mid(x):
        m_down = {2: m_lo, 4: m_hi}.get(x, 1.0)
        m_up = {1: m_lo, 3: m_hi}.get(x, 1.0)
        w_down, w_up, w_inc, w_raan, dg = coarse_weights(
            k2a[x], k2a[x - 1], k2a[x + 1], m_down, m_up, k2b[x, 0], k2b[x, 1], 0.25, 2)
        for n, value in enumerate((w_down, w_up, w_inc, w_raan, dg, OMEGA / dg)):
            w2[x, n] = value

    second_sweep = functools.partial(sweep_fine, v1, v2)
    layers(2, 6, second_sweep)

    def residual_fine(l):
        return target_fine(v2, l) - diag[l] * v2[l]

    for l in (3, 4):
        p2[l] = residual_fine(l)
    swept.wait_recv()
    second_sweep(1)
    second_sweep(6)
    coarse_alt.wait_recv()
    weights_mid(2)
    weights_mid(3)
    for j in range(2):
        rhs2[2 + j] = coarsen_fine(p2[3 + j] + residual_fine(2 + 3 * j))
        c2a[2 + j] = rhs2[2 + j] * w2[2 + j, 5]
    sb4[0, 0] = rhs2[3]
    sb4[0, 1] = c2a[2]
    sb4[1, 0] = rhs2[2]
    sb4[1, 1] = c2a[3]
    mid = exchange([(sb4.at[0], rb4.at[0])], [(sb4.at[1], rb4.at[1])])

    send_far_k(2)
    send_far_k(3)
    hear(2)
    send_far_k(4)
    coarse.wait_recv()
    weights_mid(1)
    weights_mid(4)

    def weights_far(x):
        at = a + x - FAR
        m_down = jnp.where(at == 0, 0.0, 1.0).astype(jnp.float32)
        m_up = jnp.where(at == n_alt - 1, 0.0, 1.0).astype(jnp.float32)
        w_down, w_up, w_inc, w_raan, dg = coarse_weights(
            k3[x, 0], k3[x - 1, 0], k3[x + 1, 0], m_down, m_up, k3[x, 1], k3[x, 2], 0.0625, 4)
        for n, value in enumerate((w_down, w_up, w_inc, w_raan, OMEGA / dg)):
            w3[x, n] = value

    def take_far(x):
        for n in range(1 if x in (0, 2 * FAR) else 3):
            k3[x, n] = unfold(lk[x, n])

    far_k[0].wait_recv()
    take_far(FAR - 1)
    take_far(FAR + 1)
    weights_far(FAR)

    mid.wait_recv()
    rhs2[1] = rb4[0, 0]
    rhs2[4] = rb4[1, 0]

    def target_mid(values, x):
        return rhs2[x] + beside_coarse(
            values[x], values[x - 1], values[x + 1], w2[x, 0], w2[x, 1], w2[x, 2], w2[x, 3], 2)

    def sweep_mid(values, x):
        return 0.25 * values[x] + w2[x, 5] * target_mid(values, x)

    before = [rb4[0, 1], rb4[0, 0] * w2[1, 5], c2a[2], c2a[3], rb4[1, 0] * w2[4, 5], rb4[1, 1]]
    before[1:5] = [sweep_mid(before, x) for x in range(1, 5)]
    residual = [target_mid(before, x) - w2[x, 4] * before[x] for x in (2, 3)]
    r3[FAR] = coarsen_mid(residual[0] + residual[1])
    sr[0] = fold(r3[FAR])
    first3 = r3[FAR] * w3[FAR, 4]
    sr[1] = fold(first3)
    far = []
    for d in range(FAR, 0, -1):
        part = sr.at[0 if d < FAR else 1]
        far.append(exchange([(part, lr.at[FAR - d])], [(part, lr.at[FAR + d])], d))
    for x in range(1, 5):
        c2b[x] = before[x]
    ends = exchange([(c2b.at[2], c2b.at[0])], [(c2b.at[3], c2b.at[5])])
    dens2 = exchange([(v2.at[4], v2.at[0])], [(v2.at[3], v2.at[7])])

    for copy in far_k[1:]:
        copy.wait_recv()
    for x in range(2 * FAR + 1):
        if abs(x - FAR) > 1:
            take_far(x)
    for x in range(1, 2 * FAR):
        if x != FAR:
            weights_far(x)
    for copy in far:
        copy.wait_recv()
    for x in range(2 * FAR + 1):
        if x != FAR:
            r3[x] = unfold(lr[x])
    v3 = [r3[x] if x in (0, 2 * FAR) else r3[x] * w3[x, 4] for x in range(2 * FAR + 1)]
    for n in range(3):
        old = list(v3)
        for x in range(1 + n, 2 * FAR - n):
            total = r3[x] + beside_coarse(old[x], old[x - 1], old[x + 1], w3[x, 0], w3[x, 1], w3[x, 2], w3[x, 3], 4)
            v3[x] = 0.25 * old[x] + w3[x, 4] * total

    ends.wait_recv()
    after = [None] * 6
    for j in range(3):
        part = twice(tmp2, v3[FAR - 1 + j])
        for x in (2 * j, 2 * j + 1):
            after[x] = c2b[x] + part
    after[1:5] = [sweep_mid(after, x) for x in range(1, 5)]
    for x in (2, 3):
        q2[x] = sweep_mid(after, x)
    up2 = exchange([(q2.at[3], q2.at[1])], [(q2.at[2], q2.at[4])])

    def refine_mid(x):
        c = q2[x]
        part_a = jnp.where(even2, c, lane_roll(c, 1))
        part_b = jnp.where(even2, lane_roll(c, -1), c)
        rf[x] = twice(tmp, jnp.concatenate([part_a, part_b], axis=0))

    def correct(x):
        refine_mid(x)
        for l in (2 * x - 2, 2 * x - 1):
            p0[l] = v2[l] + rf[x]

    correct(2)
    correct(3)
    last_sweep = functools.partial(sweep_fine, p0, p1)
    layers(3, 5, last_sweep)
    inner = exchange([(p1.at[4, :, cols], p1.at[0, :, cols])], [(p1.at[3, :, cols], p1.at[7, :, cols])])
    dens2.wait_recv()
    up2.wait_recv()
    correct(1)
    correct(4)
    layers(1, 3, last_sweep)
    layers(5, 7, last_sweep)
    def final_sweep(l):
        sweep_fine(p1, p2, l)
        result[l - HALO] = p2[l, :, cols]

    def last_residual(l):
        value = (1.0 / OMEGA) * (invd[l] * target_fine(p2, l)) - p2[l]
        result[l - HALO + OWN] = value[:, 0:COLS]

    layers(2, 6, final_sweep)
    layers(3, 5, last_residual)
    inner.wait_recv()
    sweep_fine(p1, p2, 1)
    sweep_fine(p1, p2, 6)
    last_residual(2)
    last_residual(5)
    for copy in sends:
        copy.wait_send()


def solution(mesh):
    n_alt, n_raan = mesh.shape["alt"], mesh.shape["raan"]
    spec = P("alt", None, "raan")

    def vmem(*shape):
        return pltpu.VMEM(shape, jnp.float32)

    def shards(source, k_alt, k_inc, k_raan):
        scratch = [vmem(LAYERS, INC, WIDE)] * 14
        scratch += [vmem(4, OWN, 2, 16, 128), vmem(4, OWN, 2, 16, 128), vmem(2, 6, 2, 16, 128),
                    vmem(4, TILES, INC, 128), vmem(4, TILES, 16, 128)]
        scratch += [vmem(6, 16, WIDE), vmem(6, 2, 16, WIDE), vmem(6, 6, 16, WIDE), vmem(2, 2, 16, WIDE),
                    vmem(2, 2, 16, WIDE)] + [vmem(6, 16, WIDE)] * 4 + [vmem(6, INC, WIDE)]
        scratch += [vmem(2 * FAR + 1, 3, 8, WIDE), vmem(2 * FAR + 1, 5, 8, WIDE), vmem(2 * FAR + 1, 8, WIDE),
                    vmem(3, 4, WIDE), vmem(2 * FAR + 1, 3, 4, WIDE),
                    vmem(2, 4, WIDE), vmem(2 * FAR + 1, 4, WIDE)]
        scratch += [pltpu.SemaphoreType.DMA((4,)),
                    pltpu.SemaphoreType.DMA((64,)), pltpu.SemaphoreType.DMA((64,)),
                    pltpu.SemaphoreType.REGULAR((3, 2))]
        shape = pltpu.VMEM((2 * OWN, INC, COLS), source.dtype)
        result = pl.pallas_call(
            functools.partial(kernel, n_alt, n_raan),
            out_shape=shape,
            in_specs=[pl.BlockSpec(memory_space=pltpu.HBM)] * 4,
            out_specs=pl.BlockSpec(memory_space=pltpu.VMEM),
            scratch_shapes=scratch,
            compiler_params=pltpu.CompilerParams(
                collective_id=0, has_side_effects=True, vmem_limit_bytes=60 * 1024 * 1024),
            name="vcycle",
        )(source, k_alt, k_inc, k_raan)
        return result[:OWN], result[OWN:]

    return jax.shard_map(shards, mesh=mesh, in_specs=(spec,) * 4, out_specs=(spec, spec), check_vma=False)
```

```python
import functools

import jax
import jax.numpy as jnp
from jax import lax
from jax.experimental import pallas as pl
from jax.experimental.pallas import tpu as pltpu
from jax.sharding import PartitionSpec as P

OMEGA = 0.75
MESH = pl.DeviceIdType.MESH

INC = 64
COLS = 256
WIDE = 384
HALO = 2
OWN = 4
TILES = WIDE // 128
LAYERS = OWN + 2 * HALO
FAR = 4


def lane_roll(x, shift):
    return pltpu.roll(x, shift % x.shape[-1], axis=x.ndim - 1)


def row_roll(x, shift):
    return pltpu.roll(x, shift % x.shape[-2], axis=x.ndim - 2)


def iota(shape, dim):
    return lax.broadcasted_iota(jnp.int32, shape, dim)


def beside_fine(v, down, up, w_down, w_up, w_inc, w_raan):
    total = w_down * down + w_up * up
    total = total + w_inc * row_roll(v, 1) + row_roll(w_inc * v, -1)
    return total + w_raan * lane_roll(v, 1) + lane_roll(w_raan * v, -1)


def prev_row(v):
    turned = row_roll(v, 1)
    top = turned[0:8]
    top = jnp.where(iota(top.shape, 0) == 0, lane_roll(top, 1), top)
    return top if v.shape[0] == 8 else jnp.concatenate([top, turned[8:]], axis=0)


def next_row(v):
    turned = row_roll(v, -1)
    end = turned[-8:]
    end = jnp.where(iota(end.shape, 0) == 7, lane_roll(end, -1), end)
    return end if v.shape[0] == 8 else jnp.concatenate([turned[:-8], end], axis=0)


def coarse_weights(k_alt, k_down, k_up, m_down, m_up, k_inc, k_raan, factor, step):
    half = 0.5 * factor
    lo = half * (k_alt + m_down * k_down)
    hi = half * (k_alt + m_up * k_up)
    outer = (iota(k_inc.shape, 0) == 0) & (iota(k_inc.shape, 1) % 2 == 0)
    w_inc = jnp.where(outer, 0.0, half * (k_inc + prev_row(k_inc)))
    w_raan = half * (k_raan + lane_roll(k_raan, step))
    diagonal = 1.0 + (lo + hi + w_inc + next_row(w_inc) + w_raan + lane_roll(w_raan, -step))
    return m_down * lo, m_up * hi, w_inc, w_raan, diagonal


def beside_coarse(v, down, up, w_down, w_up, w_inc, w_raan, step):
    total = w_down * down + w_up * up
    total = total + w_inc * prev_row(v) + next_row(w_inc * v)
    return total + w_raan * lane_roll(v, step) + lane_roll(w_raan * v, -step)


class Exchange:
    def __init__(self, ups, downs, distance, has_up, has_down):
        self.ups, self.downs = ups, downs
        self.has_up, self.has_down = has_up(distance), has_down(distance)

    def start(self):
        @pl.when(self.has_up)
        def _():
            for copy in self.ups:
                copy.start()

        @pl.when(self.has_down)
        def _():
            for copy in self.downs:
                copy.start()

    def wait_recv(self):
        @pl.when(self.has_down)
        def _():
            for copy in self.ups:
                copy.wait_recv()

        @pl.when(self.has_up)
        def _():
            for copy in self.downs:
                copy.wait_recv()

    def wait_send(self):
        @pl.when(self.has_up)
        def _():
            for copy in self.ups:
                copy.wait_send()

        @pl.when(self.has_down)
        def _():
            for copy in self.downs:
                copy.wait_send()


def kernel(n_alt, n_raan, f_hbm, ka_hbm, ki_hbm, kr_hbm, result,
           ef, eka, eki, ekr, v1, v2, p0, p1, p2, wa, wi, wr, invd, diag,
           pack, rb, xb, vs, vr, tmp, tmp2,
           k2a, k2b, w2, sb4, rb4, rhs2, c2a, c2b, q2, rf,
           k3, w3, r3, sk, lk, sr, lr,
           load_sem, send_sem, recv_sem, near):
    a = lax.axis_index("alt")
    r = lax.axis_index("raan")
    m_lo = jnp.where(a == 0, 0.0, 1.0).astype(jnp.float32)
    m_hi = jnp.where(a == n_alt - 1, 0.0, 1.0).astype(jnp.float32)

    def has_up(d):
        return a < n_alt - d

    def has_down(d):
        return a >= d

    def alt_dev(d):
        return (lax.rem(a + d + n_alt, n_alt), r)

    def raan_dev(d):
        return (a, lax.rem(r + d + n_raan, n_raan))

    count = [0]
    sends = []

    def describe(src, dst, device):
        k = count[0]
        count[0] += 1
        return pltpu.make_async_remote_copy(
            src_ref=src, dst_ref=dst, send_sem=send_sem.at[k], recv_sem=recv_sem.at[k],
            device_id=device, device_id_type=MESH)

    def remote(src, dst, device):
        copy = describe(src, dst, device)
        copy.start()
        sends.append(copy)
        return copy

    def exchange(ups, downs, distance=1):
        copy = Exchange([describe(s, d, alt_dev(distance)) for s, d in ups],
                        [describe(s, d, alt_dev(-distance)) for s, d in downs], distance, has_up, has_down)
        copy.start()
        sends.append(copy)
        return copy

    hbm = (f_hbm, ka_hbm, ki_hbm, kr_hbm)
    ext = (ef, eka, eki, ekr)
    cols = slice(0, COLS)
    own = slice(HALO, HALO + OWN)
    loads = []
    for i in range(4):
        loads.append(pltpu.make_async_copy(hbm[i], ext[i].at[own, :, cols], load_sem.at[i]))

    barrier = pltpu.get_barrier_semaphore()

    def greet(sem_up, sem_down):
        @pl.when(has_up(1))
        def _():
            pl.semaphore_signal(sem_up, inc=1, device_id=alt_dev(1), device_id_type=MESH)

        @pl.when(has_down(1))
        def _():
            pl.semaphore_signal(sem_down, inc=1, device_id=alt_dev(-1), device_id_type=MESH)

    greet(barrier, barrier)
    for side in (1, -1):
        pl.semaphore_signal(barrier, inc=1, device_id=raan_dev(side), device_id_type=MESH)
    for i in range(4):
        loads[i].start()

    @pl.when(a == 0)
    def _():
        for ref in (ef, eka, eki, ekr, v1, v2, p1):
            ref[0:HALO] = jnp.zeros((HALO, INC, WIDE), jnp.float32)
        xb[0] = jnp.zeros(xb.shape[1:], jnp.float32)
        vr[0] = jnp.zeros(vr.shape[1:], jnp.float32)
        rb4[0] = jnp.zeros(rb4.shape[1:], jnp.float32)
        for ref in (k2a, k2b, c2b, q2):
            ref[0:2] = jnp.zeros((2,) + ref.shape[1:], jnp.float32)

    @pl.when(a == n_alt - 1)
    def _():
        for ref in (ef, eka, eki, ekr, v1, v2, p1):
            ref[HALO + OWN:LAYERS] = jnp.zeros((HALO, INC, WIDE), jnp.float32)
        xb[1] = jnp.zeros(xb.shape[1:], jnp.float32)
        vr[1] = jnp.zeros(vr.shape[1:], jnp.float32)
        rb4[1] = jnp.zeros(rb4.shape[1:], jnp.float32)
        for ref in (k2a, k2b, c2b, q2):
            ref[4:6] = jnp.zeros((2,) + ref.shape[1:], jnp.float32)

    for d in range(1, FAR + 1):
        for side, here in ((d, has_up(d)), (-d, has_down(d))):
            @pl.when(jnp.logical_not(here))
            def _():
                lk[FAR + side] = jnp.zeros((3, 4, WIDE), jnp.float32)
                lr[FAR + side] = jnp.zeros((4, WIDE), jnp.float32)

    quarter = iota((16, 128), 1) // 32
    for i in range(4):
        loads[i].wait()
        for l in range(OWN):
            low = ext[i][HALO + l, :, 0:128]
            high = ext[i][HALO + l, :, 128:256]
            first = low[0:16]
            last = high[0:16]
            for g in range(1, 4):
                first = jnp.where(quarter == g, lane_roll(low[16 * g:16 * g + 16], 32 * g), first)
                last = jnp.where(quarter == (3 + g) % 4, lane_roll(high[16 * g:16 * g + 16], 32 * g), last)
            pack[i, l, 0] = first
            pack[i, l, 1] = last

    pl.semaphore_wait(barrier, 2 + has_up(1).astype(jnp.int32) + has_down(1).astype(jnp.int32))

    def hear(step):
        @pl.when(has_down(1))
        def _():
            pl.semaphore_wait(near.at[step, 0], 1)

        @pl.when(has_up(1))
        def _():
            pl.semaphore_wait(near.at[step, 1], 1)

    greet(near.at[0, 0], near.at[0, 1])

    ring = []
    for i in range(4):
        ring.append((remote(pack.at[i, :, 0], rb.at[i, :, 0], raan_dev(-1)),
                     remote(pack.at[i, :, 1], rb.at[i, :, 1], raan_dev(1))))

    low2, high2, low1, high1 = slice(0, 2), slice(2, 4), slice(0, 1), slice(3, 4)
    below2, above2, below1, above1 = slice(0, 2), slice(6, 8), slice(1, 2), slice(6, 7)
    bulk = exchange(
        [(ext[i].at[slice(4, 6) if i < 2 else slice(5, 6), :, cols], ext[i].at[below2 if i < 2 else below1, :, cols])
         for i in range(4)],
        [(ext[i].at[slice(2, 4) if i < 2 else slice(2, 3), :, cols], ext[i].at[above2 if i < 2 else above1, :, cols])
         for i in range(4)])

    def unpack(first, last, dst, layer):
        for g in range(4):
            both = jnp.where(quarter == g, first, last)
            dst[layer, 16 * g:16 * g + 16, COLS:WIDE] = lane_roll(both, -32 * g) if g else both

    relay = []
    x_slot = (slice(0, 2), slice(2, 4), slice(4, 5), slice(5, 6))
    for i in range(4):
        for copy in ring[i]:
            copy.wait_recv()
        relay.append(exchange([(rb.at[i, high2 if i < 2 else high1], xb.at[0, x_slot[i]])],
                              [(rb.at[i, low2 if i < 2 else low1], xb.at[1, x_slot[i]])]))
        if i == 1:
            hear(0)
            greet(near.at[1, 0], near.at[1, 1])
        for l in range(OWN) if i < 2 else (1, 2):
            unpack(rb[i, l, 0], rb[i, l, 1], ext[i], HALO + l)

    row0 = iota((INC, WIDE), 0) == 0

    def fine_weights(l):
        m_down = {HALO: m_lo, HALO + OWN: m_hi}.get(l, 1.0)
        m_up = {HALO - 1: m_lo, HALO + OWN - 1: m_hi}.get(l, 1.0)
        k_alt = eka[l]
        lo = 0.5 * (k_alt + m_down * eka[l - 1])
        hi = 0.5 * (k_alt + m_up * eka[l + 1])
        k_inc = eki[l]
        w_inc = jnp.where(row0, 0.0, 0.5 * (k_inc + row_roll(k_inc, 1)))
        k_raan = ekr[l]
        w_raan = 0.5 * (k_raan + lane_roll(k_raan, 1))
        dg = 1.0 + (lo + hi + w_inc + row_roll(w_inc, -1) + w_raan + lane_roll(w_raan, -1))
        wa[l - 1] = m_down * lo
        wa[l] = m_up * hi
        wi[l] = w_inc
        wr[l] = w_raan
        diag[l] = dg
        invd[l] = OMEGA / dg

    def target_fine(src, l):
        return ef[l] + beside_fine(src[l], src[l - 1], src[l + 1], wa[l - 1], wa[l], wi[l], wr[l])

    def sweep_fine(src, dst, l):
        dst[l] = 0.25 * src[l] + invd[l] * target_fine(src, l)

    def layers(lo, hi, *bodies):
        for l in range(lo, hi):
            for one in bodies:
                one(l)

    first_sweep = functools.partial(sweep_fine, ef, v1)
    layers(3, 5, fine_weights, first_sweep)
    between = (iota((32, 128), 1) >= 32) & (iota((32, 128), 1) < 96)
    for n, l in enumerate((4, 3)):
        side = v1[l, :, COLS:WIDE]
        vs[n] = jnp.where(between, lane_roll(side[32:64], 64), side[0:32])
    swept = exchange([(v1.at[4, :, cols], v1.at[0, :, cols]), (vs.at[0], vr.at[0])],
                     [(v1.at[3, :, cols], v1.at[7, :, cols]), (vs.at[1], vr.at[1])])

    def edge_before(l, inner):
        face = wa[min(l, inner)]
        k_inc = eki[l]
        w_inc = jnp.where(row0, 0.0, 0.5 * (k_inc + row_roll(k_inc, 1)))
        k_raan = ekr[l]
        w_raan = 0.5 * (k_raan + lane_roll(k_raan, 1))
        wi[l] = w_inc
        wr[l] = w_raan
        diag[l] = 1.0 + (face + w_inc + row_roll(w_inc, -1) + w_raan + lane_roll(w_raan, -1))
        v = ef[l]
        total = v + face * ef[inner] + w_inc * row_roll(v, 1) + row_roll(w_inc * v, -1)
        v1[l] = total + w_raan * lane_roll(v, 1) + lane_roll(w_raan * v, -1)

    def edge_after(l, outer, m):
        face = 0.5 * (eka[l] + m * eka[outer])
        dg = diag[l] + face
        inv = OMEGA / dg
        wa[min(l, outer)] = m * face
        diag[l] = dg
        invd[l] = inv
        v1[l] = 0.25 * ef[l] + inv * (v1[l] + (m * face) * ef[outer])

    for i in (2, 3):
        for l in (0, 3):
            unpack(rb[i, l, 0], rb[i, l, 1], ext[i], HALO + l)
    edge_before(2, 3)
    edge_before(5, 4)

    even2 = iota((16, WIDE), 1) % 2 == 0

    slot_of = [0]

    def fresh(scratch):
        slot_of[0] += 1
        return scratch.at[slot_of[0] % scratch.shape[0]]

    def row_pairs(slots, x):
        scratch = fresh(slots)
        n = x.shape[0] // 2
        for t in range(TILES):
            scratch[t] = x[:, 128 * t:128 * t + 128]
        return jnp.concatenate(
            [scratch[t, pl.ds(0, n, stride=2)] + scratch[t, pl.ds(1, n, stride=2)] for t in range(TILES)], axis=1)

    def twice(slots, x):
        scratch = fresh(slots)
        n = x.shape[0]
        for t in range(TILES):
            part = x[:, 128 * t:128 * t + 128]
            scratch[t, pl.ds(0, n, stride=2)] = part
            scratch[t, pl.ds(1, n, stride=2)] = part
        return jnp.concatenate([scratch[t] for t in range(TILES)], axis=1)

    def coarsen_fine(total):
        pairs = row_pairs(tmp, total)
        t_a, t_b = pairs[0:16], pairs[16:32]
        return 0.125 * (jnp.where(even2, t_a, t_b) + jnp.where(even2, lane_roll(t_a, -1), lane_roll(t_b, 1)))

    low3 = iota((8, WIDE), 1) % 4 < 2

    def coarsen_mid(total):
        t = row_pairs(tmp2, total)
        return 0.125 * (t + jnp.where(low3, lane_roll(t, -2), lane_roll(t, 2)))

    def fold(x):
        return jnp.where(low3, x, row_roll(x, 4))[0:4]

    upper3 = iota((8, WIDE), 0) < 4

    def unfold(part):
        both = jnp.concatenate([part, part], axis=0)
        return jnp.where(upper3, jnp.where(low3, both, lane_roll(both, 2)), jnp.where(low3, lane_roll(both, -2), both))

    for j in range(2):
        k2a[2 + j] = coarsen_fine(eka[2 + 2 * j] + eka[3 + 2 * j])
        k2b[2 + j, 0] = coarsen_fine(eki[2 + 2 * j] + eki[3 + 2 * j])
        k2b[2 + j, 1] = coarsen_fine(ekr[2 + 2 * j] + ekr[3 + 2 * j])
    k3[FAR, 0] = coarsen_mid(k2a[2] + k2a[3])
    k3[FAR, 1] = coarsen_mid(k2b[2, 0] + k2b[3, 0])
    k3[FAR, 2] = coarsen_mid(k2b[2, 1] + k2b[3, 1])
    coarse_alt = exchange([(k2a.at[3], k2a.at[1])], [(k2a.at[2], k2a.at[4])])
    coarse = exchange([(k2a.at[2], k2a.at[0]), (k2b.at[3], k2b.at[1])],
                      [(k2a.at[3], k2a.at[5]), (k2b.at[2], k2b.at[4])])
    for n in range(3):
        sk[n] = fold(k3[FAR, n])
    far_k = []

    def send_far_k(d):
        part = slice(0, 3) if d < FAR else slice(0, 1)
        far_k.append(exchange([(sk.at[part], lk.at[FAR - d, part])], [(sk.at[part], lk.at[FAR + d, part])], d))

    send_far_k(1)
    hear(1)
    greet(near.at[2, 0], near.at[2, 1])

    bulk.wait_recv()
    for i, slots in ((0, (0, 1)), (1, (2, 3)), (2, (4,)), (3, (5,))):
        relay[i].wait_recv()
        for n, slot in enumerate(slots):
            unpack(xb[0, slot, 0], xb[0, slot, 1], ext[i], n if len(slots) == 2 else 1)
            unpack(xb[1, slot, 0], xb[1, slot, 1], ext[i], 6 + n)
        if i == 1:
            edge_after(2, 1, m_lo)
            edge_after(5, 6, m_hi)
    for l in (1, 6):
        fine_weights(l)
        first_sweep(l)

    def weights_mid(x):
        m_down = {2: m_lo, 4: m_hi}.get(x, 1.0)
        m_up = {1: m_lo, 3: m_hi}.get(x, 1.0)
        w_down, w_up, w_inc, w_raan, dg = coarse_weights(
            k2a[x], k2a[x - 1], k2a[x + 1], m_down, m_up, k2b[x, 0], k2b[x, 1], 0.25, 2)
        for n, value in enumerate((w_down, w_up, w_inc, w_raan, dg, OMEGA / dg)):
            w2[x, n] = value

    second_sweep = functools.partial(sweep_fine, v1, v2)
    layers(2, 6, second_sweep)

    def residual_fine(l):
        return target_fine(v2, l) - diag[l] * v2[l]

    for l in (3, 4):
        p2[l] = residual_fine(l)
    swept.wait_recv()
    for n, l in enumerate((0, 7)):
        v1[l, 0:32, COLS:WIDE] = vr[n]
        v1[l, 32:64, COLS:WIDE] = lane_roll(vr[n], 64)
    second_sweep(1)
    second_sweep(6)
    coarse_alt.wait_recv()
    weights_mid(2)
    weights_mid(3)
    for j in range(2):
        rhs2[2 + j] = coarsen_fine(p2[3 + j] + residual_fine(2 + 3 * j))
        c2a[2 + j] = rhs2[2 + j] * w2[2 + j, 5]
    sb4[0, 0] = rhs2[3]
    sb4[0, 1] = c2a[2]
    sb4[1, 0] = rhs2[2]
    sb4[1, 1] = c2a[3]
    mid = exchange([(sb4.at[0], rb4.at[0])], [(sb4.at[1], rb4.at[1])])

    send_far_k(2)
    send_far_k(3)
    hear(2)
    send_far_k(4)
    coarse.wait_recv()
    weights_mid(1)
    weights_mid(4)

    def weights_far(x):
        at = a + x - FAR
        m_down = jnp.where(at == 0, 0.0, 1.0).astype(jnp.float32)
        m_up = jnp.where(at == n_alt - 1, 0.0, 1.0).astype(jnp.float32)
        w_down, w_up, w_inc, w_raan, dg = coarse_weights(
            k3[x, 0], k3[x - 1, 0], k3[x + 1, 0], m_down, m_up, k3[x, 1], k3[x, 2], 0.0625, 4)
        for n, value in enumerate((w_down, w_up, w_inc, w_raan, OMEGA / dg)):
            w3[x, n] = value

    def take_far(x):
        for n in range(1 if x in (0, 2 * FAR) else 3):
            k3[x, n] = unfold(lk[x, n])

    far_k[0].wait_recv()
    take_far(FAR - 1)
    take_far(FAR + 1)
    weights_far(FAR)

    mid.wait_recv()
    rhs2[1] = rb4[0, 0]
    rhs2[4] = rb4[1, 0]

    def target_mid(values, x):
        return rhs2[x] + beside_coarse(
            values[x], values[x - 1], values[x + 1], w2[x, 0], w2[x, 1], w2[x, 2], w2[x, 3], 2)

    def sweep_mid(values, x):
        return 0.25 * values[x] + w2[x, 5] * target_mid(values, x)

    before = [rb4[0, 1], rb4[0, 0] * w2[1, 5], c2a[2], c2a[3], rb4[1, 0] * w2[4, 5], rb4[1, 1]]
    before[1:5] = [sweep_mid(before, x) for x in range(1, 5)]
    residual = [target_mid(before, x) - w2[x, 4] * before[x] for x in (2, 3)]
    r3[FAR] = coarsen_mid(residual[0] + residual[1])
    sr[0] = fold(r3[FAR])
    first3 = r3[FAR] * w3[FAR, 4]
    sr[1] = fold(first3)
    far = []
    for d in range(FAR, 0, -1):
        part = sr.at[0 if d < FAR else 1]
        far.append(exchange([(part, lr.at[FAR - d])], [(part, lr.at[FAR + d])], d))
    for x in range(1, 5):
        c2b[x] = before[x]
    ends = exchange([(c2b.at[2], c2b.at[0])], [(c2b.at[3], c2b.at[5])])
    dens2 = exchange([(v2.at[4], v2.at[0])], [(v2.at[3], v2.at[7])])

    for copy in far_k[1:]:
        copy.wait_recv()
    for x in range(2 * FAR + 1):
        if abs(x - FAR) > 1:
            take_far(x)
    for x in range(1, 2 * FAR):
        if x != FAR:
            weights_far(x)
    for copy in far:
        copy.wait_recv()
    for x in range(2 * FAR + 1):
        if x != FAR:
            r3[x] = unfold(lr[x])
    v3 = [r3[x] if x in (0, 2 * FAR) else r3[x] * w3[x, 4] for x in range(2 * FAR + 1)]
    for n in range(3):
        old = list(v3)
        for x in range(1 + n, 2 * FAR - n):
            total = r3[x] + beside_coarse(old[x], old[x - 1], old[x + 1], w3[x, 0], w3[x, 1], w3[x, 2], w3[x, 3], 4)
            v3[x] = 0.25 * old[x] + w3[x, 4] * total

    ends.wait_recv()
    after = [None] * 6
    for j in range(3):
        part = twice(tmp2, v3[FAR - 1 + j])
        for x in (2 * j, 2 * j + 1):
            after[x] = c2b[x] + part
    after[1:5] = [sweep_mid(after, x) for x in range(1, 5)]
    for x in (2, 3):
        q2[x] = sweep_mid(after, x)
    up2 = exchange([(q2.at[3], q2.at[1])], [(q2.at[2], q2.at[4])])

    def refine_mid(x):
        c = q2[x]
        part_a = jnp.where(even2, c, lane_roll(c, 1))
        part_b = jnp.where(even2, lane_roll(c, -1), c)
        rf[x] = twice(tmp, jnp.concatenate([part_a, part_b], axis=0))

    def correct(x):
        refine_mid(x)
        for l in (2 * x - 2, 2 * x - 1):
            p0[l] = v2[l] + rf[x]

    correct(2)
    correct(3)
    last_sweep = functools.partial(sweep_fine, p0, p1)
    layers(3, 5, last_sweep)
    inner = exchange([(p1.at[4, :, cols], p1.at[0, :, cols])], [(p1.at[3, :, cols], p1.at[7, :, cols])])

    def last_before(l, inward):
        v = p0[l]
        total = ef[l] + wa[min(l, inward)] * p0[inward] + wi[l] * row_roll(v, 1) + row_roll(wi[l] * v, -1)
        p1[l] = total + wr[l] * lane_roll(v, 1) + lane_roll(wr[l] * v, -1)

    def last_after(l, outward):
        p1[l] = 0.25 * p0[l] + invd[l] * (p1[l] + wa[min(l, outward)] * p0[outward])

    last_before(2, 3)
    last_before(5, 4)
    dens2.wait_recv()
    up2.wait_recv()
    correct(1)
    correct(4)
    last_after(2, 1)
    last_after(5, 6)
    last_sweep(1)
    last_sweep(6)
    def final_sweep(l):
        sweep_fine(p1, p2, l)
        result[l - HALO] = p2[l, :, cols]

    def last_residual(l):
        value = (1.0 / OMEGA) * (invd[l] * target_fine(p2, l)) - p2[l]
        result[l - HALO + OWN] = value[:, 0:COLS]

    layers(2, 6, final_sweep)
    layers(3, 5, last_residual)
    inner.wait_recv()
    sweep_fine(p1, p2, 1)
    sweep_fine(p1, p2, 6)
    last_residual(2)
    last_residual(5)
    for copy in sends:
        copy.wait_send()


def solution(mesh):
    n_alt, n_raan = mesh.shape["alt"], mesh.shape["raan"]
    spec = P("alt", None, "raan")

    def vmem(*shape):
        return pltpu.VMEM(shape, jnp.float32)

    def shards(source, k_alt, k_inc, k_raan):
        scratch = [vmem(LAYERS, INC, WIDE)] * 14
        scratch += [vmem(4, OWN, 2, 16, 128), vmem(4, OWN, 2, 16, 128), vmem(2, 6, 2, 16, 128), vmem(2, 32, 128), vmem(2, 32, 128),
                    vmem(4, TILES, INC, 128), vmem(4, TILES, 16, 128)]
        scratch += [vmem(6, 16, WIDE), vmem(6, 2, 16, WIDE), vmem(6, 6, 16, WIDE), vmem(2, 2, 16, WIDE),
                    vmem(2, 2, 16, WIDE)] + [vmem(6, 16, WIDE)] * 4 + [vmem(6, INC, WIDE)]
        scratch += [vmem(2 * FAR + 1, 3, 8, WIDE), vmem(2 * FAR + 1, 5, 8, WIDE), vmem(2 * FAR + 1, 8, WIDE),
                    vmem(3, 4, WIDE), vmem(2 * FAR + 1, 3, 4, WIDE),
                    vmem(2, 4, WIDE), vmem(2 * FAR + 1, 4, WIDE)]
        scratch += [pltpu.SemaphoreType.DMA((4,)),
                    pltpu.SemaphoreType.DMA((64,)), pltpu.SemaphoreType.DMA((64,)),
                    pltpu.SemaphoreType.REGULAR((3, 2))]
        shape = pltpu.VMEM((2 * OWN, INC, COLS), source.dtype)
        result = pl.pallas_call(
            functools.partial(kernel, n_alt, n_raan),
            out_shape=shape,
            in_specs=[pl.BlockSpec(memory_space=pltpu.HBM)] * 4,
            out_specs=pl.BlockSpec(memory_space=pltpu.VMEM),
            scratch_shapes=scratch,
            compiler_params=pltpu.CompilerParams(
                collective_id=0, has_side_effects=True, vmem_limit_bytes=60 * 1024 * 1024),
            name="vcycle",
        )(source, k_alt, k_inc, k_raan)
        return result[:OWN], result[OWN:]

    return jax.shard_map(shards, mesh=mesh, in_specs=(spec,) * 4, out_specs=(spec, spec), check_vma=False)
```

```python
import functools

import jax
import jax.numpy as jnp
from jax import lax
from jax.experimental import pallas as pl
from jax.experimental.pallas import tpu as pltpu
from jax.sharding import PartitionSpec as P

OMEGA = 0.75
MESH = pl.DeviceIdType.MESH

INC = 64
COLS = 256
WIDE = 384
HALO = 2
OWN = 4
TILES = WIDE // 128
LAYERS = OWN + 2 * HALO
FAR = 4


def lane_roll(x, shift):
    return pltpu.roll(x, shift % x.shape[-1], axis=x.ndim - 1)


def row_roll(x, shift):
    return pltpu.roll(x, shift % x.shape[-2], axis=x.ndim - 2)


def iota(shape, dim):
    return lax.broadcasted_iota(jnp.int32, shape, dim)


def beside_fine(v, down, up, w_down, w_up, w_inc, w_raan):
    total = w_down * down + w_up * up
    total = total + w_inc * row_roll(v, 1) + row_roll(w_inc * v, -1)
    return total + w_raan * lane_roll(v, 1) + lane_roll(w_raan * v, -1)


def prev_row(v):
    turned = row_roll(v, 1)
    top = turned[0:8]
    top = jnp.where(iota(top.shape, 0) == 0, lane_roll(top, 1), top)
    return top if v.shape[0] == 8 else jnp.concatenate([top, turned[8:]], axis=0)


def next_row(v):
    turned = row_roll(v, -1)
    end = turned[-8:]
    end = jnp.where(iota(end.shape, 0) == 7, lane_roll(end, -1), end)
    return end if v.shape[0] == 8 else jnp.concatenate([turned[:-8], end], axis=0)


def coarse_weights(k_alt, k_down, k_up, m_down, m_up, k_inc, k_raan, factor, step):
    half = 0.5 * factor
    lo = half * (k_alt + m_down * k_down)
    hi = half * (k_alt + m_up * k_up)
    outer = (iota(k_inc.shape, 0) == 0) & (iota(k_inc.shape, 1) % 2 == 0)
    w_inc = jnp.where(outer, 0.0, half * (k_inc + prev_row(k_inc)))
    w_raan = half * (k_raan + lane_roll(k_raan, step))
    diagonal = 1.0 + (lo + hi + w_inc + next_row(w_inc) + w_raan + lane_roll(w_raan, -step))
    return m_down * lo, m_up * hi, w_inc, w_raan, diagonal


def beside_coarse(v, down, up, w_down, w_up, w_inc, w_raan, step):
    total = w_down * down + w_up * up
    total = total + w_inc * prev_row(v) + next_row(w_inc * v)
    return total + w_raan * lane_roll(v, step) + lane_roll(w_raan * v, -step)


class Exchange:
    def __init__(self, ups, downs, distance, has_up, has_down):
        self.ups, self.downs = ups, downs
        self.has_up, self.has_down = has_up(distance), has_down(distance)

    def start(self):
        @pl.when(self.has_up)
        def _():
            for copy in self.ups:
                copy.start()

        @pl.when(self.has_down)
        def _():
            for copy in self.downs:
                copy.start()

    def wait_recv(self):
        @pl.when(self.has_down)
        def _():
            for copy in self.ups:
                copy.wait_recv()

        @pl.when(self.has_up)
        def _():
            for copy in self.downs:
                copy.wait_recv()

    def wait_send(self):
        @pl.when(self.has_up)
        def _():
            for copy in self.ups:
                copy.wait_send()

        @pl.when(self.has_down)
        def _():
            for copy in self.downs:
                copy.wait_send()


def kernel(n_alt, n_raan, f_hbm, ka_hbm, ki_hbm, kr_hbm, result,
           ef, eka, eki, ekr, v1, v2, p0, p1, p2, wa, wi, wr, invd, diag,
           pack, rb, xb, vs, vr, tmp, tmp2,
           k2a, k2b, w2, sb4, rb4, rhs2, c2a, c2b, q2, rf,
           k3, w3, r3, sk, lk, sr, lr,
           load_sem, send_sem, recv_sem, near):
    a = lax.axis_index("alt")
    r = lax.axis_index("raan")
    m_lo = jnp.where(a == 0, 0.0, 1.0).astype(jnp.float32)
    m_hi = jnp.where(a == n_alt - 1, 0.0, 1.0).astype(jnp.float32)

    def has_up(d):
        return a < n_alt - d

    def has_down(d):
        return a >= d

    def alt_dev(d):
        return (lax.rem(a + d + n_alt, n_alt), r)

    def raan_dev(d):
        return (a, lax.rem(r + d + n_raan, n_raan))

    count = [0]
    sends = []

    def describe(src, dst, device):
        k = count[0]
        count[0] += 1
        return pltpu.make_async_remote_copy(
            src_ref=src, dst_ref=dst, send_sem=send_sem.at[k], recv_sem=recv_sem.at[k],
            device_id=device, device_id_type=MESH)

    def remote(src, dst, device):
        copy = describe(src, dst, device)
        copy.start()
        sends.append(copy)
        return copy

    def exchange(ups, downs, distance=1):
        copy = Exchange([describe(s, d, alt_dev(distance)) for s, d in ups],
                        [describe(s, d, alt_dev(-distance)) for s, d in downs], distance, has_up, has_down)
        copy.start()
        sends.append(copy)
        return copy

    hbm = (f_hbm, ka_hbm, ki_hbm, kr_hbm)
    ext = (ef, eka, eki, ekr)
    cols = slice(0, COLS)
    own = slice(HALO, HALO + OWN)
    loads = []
    for i in range(4):
        loads.append(pltpu.make_async_copy(hbm[i], ext[i].at[own, :, cols], load_sem.at[i]))

    barrier = pltpu.get_barrier_semaphore()

    def greet(sem_up, sem_down):
        @pl.when(has_up(1))
        def _():
            pl.semaphore_signal(sem_up, inc=1, device_id=alt_dev(1), device_id_type=MESH)

        @pl.when(has_down(1))
        def _():
            pl.semaphore_signal(sem_down, inc=1, device_id=alt_dev(-1), device_id_type=MESH)

    greet(barrier, barrier)
    for side in (1, -1):
        pl.semaphore_signal(barrier, inc=1, device_id=raan_dev(side), device_id_type=MESH)
    for i in range(4):
        loads[i].start()

    @pl.when(a == 0)
    def _():
        for ref in (ef, eka, eki, ekr, v1, v2, p1):
            ref[0:HALO] = jnp.zeros((HALO, INC, WIDE), jnp.float32)
        xb[0] = jnp.zeros(xb.shape[1:], jnp.float32)
        vr[0] = jnp.zeros(vr.shape[1:], jnp.float32)
        rb4[0] = jnp.zeros(rb4.shape[1:], jnp.float32)
        for ref in (k2a, k2b, c2b, q2):
            ref[0:2] = jnp.zeros((2,) + ref.shape[1:], jnp.float32)

    @pl.when(a == n_alt - 1)
    def _():
        for ref in (ef, eka, eki, ekr, v1, v2, p1):
            ref[HALO + OWN:LAYERS] = jnp.zeros((HALO, INC, WIDE), jnp.float32)
        xb[1] = jnp.zeros(xb.shape[1:], jnp.float32)
        vr[1] = jnp.zeros(vr.shape[1:], jnp.float32)
        rb4[1] = jnp.zeros(rb4.shape[1:], jnp.float32)
        for ref in (k2a, k2b, c2b, q2):
            ref[4:6] = jnp.zeros((2,) + ref.shape[1:], jnp.float32)

    for d in range(1, FAR + 1):
        for side, here in ((d, has_up(d)), (-d, has_down(d))):
            @pl.when(jnp.logical_not(here))
            def _():
                lk[FAR + side] = jnp.zeros((3, 4, WIDE), jnp.float32)
                lr[FAR + side] = jnp.zeros((4, WIDE), jnp.float32)

    quarter = iota((16, 128), 1) // 32
    for i in range(4):
        loads[i].wait()
        for l in range(OWN):
            low = ext[i][HALO + l, :, 0:128]
            high = ext[i][HALO + l, :, 128:256]
            first = low[0:16]
            last = high[0:16]
            for g in range(1, 4):
                first = jnp.where(quarter == g, lane_roll(low[16 * g:16 * g + 16], 32 * g), first)
                last = jnp.where(quarter == (3 + g) % 4, lane_roll(high[16 * g:16 * g + 16], 32 * g), last)
            pack[i, l, 0] = first
            pack[i, l, 1] = last

    pl.semaphore_wait(barrier, 2 + has_up(1).astype(jnp.int32) + has_down(1).astype(jnp.int32))

    def hear(step):
        @pl.when(has_down(1))
        def _():
            pl.semaphore_wait(near.at[step, 0], 1)

        @pl.when(has_up(1))
        def _():
            pl.semaphore_wait(near.at[step, 1], 1)

    greet(near.at[0, 0], near.at[0, 1])

    ring = []
    for i in range(4):
        ring.append((remote(pack.at[i, :, 0], rb.at[i, :, 0], raan_dev(-1)),
                     remote(pack.at[i, :, 1], rb.at[i, :, 1], raan_dev(1))))

    low2, high2, low1, high1 = slice(0, 2), slice(2, 4), slice(0, 1), slice(3, 4)
    below2, above2, below1, above1 = slice(0, 2), slice(6, 8), slice(1, 2), slice(6, 7)
    bulk = exchange(
        [(ext[i].at[slice(4, 6) if i < 2 else slice(5, 6), :, cols], ext[i].at[below2 if i < 2 else below1, :, cols])
         for i in range(4)],
        [(ext[i].at[slice(2, 4) if i < 2 else slice(2, 3), :, cols], ext[i].at[above2 if i < 2 else above1, :, cols])
         for i in range(4)])

    def unpack(first, last, dst, layer):
        for g in range(4):
            both = jnp.where(quarter == g, first, last)
            dst[layer, 16 * g:16 * g + 16, COLS:WIDE] = lane_roll(both, -32 * g) if g else both

    relay = []
    x_slot = (slice(0, 2), slice(2, 4), slice(4, 5), slice(5, 6))
    for i in range(4):
        for copy in ring[i]:
            copy.wait_recv()
        relay.append(exchange([(rb.at[i, high2 if i < 2 else high1], xb.at[0, x_slot[i]])],
                              [(rb.at[i, low2 if i < 2 else low1], xb.at[1, x_slot[i]])]))
        if i == 1:
            hear(0)
            greet(near.at[1, 0], near.at[1, 1])
        for l in range(OWN) if i < 2 else (1, 2):
            unpack(rb[i, l, 0], rb[i, l, 1], ext[i], HALO + l)

    row0 = iota((INC, WIDE), 0) == 0

    def fine_weights(l):
        m_down = {HALO: m_lo, HALO + OWN: m_hi}.get(l, 1.0)
        m_up = {HALO - 1: m_lo, HALO + OWN - 1: m_hi}.get(l, 1.0)
        k_alt = eka[l]
        lo = 0.5 * (k_alt + m_down * eka[l - 1])
        hi = 0.5 * (k_alt + m_up * eka[l + 1])
        k_inc = eki[l]
        w_inc = jnp.where(row0, 0.0, 0.5 * (k_inc + row_roll(k_inc, 1)))
        k_raan = ekr[l]
        w_raan = 0.5 * (k_raan + lane_roll(k_raan, 1))
        dg = 1.0 + (lo + hi + w_inc + row_roll(w_inc, -1) + w_raan + lane_roll(w_raan, -1))
        wa[l - 1] = m_down * lo
        wa[l] = m_up * hi
        wi[l] = w_inc
        wr[l] = w_raan
        diag[l] = dg
        invd[l] = OMEGA / dg

    def target_fine(src, l):
        return ef[l] + beside_fine(src[l], src[l - 1], src[l + 1], wa[l - 1], wa[l], wi[l], wr[l])

    def sweep_fine(src, dst, l):
        dst[l] = 0.25 * src[l] + invd[l] * target_fine(src, l)

    def layers(lo, hi, *bodies):
        for l in range(lo, hi):
            for one in bodies:
                one(l)

    first_sweep = functools.partial(sweep_fine, ef, v1)
    layers(3, 5, fine_weights, first_sweep)
    between = (iota((32, 128), 1) >= 32) & (iota((32, 128), 1) < 96)
    for n, l in enumerate((4, 3)):
        side = v1[l, :, COLS:WIDE]
        vs[n] = jnp.where(between, lane_roll(side[32:64], 64), side[0:32])
    swept = exchange([(v1.at[4, :, cols], v1.at[0, :, cols]), (vs.at[0], vr.at[0])],
                     [(v1.at[3, :, cols], v1.at[7, :, cols]), (vs.at[1], vr.at[1])])

    def edge_before(l, inner):
        face = wa[min(l, inner)]
        k_inc = eki[l]
        w_inc = jnp.where(row0, 0.0, 0.5 * (k_inc + row_roll(k_inc, 1)))
        k_raan = ekr[l]
        w_raan = 0.5 * (k_raan + lane_roll(k_raan, 1))
        wi[l] = w_inc
        wr[l] = w_raan
        diag[l] = 1.0 + (face + w_inc + row_roll(w_inc, -1) + w_raan + lane_roll(w_raan, -1))
        v = ef[l]
        total = v + face * ef[inner] + w_inc * row_roll(v, 1) + row_roll(w_inc * v, -1)
        v1[l] = total + w_raan * lane_roll(v, 1) + lane_roll(w_raan * v, -1)

    def edge_after(l, outer, m):
        face = 0.5 * (eka[l] + m * eka[outer])
        dg = diag[l] + face
        inv = OMEGA / dg
        wa[min(l, outer)] = m * face
        diag[l] = dg
        invd[l] = inv
        v1[l] = 0.25 * ef[l] + inv * (v1[l] + (m * face) * ef[outer])

    for i in (2, 3):
        for l in (0, 3):
            unpack(rb[i, l, 0], rb[i, l, 1], ext[i], HALO + l)
    edge_before(2, 3)
    edge_before(5, 4)

    even2 = iota((16, WIDE), 1) % 2 == 0

    slot_of = [0]

    def fresh(scratch):
        slot_of[0] += 1
        return scratch.at[slot_of[0] % scratch.shape[0]]

    def row_pairs(slots, x):
        scratch = fresh(slots)
        n = x.shape[0] // 2
        for t in range(TILES):
            scratch[t, 0:2 * n] = x[:, 128 * t:128 * t + 128]
        return jnp.concatenate(
            [scratch[t, pl.ds(0, n, stride=2)] + scratch[t, pl.ds(1, n, stride=2)] for t in range(TILES)], axis=1)

    def twice(slots, x):
        scratch = fresh(slots)
        n = x.shape[0]
        for t in range(TILES):
            part = x[:, 128 * t:128 * t + 128]
            scratch[t, pl.ds(0, n, stride=2)] = part
            scratch[t, pl.ds(1, n, stride=2)] = part
        return jnp.concatenate([scratch[t, 0:2 * n] for t in range(TILES)], axis=1)

    def coarsen_fine(total):
        pairs = row_pairs(tmp, total)
        t_a, t_b = pairs[0:16], pairs[16:32]
        return 0.125 * (jnp.where(even2, t_a, t_b) + jnp.where(even2, lane_roll(t_a, -1), lane_roll(t_b, 1)))

    low3 = iota((8, WIDE), 1) % 4 < 2

    def coarsen_mid(total):
        t = row_pairs(tmp2, total)
        return 0.125 * (t + jnp.where(low3, lane_roll(t, -2), lane_roll(t, 2)))

    def fold(x):
        return jnp.where(low3, x, row_roll(x, 4))[0:4]

    upper3 = iota((8, WIDE), 0) < 4

    def unfold(part):
        both = jnp.concatenate([part, part], axis=0)
        return jnp.where(upper3, jnp.where(low3, both, lane_roll(both, 2)), jnp.where(low3, lane_roll(both, -2), both))

    for j in range(2):
        k2a[2 + j] = coarsen_fine(eka[2 + 2 * j] + eka[3 + 2 * j])
        k2b[2 + j, 0] = coarsen_fine(eki[2 + 2 * j] + eki[3 + 2 * j])
        k2b[2 + j, 1] = coarsen_fine(ekr[2 + 2 * j] + ekr[3 + 2 * j])
    k3[FAR, 0] = coarsen_mid(k2a[2] + k2a[3])
    k3[FAR, 1] = coarsen_mid(k2b[2, 0] + k2b[3, 0])
    k3[FAR, 2] = coarsen_mid(k2b[2, 1] + k2b[3, 1])
    coarse_alt = exchange([(k2a.at[3], k2a.at[1])], [(k2a.at[2], k2a.at[4])])
    coarse = exchange([(k2a.at[2], k2a.at[0]), (k2b.at[3], k2b.at[1])],
                      [(k2a.at[3], k2a.at[5]), (k2b.at[2], k2b.at[4])])
    for n in range(3):
        sk[n] = fold(k3[FAR, n])
    far_k = []

    def send_far_k(d):
        part = slice(0, 3) if d < FAR else slice(0, 1)
        far_k.append(exchange([(sk.at[part], lk.at[FAR - d, part])], [(sk.at[part], lk.at[FAR + d, part])], d))

    send_far_k(1)
    hear(1)
    greet(near.at[2, 0], near.at[2, 1])

    bulk.wait_recv()
    for i, slots in ((0, (0, 1)), (1, (2, 3)), (2, (4,)), (3, (5,))):
        relay[i].wait_recv()
        for n, slot in enumerate(slots):
            unpack(xb[0, slot, 0], xb[0, slot, 1], ext[i], n if len(slots) == 2 else 1)
            unpack(xb[1, slot, 0], xb[1, slot, 1], ext[i], 6 + n)
        if i == 1:
            edge_after(2, 1, m_lo)
            edge_after(5, 6, m_hi)
    for l in (1, 6):
        fine_weights(l)
        first_sweep(l)

    def weights_mid(x):
        m_down = {2: m_lo, 4: m_hi}.get(x, 1.0)
        m_up = {1: m_lo, 3: m_hi}.get(x, 1.0)
        w_down, w_up, w_inc, w_raan, dg = coarse_weights(
            k2a[x], k2a[x - 1], k2a[x + 1], m_down, m_up, k2b[x, 0], k2b[x, 1], 0.25, 2)
        for n, value in enumerate((w_down, w_up, w_inc, w_raan, dg, OMEGA / dg)):
            w2[x, n] = value

    second_sweep = functools.partial(sweep_fine, v1, v2)
    layers(2, 6, second_sweep)

    def residual_fine(l):
        return target_fine(v2, l) - diag[l] * v2[l]

    for l in (3, 4):
        p2[l] = residual_fine(l)
    swept.wait_recv()
    for n, l in enumerate((0, 7)):
        v1[l, 0:32, COLS:WIDE] = vr[n]
        v1[l, 32:64, COLS:WIDE] = lane_roll(vr[n], 64)
    second_sweep(1)
    second_sweep(6)
    coarse_alt.wait_recv()
    weights_mid(2)
    weights_mid(3)
    for j in range(2):
        rhs2[2 + j] = coarsen_fine(p2[3 + j] + residual_fine(2 + 3 * j))
        c2a[2 + j] = rhs2[2 + j] * w2[2 + j, 5]
    sb4[0, 0] = rhs2[3]
    sb4[0, 1] = c2a[2]
    sb4[1, 0] = rhs2[2]
    sb4[1, 1] = c2a[3]
    mid = exchange([(sb4.at[0], rb4.at[0])], [(sb4.at[1], rb4.at[1])])

    send_far_k(2)
    send_far_k(3)
    hear(2)
    send_far_k(4)
    coarse.wait_recv()
    weights_mid(1)
    weights_mid(4)

    def weights_far(x):
        at = a + x - FAR
        m_down = jnp.where(at == 0, 0.0, 1.0).astype(jnp.float32)
        m_up = jnp.where(at == n_alt - 1, 0.0, 1.0).astype(jnp.float32)
        w_down, w_up, w_inc, w_raan, dg = coarse_weights(
            k3[x, 0], k3[x - 1, 0], k3[x + 1, 0], m_down, m_up, k3[x, 1], k3[x, 2], 0.0625, 4)
        for n, value in enumerate((w_down, w_up, w_inc, w_raan, OMEGA / dg)):
            w3[x, n] = value

    def take_far(x):
        for n in range(1 if x in (0, 2 * FAR) else 3):
            k3[x, n] = unfold(lk[x, n])

    far_k[0].wait_recv()
    take_far(FAR - 1)
    take_far(FAR + 1)
    weights_far(FAR)

    mid.wait_recv()
    rhs2[1] = rb4[0, 0]
    rhs2[4] = rb4[1, 0]

    def target_mid(values, x):
        return rhs2[x] + beside_coarse(
            values[x], values[x - 1], values[x + 1], w2[x, 0], w2[x, 1], w2[x, 2], w2[x, 3], 2)

    def sweep_mid(values, x):
        return 0.25 * values[x] + w2[x, 5] * target_mid(values, x)

    before = [rb4[0, 1], rb4[0, 0] * w2[1, 5], c2a[2], c2a[3], rb4[1, 0] * w2[4, 5], rb4[1, 1]]
    before[1:5] = [sweep_mid(before, x) for x in range(1, 5)]
    residual = [target_mid(before, x) - w2[x, 4] * before[x] for x in (2, 3)]
    r3[FAR] = coarsen_mid(residual[0] + residual[1])
    sr[0] = fold(r3[FAR])
    first3 = r3[FAR] * w3[FAR, 4]
    sr[1] = fold(first3)
    far = []
    for d in range(FAR, 0, -1):
        part = sr.at[0 if d < FAR else 1]
        far.append(exchange([(part, lr.at[FAR - d])], [(part, lr.at[FAR + d])], d))
    for x in range(1, 5):
        c2b[x] = before[x]
    ends = exchange([(c2b.at[2], c2b.at[0])], [(c2b.at[3], c2b.at[5])])
    dens2 = exchange([(v2.at[4], v2.at[0])], [(v2.at[3], v2.at[7])])

    for copy in far_k[1:]:
        copy.wait_recv()
    for x in range(2 * FAR + 1):
        if abs(x - FAR) > 1:
            take_far(x)
    for x in range(1, 2 * FAR):
        if x != FAR:
            weights_far(x)
    for copy in far:
        copy.wait_recv()
    for x in range(2 * FAR + 1):
        if x != FAR:
            r3[x] = unfold(lr[x])
    v3 = [r3[x] if x in (0, 2 * FAR) else r3[x] * w3[x, 4] for x in range(2 * FAR + 1)]
    for n in range(3):
        old = list(v3)
        for x in range(1 + n, 2 * FAR - n):
            total = r3[x] + beside_coarse(old[x], old[x - 1], old[x + 1], w3[x, 0], w3[x, 1], w3[x, 2], w3[x, 3], 4)
            v3[x] = 0.25 * old[x] + w3[x, 4] * total

    ends.wait_recv()
    after = [None] * 6
    for j in range(3):
        part = twice(tmp2, v3[FAR - 1 + j])
        for x in (2 * j, 2 * j + 1):
            after[x] = c2b[x] + part
    after[1:5] = [sweep_mid(after, x) for x in range(1, 5)]
    for x in (2, 3):
        q2[x] = sweep_mid(after, x)
    up2 = exchange([(q2.at[3], q2.at[1])], [(q2.at[2], q2.at[4])])

    def refine_mid(x):
        c = q2[x]
        part_a = jnp.where(even2, c, lane_roll(c, 1))
        part_b = jnp.where(even2, lane_roll(c, -1), c)
        rf[x] = twice(tmp, jnp.concatenate([part_a, part_b], axis=0))

    def correct(x):
        refine_mid(x)
        for l in (2 * x - 2, 2 * x - 1):
            p0[l] = v2[l] + rf[x]

    correct(2)
    correct(3)
    last_sweep = functools.partial(sweep_fine, p0, p1)
    layers(3, 5, last_sweep)
    inner = exchange([(p1.at[4, :, cols], p1.at[0, :, cols])], [(p1.at[3, :, cols], p1.at[7, :, cols])])

    def last_before(l, inward):
        v = p0[l]
        total = ef[l] + wa[min(l, inward)] * p0[inward] + wi[l] * row_roll(v, 1) + row_roll(wi[l] * v, -1)
        p1[l] = total + wr[l] * lane_roll(v, 1) + lane_roll(wr[l] * v, -1)

    def last_after(l, outward):
        p1[l] = 0.25 * p0[l] + invd[l] * (p1[l] + wa[min(l, outward)] * p0[outward])

    last_before(2, 3)
    last_before(5, 4)
    dens2.wait_recv()
    up2.wait_recv()
    correct(1)
    correct(4)
    last_after(2, 1)
    last_after(5, 6)
    last_sweep(1)
    last_sweep(6)
    def final_sweep(l):
        sweep_fine(p1, p2, l)
        result[l - HALO] = p2[l, :, cols]

    def last_residual(l):
        value = (1.0 / OMEGA) * (invd[l] * target_fine(p2, l)) - p2[l]
        result[l - HALO + OWN] = value[:, 0:COLS]

    layers(2, 6, final_sweep)
    layers(3, 5, last_residual)
    inner.wait_recv()
    sweep_fine(p1, p2, 1)
    sweep_fine(p1, p2, 6)
    last_residual(2)
    last_residual(5)
    for copy in sends:
        copy.wait_send()


def solution(mesh):
    n_alt, n_raan = mesh.shape["alt"], mesh.shape["raan"]
    spec = P("alt", None, "raan")

    def vmem(*shape):
        return pltpu.VMEM(shape, jnp.float32)

    def shards(source, k_alt, k_inc, k_raan):
        scratch = [vmem(LAYERS, INC, WIDE)] * 14
        scratch += [vmem(4, OWN, 2, 16, 128), vmem(4, OWN, 2, 16, 128), vmem(2, 6, 2, 16, 128), vmem(2, 32, 128), vmem(2, 32, 128),
                    vmem(4, TILES, INC + 8, 128), vmem(4, TILES, 24, 128)]
        scratch += [vmem(6, 16, WIDE), vmem(6, 2, 16, WIDE), vmem(6, 6, 16, WIDE), vmem(2, 2, 16, WIDE),
                    vmem(2, 2, 16, WIDE)] + [vmem(6, 16, WIDE)] * 4 + [vmem(6, INC, WIDE)]
        scratch += [vmem(2 * FAR + 1, 3, 8, WIDE), vmem(2 * FAR + 1, 5, 8, WIDE), vmem(2 * FAR + 1, 8, WIDE),
                    vmem(4, 4, WIDE), vmem(2 * FAR + 2, 3, 4, WIDE),
                    vmem(3, 4, WIDE), vmem(2 * FAR + 2, 4, WIDE)]
        scratch += [pltpu.SemaphoreType.DMA((4,)),
                    pltpu.SemaphoreType.DMA((64,)), pltpu.SemaphoreType.DMA((64,)),
                    pltpu.SemaphoreType.REGULAR((3, 2))]
        shape = pltpu.VMEM((2 * OWN, INC, COLS), source.dtype)
        result = pl.pallas_call(
            functools.partial(kernel, n_alt, n_raan),
            out_shape=shape,
            in_specs=[pl.BlockSpec(memory_space=pltpu.HBM)] * 4,
            out_specs=pl.BlockSpec(memory_space=pltpu.VMEM),
            scratch_shapes=scratch,
            compiler_params=pltpu.CompilerParams(
                collective_id=0, has_side_effects=True, vmem_limit_bytes=60 * 1024 * 1024),
            name="vcycle",
        )(source, k_alt, k_inc, k_raan)
        return result[:OWN], result[OWN:]

    return jax.shard_map(shards, mesh=mesh, in_specs=(spec,) * 4, out_specs=(spec, spec), check_vma=False)
```

```python
import functools

import jax
import jax.numpy as jnp
from jax import lax
from jax.experimental import pallas as pl
from jax.experimental.pallas import tpu as pltpu
from jax.sharding import PartitionSpec as P

OMEGA = 0.75
MESH = pl.DeviceIdType.MESH

INC = 64
COLS = 256
WIDE = 384
HALO = 2
OWN = 4
TILES = WIDE // 128
LAYERS = OWN + 2 * HALO
FAR = 4


def lane_roll(x, shift):
    return pltpu.roll(x, shift % x.shape[-1], axis=x.ndim - 1)


def row_roll(x, shift):
    return pltpu.roll(x, shift % x.shape[-2], axis=x.ndim - 2)


def iota(shape, dim):
    return lax.broadcasted_iota(jnp.int32, shape, dim)


def beside_fine(v, down, up, w_down, w_up, w_inc, w_raan):
    total = w_down * down + w_up * up
    total = total + w_inc * row_roll(v, 1) + row_roll(w_inc * v, -1)
    return total + w_raan * lane_roll(v, 1) + lane_roll(w_raan * v, -1)


def prev_row(v):
    turned = row_roll(v, 1)
    top = turned[0:8]
    top = jnp.where(iota(top.shape, 0) == 0, lane_roll(top, 1), top)
    return top if v.shape[0] == 8 else jnp.concatenate([top, turned[8:]], axis=0)


def next_row(v):
    turned = row_roll(v, -1)
    end = turned[-8:]
    end = jnp.where(iota(end.shape, 0) == 7, lane_roll(end, -1), end)
    return end if v.shape[0] == 8 else jnp.concatenate([turned[:-8], end], axis=0)


def coarse_weights(k_alt, k_down, k_up, m_down, m_up, k_inc, k_raan, factor, step):
    half = 0.5 * factor
    lo = half * (k_alt + m_down * k_down)
    hi = half * (k_alt + m_up * k_up)
    outer = (iota(k_inc.shape, 0) == 0) & (iota(k_inc.shape, 1) % 2 == 0)
    w_inc = jnp.where(outer, 0.0, half * (k_inc + prev_row(k_inc)))
    w_raan = half * (k_raan + lane_roll(k_raan, step))
    diagonal = 1.0 + (lo + hi + w_inc + next_row(w_inc) + w_raan + lane_roll(w_raan, -step))
    return m_down * lo, m_up * hi, w_inc, w_raan, diagonal


def beside_coarse(v, down, up, w_down, w_up, w_inc, w_raan, step):
    total = w_down * down + w_up * up
    total = total + w_inc * prev_row(v) + next_row(w_inc * v)
    return total + w_raan * lane_roll(v, step) + lane_roll(w_raan * v, -step)


class Exchange:
    def __init__(self, ups, downs, distance, has_up, has_down):
        self.ups, self.downs = ups, downs
        self.has_up, self.has_down = has_up(distance), has_down(distance)

    def start(self):
        @pl.when(self.has_up)
        def _():
            for copy in self.ups:
                copy.start()

        @pl.when(self.has_down)
        def _():
            for copy in self.downs:
                copy.start()

    def wait_recv(self):
        @pl.when(self.has_down)
        def _():
            for copy in self.ups:
                copy.wait_recv()

        @pl.when(self.has_up)
        def _():
            for copy in self.downs:
                copy.wait_recv()

    def wait_send(self):
        @pl.when(self.has_up)
        def _():
            for copy in self.ups:
                copy.wait_send()

        @pl.when(self.has_down)
        def _():
            for copy in self.downs:
                copy.wait_send()


def kernel(n_alt, n_raan, f_hbm, ka_hbm, ki_hbm, kr_hbm, result,
           ef, eka, eki, ekr, v1, v2, p0, p1, p2, wa, wi, wr, invd, diag,
           pack, rb, xb, vs, vr, tmp, tmp2,
           k2a, k2b, w2, sb4, rb4, rhs2, c2a, c2b, q2, rf,
           k3, w3, r3, sk, lk, sr, lr,
           load_sem, send_sem, recv_sem, near):
    a = lax.axis_index("alt")
    r = lax.axis_index("raan")
    m_lo = jnp.where(a == 0, 0.0, 1.0).astype(jnp.float32)
    m_hi = jnp.where(a == n_alt - 1, 0.0, 1.0).astype(jnp.float32)

    def has_up(d):
        return a < n_alt - d

    def has_down(d):
        return a >= d

    def alt_dev(d):
        return (lax.rem(a + d + n_alt, n_alt), r)

    def raan_dev(d):
        return (a, lax.rem(r + d + n_raan, n_raan))

    count = [0]
    sends = []

    def describe(src, dst, device):
        k = count[0]
        count[0] += 1
        return pltpu.make_async_remote_copy(
            src_ref=src, dst_ref=dst, send_sem=send_sem.at[k], recv_sem=recv_sem.at[k],
            device_id=device, device_id_type=MESH)

    def remote(src, dst, device):
        copy = describe(src, dst, device)
        copy.start()
        sends.append(copy)
        return copy

    def exchange(ups, downs, distance=1):
        copy = Exchange([describe(s, d, alt_dev(distance)) for s, d in ups],
                        [describe(s, d, alt_dev(-distance)) for s, d in downs], distance, has_up, has_down)
        copy.start()
        sends.append(copy)
        return copy

    hbm = (f_hbm, ka_hbm, ki_hbm, kr_hbm)
    ext = (ef, eka, eki, ekr)
    cols = slice(0, COLS)
    own = slice(HALO, HALO + OWN)
    loads = []
    for i in range(4):
        loads.append(pltpu.make_async_copy(hbm[i], ext[i].at[own, :, cols], load_sem.at[i]))

    barrier = pltpu.get_barrier_semaphore()

    def greet(sem_up, sem_down):
        @pl.when(has_up(1))
        def _():
            pl.semaphore_signal(sem_up, inc=1, device_id=alt_dev(1), device_id_type=MESH)

        @pl.when(has_down(1))
        def _():
            pl.semaphore_signal(sem_down, inc=1, device_id=alt_dev(-1), device_id_type=MESH)

    greet(barrier, barrier)
    for side in (1, -1):
        pl.semaphore_signal(barrier, inc=1, device_id=raan_dev(side), device_id_type=MESH)
    for i in range(4):
        loads[i].start()

    @pl.when(a == 0)
    def _():
        for ref in (ef, eka, eki, ekr, v1, v2, p1):
            ref[0:HALO] = jnp.zeros((HALO, INC, WIDE), jnp.float32)
        xb[0] = jnp.zeros(xb.shape[1:], jnp.float32)
        vr[0] = jnp.zeros(vr.shape[1:], jnp.float32)
        rb4[0] = jnp.zeros(rb4.shape[1:], jnp.float32)
        for ref in (k2a, k2b, c2b, q2):
            ref[0:2] = jnp.zeros((2,) + ref.shape[1:], jnp.float32)

    @pl.when(a == n_alt - 1)
    def _():
        for ref in (ef, eka, eki, ekr, v1, v2, p1):
            ref[HALO + OWN:LAYERS] = jnp.zeros((HALO, INC, WIDE), jnp.float32)
        xb[1] = jnp.zeros(xb.shape[1:], jnp.float32)
        vr[1] = jnp.zeros(vr.shape[1:], jnp.float32)
        rb4[1] = jnp.zeros(rb4.shape[1:], jnp.float32)
        for ref in (k2a, k2b, c2b, q2):
            ref[4:6] = jnp.zeros((2,) + ref.shape[1:], jnp.float32)

    for d in range(1, FAR + 1):
        for side, here in ((d, has_up(d)), (-d, has_down(d))):
            @pl.when(jnp.logical_not(here))
            def _():
                lk[FAR + side] = jnp.zeros((3, 4, WIDE), jnp.float32)
                lr[FAR + side] = jnp.zeros((4, WIDE), jnp.float32)

    quarter = iota((16, 128), 1) // 32
    for i in range(4):
        loads[i].wait()
        for l in range(OWN):
            low = ext[i][HALO + l, :, 0:128]
            high = ext[i][HALO + l, :, 128:256]
            first = low[0:16]
            last = high[0:16]
            for g in range(1, 4):
                first = jnp.where(quarter == g, lane_roll(low[16 * g:16 * g + 16], 32 * g), first)
                last = jnp.where(quarter == (3 + g) % 4, lane_roll(high[16 * g:16 * g + 16], 32 * g), last)
            pack[i, l, 0] = first
            pack[i, l, 1] = last

    pl.semaphore_wait(barrier, 2 + has_up(1).astype(jnp.int32) + has_down(1).astype(jnp.int32))

    def hear(step):
        @pl.when(has_down(1))
        def _():
            pl.semaphore_wait(near.at[step, 0], 1)

        @pl.when(has_up(1))
        def _():
            pl.semaphore_wait(near.at[step, 1], 1)

    low2, high2, low1, high1 = slice(0, 2), slice(2, 4), slice(0, 1), slice(3, 4)
    below2, above2, below1, above1 = slice(0, 2), slice(6, 8), slice(1, 2), slice(6, 7)
    bulk = exchange(
        [(ext[i].at[slice(4, 6) if i < 2 else slice(5, 6), :, cols], ext[i].at[below2 if i < 2 else below1, :, cols])
         for i in range(4)],
        [(ext[i].at[slice(2, 4) if i < 2 else slice(2, 3), :, cols], ext[i].at[above2 if i < 2 else above1, :, cols])
         for i in range(4)])

    ring = []
    for i in range(4):
        ring.append((remote(pack.at[i, :, 0], rb.at[i, :, 0], raan_dev(-1)),
                     remote(pack.at[i, :, 1], rb.at[i, :, 1], raan_dev(1))))

    greet(near.at[0, 0], near.at[0, 1])

    def unpack(first, last, dst, layer):
        for g in range(4):
            both = jnp.where(quarter == g, first, last)
            dst[layer, 16 * g:16 * g + 16, COLS:WIDE] = lane_roll(both, -32 * g) if g else both

    relay = []
    x_slot = (slice(0, 2), slice(2, 4), slice(4, 5), slice(5, 6))
    for i in range(4):
        for copy in ring[i]:
            copy.wait_recv()
        relay.append(exchange([(rb.at[i, high2 if i < 2 else high1], xb.at[0, x_slot[i]])],
                              [(rb.at[i, low2 if i < 2 else low1], xb.at[1, x_slot[i]])]))
        if i == 1:
            hear(0)
            greet(near.at[1, 0], near.at[1, 1])
        for l in range(OWN) if i < 2 else (1, 2):
            unpack(rb[i, l, 0], rb[i, l, 1], ext[i], HALO + l)

    row0 = iota((INC, WIDE), 0) == 0

    def fine_weights(l):
        m_down = {HALO: m_lo, HALO + OWN: m_hi}.get(l, 1.0)
        m_up = {HALO - 1: m_lo, HALO + OWN - 1: m_hi}.get(l, 1.0)
        k_alt = eka[l]
        lo = 0.5 * (k_alt + m_down * eka[l - 1])
        hi = 0.5 * (k_alt + m_up * eka[l + 1])
        k_inc = eki[l]
        w_inc = jnp.where(row0, 0.0, 0.5 * (k_inc + row_roll(k_inc, 1)))
        k_raan = ekr[l]
        w_raan = 0.5 * (k_raan + lane_roll(k_raan, 1))
        dg = 1.0 + (lo + hi + w_inc + row_roll(w_inc, -1) + w_raan + lane_roll(w_raan, -1))
        wa[l - 1] = m_down * lo
        wa[l] = m_up * hi
        wi[l] = w_inc
        wr[l] = w_raan
        diag[l] = dg
        invd[l] = OMEGA / dg

    def target_fine(src, l):
        return ef[l] + beside_fine(src[l], src[l - 1], src[l + 1], wa[l - 1], wa[l], wi[l], wr[l])

    def sweep_fine(src, dst, l):
        dst[l] = 0.25 * src[l] + invd[l] * target_fine(src, l)

    def layers(lo, hi, *bodies):
        for l in range(lo, hi):
            for one in bodies:
                one(l)

    first_sweep = functools.partial(sweep_fine, ef, v1)
    layers(3, 5, fine_weights, first_sweep)
    between = (iota((32, 128), 1) >= 32) & (iota((32, 128), 1) < 96)
    for n, l in enumerate((4, 3)):
        side = v1[l, :, COLS:WIDE]
        vs[n] = jnp.where(between, lane_roll(side[32:64], 64), side[0:32])
    swept = exchange([(v1.at[4, :, cols], v1.at[0, :, cols]), (vs.at[0], vr.at[0])],
                     [(v1.at[3, :, cols], v1.at[7, :, cols]), (vs.at[1], vr.at[1])])

    def edge_before(l, inner):
        face = wa[min(l, inner)]
        k_inc = eki[l]
        w_inc = jnp.where(row0, 0.0, 0.5 * (k_inc + row_roll(k_inc, 1)))
        k_raan = ekr[l]
        w_raan = 0.5 * (k_raan + lane_roll(k_raan, 1))
        wi[l] = w_inc
        wr[l] = w_raan
        diag[l] = 1.0 + (face + w_inc + row_roll(w_inc, -1) + w_raan + lane_roll(w_raan, -1))
        v = ef[l]
        total = v + face * ef[inner] + w_inc * row_roll(v, 1) + row_roll(w_inc * v, -1)
        v1[l] = total + w_raan * lane_roll(v, 1) + lane_roll(w_raan * v, -1)

    def edge_after(l, outer, m):
        face = 0.5 * (eka[l] + m * eka[outer])
        dg = diag[l] + face
        inv = OMEGA / dg
        wa[min(l, outer)] = m * face
        diag[l] = dg
        invd[l] = inv
        v1[l] = 0.25 * ef[l] + inv * (v1[l] + (m * face) * ef[outer])

    for i in (2, 3):
        for l in (0, 3):
            unpack(rb[i, l, 0], rb[i, l, 1], ext[i], HALO + l)
    edge_before(2, 3)
    edge_before(5, 4)

    even2 = iota((16, WIDE), 1) % 2 == 0

    slot_of = [0]

    def fresh(scratch):
        slot_of[0] += 1
        return scratch.at[slot_of[0] % scratch.shape[0]]

    def row_pairs(slots, x):
        scratch = fresh(slots)
        n = x.shape[0] // 2
        for t in range(TILES):
            scratch[t, 0:2 * n] = x[:, 128 * t:128 * t + 128]
        return jnp.concatenate(
            [scratch[t, pl.ds(0, n, stride=2)] + scratch[t, pl.ds(1, n, stride=2)] for t in range(TILES)], axis=1)

    def twice(slots, x):
        scratch = fresh(slots)
        n = x.shape[0]
        for t in range(TILES):
            part = x[:, 128 * t:128 * t + 128]
            scratch[t, pl.ds(0, n, stride=2)] = part
            scratch[t, pl.ds(1, n, stride=2)] = part
        return jnp.concatenate([scratch[t, 0:2 * n] for t in range(TILES)], axis=1)

    def coarsen_fine(total):
        pairs = row_pairs(tmp, total)
        t_a, t_b = pairs[0:16], pairs[16:32]
        return 0.125 * (jnp.where(even2, t_a, t_b) + jnp.where(even2, lane_roll(t_a, -1), lane_roll(t_b, 1)))

    low3 = iota((8, WIDE), 1) % 4 < 2

    def coarsen_mid(total):
        t = row_pairs(tmp2, total)
        return 0.125 * (t + jnp.where(low3, lane_roll(t, -2), lane_roll(t, 2)))

    def fold(x):
        return jnp.where(low3, x, row_roll(x, 4))[0:4]

    upper3 = iota((8, WIDE), 0) < 4

    def unfold(part):
        both = jnp.concatenate([part, part], axis=0)
        return jnp.where(upper3, jnp.where(low3, both, lane_roll(both, 2)), jnp.where(low3, lane_roll(both, -2), both))

    for j in range(2):
        k2a[2 + j] = coarsen_fine(eka[2 + 2 * j] + eka[3 + 2 * j])
        k2b[2 + j, 0] = coarsen_fine(eki[2 + 2 * j] + eki[3 + 2 * j])
        k2b[2 + j, 1] = coarsen_fine(ekr[2 + 2 * j] + ekr[3 + 2 * j])
    k3[FAR, 0] = coarsen_mid(k2a[2] + k2a[3])
    k3[FAR, 1] = coarsen_mid(k2b[2, 0] + k2b[3, 0])
    k3[FAR, 2] = coarsen_mid(k2b[2, 1] + k2b[3, 1])
    coarse_alt = exchange([(k2a.at[3], k2a.at[1])], [(k2a.at[2], k2a.at[4])])
    coarse = exchange([(k2a.at[2], k2a.at[0]), (k2b.at[3], k2b.at[1])],
                      [(k2a.at[3], k2a.at[5]), (k2b.at[2], k2b.at[4])])
    for n in range(3):
        sk[n] = fold(k3[FAR, n])
    far_k = []

    def send_far_k(d):
        part = slice(0, 3) if d < FAR else slice(0, 1)
        far_k.append(exchange([(sk.at[part], lk.at[FAR - d, part])], [(sk.at[part], lk.at[FAR + d, part])], d))

    send_far_k(1)
    hear(1)
    greet(near.at[2, 0], near.at[2, 1])

    bulk.wait_recv()
    for i, slots in ((0, (0, 1)), (1, (2, 3)), (2, (4,)), (3, (5,))):
        relay[i].wait_recv()
        for n, slot in enumerate(slots):
            unpack(xb[0, slot, 0], xb[0, slot, 1], ext[i], n if len(slots) == 2 else 1)
            unpack(xb[1, slot, 0], xb[1, slot, 1], ext[i], 6 + n)
        if i == 1:
            edge_after(2, 1, m_lo)
            edge_after(5, 6, m_hi)
    for l in (1, 6):
        fine_weights(l)
        first_sweep(l)

    def weights_mid(x):
        m_down = {2: m_lo, 4: m_hi}.get(x, 1.0)
        m_up = {1: m_lo, 3: m_hi}.get(x, 1.0)
        w_down, w_up, w_inc, w_raan, dg = coarse_weights(
            k2a[x], k2a[x - 1], k2a[x + 1], m_down, m_up, k2b[x, 0], k2b[x, 1], 0.25, 2)
        for n, value in enumerate((w_down, w_up, w_inc, w_raan, dg, OMEGA / dg)):
            w2[x, n] = value

    second_sweep = functools.partial(sweep_fine, v1, v2)
    layers(2, 6, second_sweep)

    def residual_fine(l):
        return target_fine(v2, l) - diag[l] * v2[l]

    for l in (3, 4):
        p2[l] = residual_fine(l)
    swept.wait_recv()
    for n, l in enumerate((0, 7)):
        v1[l, 0:32, COLS:WIDE] = vr[n]
        v1[l, 32:64, COLS:WIDE] = lane_roll(vr[n], 64)
    second_sweep(1)
    second_sweep(6)
    coarse_alt.wait_recv()
    weights_mid(2)
    weights_mid(3)
    for j in range(2):
        rhs2[2 + j] = coarsen_fine(p2[3 + j] + residual_fine(2 + 3 * j))
        c2a[2 + j] = rhs2[2 + j] * w2[2 + j, 5]
    sb4[0, 0] = rhs2[3]
    sb4[0, 1] = c2a[2]
    sb4[1, 0] = rhs2[2]
    sb4[1, 1] = c2a[3]
    mid = exchange([(sb4.at[0], rb4.at[0])], [(sb4.at[1], rb4.at[1])])

    send_far_k(2)
    send_far_k(3)
    hear(2)
    send_far_k(4)
    coarse.wait_recv()
    weights_mid(1)
    weights_mid(4)

    def weights_far(x):
        at = a + x - FAR
        m_down = jnp.where(at == 0, 0.0, 1.0).astype(jnp.float32)
        m_up = jnp.where(at == n_alt - 1, 0.0, 1.0).astype(jnp.float32)
        w_down, w_up, w_inc, w_raan, dg = coarse_weights(
            k3[x, 0], k3[x - 1, 0], k3[x + 1, 0], m_down, m_up, k3[x, 1], k3[x, 2], 0.0625, 4)
        for n, value in enumerate((w_down, w_up, w_inc, w_raan, OMEGA / dg)):
            w3[x, n] = value

    def take_far(x):
        for n in range(1 if x in (0, 2 * FAR) else 3):
            k3[x, n] = unfold(lk[x, n])

    far_k[0].wait_recv()
    take_far(FAR - 1)
    take_far(FAR + 1)
    weights_far(FAR)

    mid.wait_recv()
    rhs2[1] = rb4[0, 0]
    rhs2[4] = rb4[1, 0]

    def target_mid(values, x):
        return rhs2[x] + beside_coarse(
            values[x], values[x - 1], values[x + 1], w2[x, 0], w2[x, 1], w2[x, 2], w2[x, 3], 2)

    def sweep_mid(values, x):
        return 0.25 * values[x] + w2[x, 5] * target_mid(values, x)

    before = [rb4[0, 1], rb4[0, 0] * w2[1, 5], c2a[2], c2a[3], rb4[1, 0] * w2[4, 5], rb4[1, 1]]
    before[1:5] = [sweep_mid(before, x) for x in range(1, 5)]
    residual = [target_mid(before, x) - w2[x, 4] * before[x] for x in (2, 3)]
    r3[FAR] = coarsen_mid(residual[0] + residual[1])
    sr[0] = fold(r3[FAR])
    first3 = r3[FAR] * w3[FAR, 4]
    sr[1] = fold(first3)
    far = []
    for d in range(FAR, 0, -1):
        part = sr.at[0 if d < FAR else 1]
        far.append(exchange([(part, lr.at[FAR - d])], [(part, lr.at[FAR + d])], d))
    for x in range(1, 5):
        c2b[x] = before[x]
    ends = exchange([(c2b.at[2], c2b.at[0])], [(c2b.at[3], c2b.at[5])])
    dens2 = exchange([(v2.at[4], v2.at[0])], [(v2.at[3], v2.at[7])])

    for copy in far_k[1:]:
        copy.wait_recv()
    for x in range(2 * FAR + 1):
        if abs(x - FAR) > 1:
            take_far(x)
    for x in range(1, 2 * FAR):
        if x != FAR:
            weights_far(x)
    for copy in far:
        copy.wait_recv()
    for x in range(2 * FAR + 1):
        if x != FAR:
            r3[x] = unfold(lr[x])
    v3 = [r3[x] if x in (0, 2 * FAR) else r3[x] * w3[x, 4] for x in range(2 * FAR + 1)]
    for n in range(3):
        old = list(v3)
        for x in range(1 + n, 2 * FAR - n):
            total = r3[x] + beside_coarse(old[x], old[x - 1], old[x + 1], w3[x, 0], w3[x, 1], w3[x, 2], w3[x, 3], 4)
            v3[x] = 0.25 * old[x] + w3[x, 4] * total

    ends.wait_recv()
    after = [None] * 6
    for j in range(3):
        part = twice(tmp2, v3[FAR - 1 + j])
        for x in (2 * j, 2 * j + 1):
            after[x] = c2b[x] + part
    after[1:5] = [sweep_mid(after, x) for x in range(1, 5)]
    for x in (2, 3):
        q2[x] = sweep_mid(after, x)
    up2 = exchange([(q2.at[3], q2.at[1])], [(q2.at[2], q2.at[4])])

    def refine_mid(x):
        c = q2[x]
        part_a = jnp.where(even2, c, lane_roll(c, 1))
        part_b = jnp.where(even2, lane_roll(c, -1), c)
        rf[x] = twice(tmp, jnp.concatenate([part_a, part_b], axis=0))

    def correct(x):
        refine_mid(x)
        for l in (2 * x - 2, 2 * x - 1):
            p0[l] = v2[l] + rf[x]

    correct(2)
    correct(3)
    last_sweep = functools.partial(sweep_fine, p0, p1)
    layers(3, 5, last_sweep)
    inner = exchange([(p1.at[4, :, cols], p1.at[0, :, cols])], [(p1.at[3, :, cols], p1.at[7, :, cols])])

    def last_before(l, inward):
        v = p0[l]
        total = ef[l] + wa[min(l, inward)] * p0[inward] + wi[l] * row_roll(v, 1) + row_roll(wi[l] * v, -1)
        p1[l] = total + wr[l] * lane_roll(v, 1) + lane_roll(wr[l] * v, -1)

    def last_after(l, outward):
        p1[l] = 0.25 * p0[l] + invd[l] * (p1[l] + wa[min(l, outward)] * p0[outward])

    last_before(2, 3)
    last_before(5, 4)
    dens2.wait_recv()
    up2.wait_recv()
    correct(1)
    correct(4)
    last_after(2, 1)
    last_after(5, 6)
    last_sweep(1)
    last_sweep(6)
    def final_sweep(l):
        sweep_fine(p1, p2, l)
        result[l - HALO] = p2[l, :, cols]

    def last_residual(l):
        value = (1.0 / OMEGA) * (invd[l] * target_fine(p2, l)) - p2[l]
        result[l - HALO + OWN] = value[:, 0:COLS]

    layers(2, 6, final_sweep)
    layers(3, 5, last_residual)
    inner.wait_recv()
    sweep_fine(p1, p2, 1)
    sweep_fine(p1, p2, 6)
    last_residual(2)
    last_residual(5)
    for copy in sends:
        copy.wait_send()


def solution(mesh):
    n_alt, n_raan = mesh.shape["alt"], mesh.shape["raan"]
    spec = P("alt", None, "raan")

    def vmem(*shape):
        return pltpu.VMEM(shape, jnp.float32)

    def shards(source, k_alt, k_inc, k_raan):
        scratch = [vmem(LAYERS, INC, WIDE)] * 14
        scratch += [vmem(4, OWN, 2, 16, 128), vmem(4, OWN, 2, 16, 128), vmem(2, 6, 2, 16, 128), vmem(2, 32, 128), vmem(2, 32, 128),
                    vmem(4, TILES, INC + 8, 128), vmem(4, TILES, 24, 128)]
        scratch += [vmem(6, 16, WIDE), vmem(6, 2, 16, WIDE), vmem(6, 6, 16, WIDE), vmem(2, 2, 16, WIDE),
                    vmem(2, 2, 16, WIDE)] + [vmem(6, 16, WIDE)] * 4 + [vmem(6, INC, WIDE)]
        scratch += [vmem(2 * FAR + 1, 3, 8, WIDE), vmem(2 * FAR + 1, 5, 8, WIDE), vmem(2 * FAR + 1, 8, WIDE),
                    vmem(4, 4, WIDE), vmem(2 * FAR + 2, 3, 4, WIDE),
                    vmem(3, 4, WIDE), vmem(2 * FAR + 2, 4, WIDE)]
        scratch += [pltpu.SemaphoreType.DMA((4,)),
                    pltpu.SemaphoreType.DMA((64,)), pltpu.SemaphoreType.DMA((64,)),
                    pltpu.SemaphoreType.REGULAR((3, 2))]
        shape = pltpu.VMEM((2 * OWN, INC, COLS), source.dtype)
        result = pl.pallas_call(
            functools.partial(kernel, n_alt, n_raan),
            out_shape=shape,
            in_specs=[pl.BlockSpec(memory_space=pltpu.HBM)] * 4,
            out_specs=pl.BlockSpec(memory_space=pltpu.VMEM),
            scratch_shapes=scratch,
            compiler_params=pltpu.CompilerParams(
                collective_id=0, has_side_effects=True, vmem_limit_bytes=60 * 1024 * 1024),
            name="vcycle",
        )(source, k_alt, k_inc, k_raan)
        return result[:OWN], result[OWN:]

    return jax.shard_map(shards, mesh=mesh, in_specs=(spec,) * 4, out_specs=(spec, spec), check_vma=False)
```
